128 devices in a mesh: ctx: 32 (over x, z, core), fsdp: 4 (over y).
Axes of the slice: x: 4, y: 4, z: 4, core: 2. Of those that a mesh axis runs over, the one named last changes fastest.
Arguments:
- tokens: bfloat16 [8, 4096, 1280], P('fsdp', 'ctx'), may hold values from -6 to 6
- segment_ids: int32 [8, 4096], P('fsdp', 'ctx'), may hold values from 0 to 3, as said below
- cotangent: bfloat16 [8, 4096, 1280], P('fsdp', 'ctx'), may hold values from -6 to 6
- attn_in: bfloat16 [1280, 3840], P('fsdp'), may hold values from -0.15625 to 0.15625
- attn_out: bfloat16 [1280, 1280], P('fsdp'), may hold values from -1.25 to 1.25
- ffn_in: bfloat16 [1280, 1280], P('fsdp'), may hold values from -0.15625 to 0.15625
- ffn_out: bfloat16 [1280, 1280], P('fsdp'), may hold values from -0.15625 to 0.15625
- gain_attn: bfloat16 [1280], P('fsdp'), may hold values from 0.099609375 to 1.8984375
- gain_ffn: bfloat16 [1280], P('fsdp'), may hold values from 0.099609375 to 1.8984375
- query_scale: bfloat16 [80], P('fsdp'), may hold values from -3 to 3
Outputs:
- outputs: bfloat16 [8, 4096, 1280], P('fsdp', 'ctx')
- input_grad: float32 [8, 4096, 1280], P('fsdp', 'ctx')
- grad_attn_in: float32 [1280, 3840], P('fsdp')
- grad_attn_out: float32 [1280, 1280], P('fsdp')
- grad_ffn_in: float32 [1280, 1280], P('fsdp')
- grad_ffn_out: float32 [1280, 1280], P('fsdp')
- grad_gain_attn: float32 [1280], P('fsdp')
- grad_gain_ffn: float32 [1280], P('fsdp')
- grad_query_scale: float32 [80], P('fsdp')
The draws below stay inside these ranges and needn't reach their ends.
Inputs may be any that keep to these rules, and one draw needn't show every extreme that they name: `segment_ids`: ids start at 0 at each sequence's first position and never fall, rising by at most one from a position to the next; a document is a run of equal ids. On each index of fsdp one of its 2 sequences is a single document; every other sequence has exactly 3 document starts after its first position, at positions drawn uniformly without repeats.
All inputs are finite; a program needn't handle non-finite values.
Results may differ from the reference program's by a relative error of at most 0.038.
Values may be sent and summed in bfloat16 or wider, within the bound.
No kernel may reach another device: no remote copies, remote signals or barrier semaphores. Data moves between devices by JAX's collectives and lax.ppermute only.
A program may use at most 320 MiB of HBM per device.

```python
import math
import jax
import jax.numpy as jnp
from jax import lax

D = 1280
HEADS = 16
HD = 80
FF = 1280
MICRO = 2
DOC_MEAN = 1024
SEQ_LEN = 4096
SEQS = 8


def draw_segment_ids(key, part):
    key = jax.random.fold_in(key, 7)
    start_key, pick_key = jax.random.split(key)
    starts = max(SEQ_LEN // DOC_MEAN, 2) - 1
    row_keys = jax.random.split(start_key, SEQS)
    orders = jax.vmap(lambda k: jax.random.permutation(k, SEQ_LEN - 1))(row_keys)
    chosen_starts = orders[:, :starts].astype(jnp.int32) + 1
    position = jnp.arange(SEQ_LEN, dtype=jnp.int32)
    hits = jnp.sum(jnp.where(position[None, None, :] == chosen_starts[:, :, None], 1, 0), axis=1).astype(jnp.int32)
    chosen = jax.random.randint(pick_key, (SEQS // MICRO,), 0, MICRO)
    whole = jnp.arange(SEQS, dtype=jnp.int32) % MICRO == jnp.repeat(chosen, MICRO)
    flags = jnp.where(jnp.logical_not(whole[:, None]), hits, 0).astype(jnp.int32)
    return jnp.cumsum(flags, axis=1).astype(jnp.int32)


def shard_levels(key, extent, shards, least, top_value):
    level = 1.0
    for dim, shards_of in shards:
        heights = jax.random.uniform(jax.random.fold_in(jax.random.fold_in(key, 6), dim), (shards_of,), jnp.float32, least / len(shards), top_value / len(shards))
        level = level * jnp.repeat(jnp.exp(heights), extent[dim] // shards_of).reshape((-1,) + (1,) * (len(extent) - 1 - dim))
    return level


def normal_values(key, extent, spread, limit, pieces=(), kind=jnp.bfloat16):
    values = spread * jax.random.normal(key, extent, jnp.float32)
    if pieces:
        values = values * shard_levels(key, extent, pieces, -0.22, 0.18)
    return jnp.clip(values, -limit, limit).astype(kind)


def setup_inputs(seed: int = 0) -> dict:
    seeds = jax.random.split(jax.random.key(seed), 11)
    tokens = normal_values(seeds[0], (SEQS, SEQ_LEN, D), 1.0, 6.0, ((0, 4), (1, 32)))
    segment_ids = draw_segment_ids(jax.random.fold_in(seeds[10], 71), 0)
    cotangent = normal_values(seeds[2], (SEQS, SEQ_LEN, D), 1.0, 6.0, ((0, 4), (1, 32)))
    attn_in = normal_values(seeds[3], (D, 3 * D), D ** -0.5, 0.15625, ((0, 4),))
    attn_out = normal_values(seeds[4], (D, D), (max(D // 64, 4)) ** -0.5, 1.25, ((0, 4),))
    ffn_in = normal_values(seeds[5], (D, FF), D ** -0.5, 0.15625, ((0, 4),))
    ffn_out = normal_values(seeds[6], (FF, D), FF ** -0.5, 0.15625, ((0, 4),))
    gain_attn = jnp.clip(1.0 + 0.18 * jax.random.normal(seeds[7], (D,), jnp.float32), 0.099609375, 1.8984375).astype(jnp.bfloat16)
    gain_ffn = jnp.clip(1.0 + 0.18 * jax.random.normal(seeds[8], (D,), jnp.float32), 0.099609375, 1.8984375).astype(jnp.bfloat16)
    query_scale = normal_values(seeds[9], (HD,), 1.0, 3.0, ((0, 4),))
    return dict(tokens=tokens, segment_ids=segment_ids, cotangent=cotangent, attn_in=attn_in, attn_out=attn_out, ffn_in=ffn_in, ffn_out=ffn_out, gain_attn=gain_attn, gain_ffn=gain_ffn, query_scale=query_scale)


EPS = 1e-06
QCONST = 1.442695041
NEG = -1e+30
HIGHEST = lax.Precision.HIGHEST

@jax.custom_vjp
def low(v):
    return lax.optimization_barrier(v.astype(jnp.bfloat16)).astype(jnp.float32)

@jax.custom_vjp
def low_back(v):
    return v

def low_keep(v):
    return (low(v), None)

def low_pass(kept, grad):
    return (grad,)

def back_keep(v):
    return (v, None)

def back_low(kept, grad):
    return (low(grad),)
low.defvjp(low_keep, low_pass)
low_back.defvjp(back_keep, back_low)

def norm_rows(values, gain):
    return values * lax.rsqrt(lax.optimization_barrier(jnp.mean(values * values, -1, keepdims=True)) + EPS) * gain

def attend_block(block, keys, values, key_seg):
    query_block, query_pos, query_seg = block
    key_pos = jnp.arange(keys.shape[0], dtype=jnp.int32)
    scores = low_back(jnp.einsum('qhd,khd->hqk', query_block, keys, precision=HIGHEST))
    mask = (query_seg[:, None] == key_seg[None, :]) & (key_pos[None, :] <= query_pos[:, None])
    scores = jnp.where(mask[None], scores, NEG)
    probs = jax.nn.softmax(scores, axis=-1)
    return jnp.einsum('hqk,khd->qhd', low(probs), values, precision=HIGHEST)

def one_sequence(params, inputs, seg):
    w_qkv, w_out, w_up, w_down, gain_one, gain_two, scale_raw = params
    length = inputs.shape[0]
    first = low(norm_rows(inputs, gain_one))
    project = low_back(jnp.dot(first, w_qkv, precision=HIGHEST))
    factor = jax.nn.softplus(scale_raw) * (QCONST / math.sqrt(HD))
    queries = low(project[:, :D].reshape(length, HEADS, HD) * factor)
    keys = low(project[:, D:2 * D]).reshape(length, HEADS, HD)
    values = low(project[:, 2 * D:]).reshape(length, HEADS, HD)
    block = math.gcd(length, 512)
    count = length // block
    positions = jnp.arange(length, dtype=jnp.int32)

    def per_block(item):
        return attend_block(item, keys, values, seg)
    attended = lax.map(jax.checkpoint(per_block), (queries.reshape(count, block, HEADS, HD), positions.reshape(count, block), seg.reshape(count, block)))
    attended = low(low_back(attended.reshape(length, D)))
    middle = inputs + low_back(jnp.dot(attended, w_out, precision=HIGHEST))
    second = low(norm_rows(middle, gain_two))
    hidden_pre = low_back(jnp.dot(second, w_up, precision=HIGHEST))
    hidden = low(jax.nn.silu(hidden_pre))
    return middle + low_back(jnp.dot(hidden, w_down, precision=HIGHEST))

def reference(tokens, segment_ids, cotangent, attn_in, attn_out, ffn_in, ffn_out, gain_attn, gain_ffn, query_scale):
    params = tuple((p.astype(jnp.float32) for p in (attn_in, attn_out, ffn_in, ffn_out, gain_attn, gain_ffn, query_scale)))
    inputs = tokens.astype(jnp.float32)

    def forward(weights, acts):

        def step(carry, item):
            return (carry, one_sequence(weights, item[0], item[1]))
        unused, result = lax.scan(step, jnp.float32(0.0), (acts, segment_ids))
        return result
    result, pullback = jax.vjp(forward, params, inputs)
    grads, input_grad = pullback(cotangent.astype(jnp.float32))
    return (result.astype(jnp.bfloat16), input_grad, grads[0], grads[1], grads[2], grads[3], grads[4], grads[5], grads[6])
```

```python
import math

import jax
import jax.numpy as jnp
from jax import lax
from jax.experimental import pallas as pl
from jax.experimental.pallas import tpu as pltpu
from jax.sharding import Mesh
from jax.sharding import PartitionSpec as P

D = 1280
HEADS = 16
HD = 80
EPS = 1e-06
QCONST = 1.442695041
NEG = -1e30
F32 = jnp.float32
BF16 = jnp.bfloat16
VMEM_LIMIT = 56 * 1024 * 1024
CHIPS = ("x", "z")


def dot(a, b):
    return jnp.dot(a, b, preferred_element_type=F32)


def dot_nt(a, b):
    return lax.dot_general(a, b, (((1,), (1,)), ((), ())), preferred_element_type=F32)


def dot_tn(a, b):
    return lax.dot_general(a, b, (((0,), (0,)), ((), ())), preferred_element_type=F32)


def qkv_kernel(x_ref, gain_ref, wt_ref, wkv_ref, factor_ref, first_ref, qt_ref, raw_ref, k_ref, v_ref, kt_ref, vt_ref):
    x = x_ref[...].astype(F32)
    scale = lax.rsqrt(jnp.mean(x * x, -1, keepdims=True) + EPS)
    first = (x * scale * gain_ref[...]).astype(BF16)
    first_ref[...] = first
    projected = dot_nt(wt_ref[...], first)
    raw = projected[:HD]
    queries = (raw * factor_ref[...]).astype(BF16)
    keys = projected[HD : 2 * HD].astype(BF16)
    values = projected[2 * HD :].astype(BF16)
    rows = dot(first, wkv_ref[...]).astype(BF16)
    for s in range(2):
        part = slice(128 * s, 128 * s + 128)
        qt_ref[s] = queries[:, part]
        raw_ref[s] = raw[:, part]
        kt_ref[s] = keys[:, part]
        vt_ref[s] = values[:, part]
        k_ref[s] = rows[part, :128]
        v_ref[s] = rows[part, 128:]


def qkv_call(gathered, gain, wt, wkv, factor):
    whole = lambda *shape: pl.BlockSpec(shape, lambda g: (0,) * len(shape))
    wide = pl.BlockSpec((2, HD, 128), lambda g: (0, 0, g))
    tall = pl.BlockSpec((2, 128, 128), lambda g: (0, g, 0))
    return pl.pallas_call(
        qkv_kernel,
        grid=(16,),
        in_specs=[
            pl.BlockSpec((256, D), lambda g: (g, 0)),
            whole(1, D),
            whole(3 * HD, D),
            whole(D, 256),
            whole(HD, 1),
        ],
        out_specs=[pl.BlockSpec((256, D), lambda g: (g, 0)), wide, wide, tall, tall, wide, wide],
        out_shape=[
            jax.ShapeDtypeStruct((4096, D), BF16),
            jax.ShapeDtypeStruct((2, HD, 2048), BF16),
            jax.ShapeDtypeStruct((2, HD, 2048), F32),
            jax.ShapeDtypeStruct((2, 2048, 128), BF16),
            jax.ShapeDtypeStruct((2, 2048, 128), BF16),
            jax.ShapeDtypeStruct((2, HD, 2048), BF16),
            jax.ShapeDtypeStruct((2, HD, 2048), BF16),
        ],
        compiler_params=pltpu.CompilerParams(vmem_limit_bytes=VMEM_LIMIT),
        name="qkv",
    )(gathered, gain, wt, wkv, factor)


def tile_positions():
    row = lax.broadcasted_iota(jnp.int32, (256, 256), 0)
    column = lax.broadcasted_iota(jnp.int32, (1, 256), 1)
    spread = lambda r: r + jnp.where(r >= 128, 128, 0)
    return spread(row), spread(column)


def forward_kernel(bounds, qt_ref, ko_ref, kx_ref, vto_ref, vtx_ref, start_ref, out_ref, low_ref, lse_ref):
    core = bounds[32]
    key_base, query_base = tile_positions()

    def query_tile(index, unused):
        s, t = index // 8, index % 8
        columns = pl.ds(pl.multiple_of(t * 256, 256), 256)
        queries = qt_ref[s, :, columns]
        query_pos = query_base + (512 * t + 128 * core)
        starts = start_ref[s, :, columns]

        def score(keys_ref, block, which, masked):
            rows = pl.ds(pl.multiple_of(block * 256, 256), 256)
            scores = dot(keys_ref[s, rows, :HD], queries)
            if masked:
                shift = 512 * block + 128 * which
                mask = (key_base <= query_pos - shift) & (key_base >= starts - shift)
                scores = jnp.where(mask, scores, NEG)
            return scores

        def tile(block, masked, state):
            best, total, accum = state
            one = score(ko_ref, block, core, masked)
            two = score(kx_ref, block, 1 - core, masked)
            newest = jnp.maximum(
                best, jnp.max(jnp.maximum(one, two), 0, keepdims=True)
            )
            one = jnp.exp(one - newest)
            two = jnp.exp(two - newest)
            decay = jnp.exp(best - newest)
            columns = pl.ds(pl.multiple_of(block * 256, 256), 256)
            total = total * decay + jnp.sum(one + two, 0, keepdims=True)
            accum = (
                accum * decay
                + dot(vto_ref[s, :, columns], one.astype(BF16))
                + dot(vtx_ref[s, :, columns], two.astype(BF16))
            )
            return newest, total, accum

        state = (jnp.full((1, 256), NEG, F32), jnp.zeros((1, 256), F32), jnp.zeros((HD, 256), F32))
        state = tile(t, True, state)
        low, high = bounds[index], bounds[16 + index]
        state = lax.fori_loop(high, t, lambda b, st: tile(b, False, st), state)
        best, total, accum = lax.fori_loop(low, high, lambda b, st: tile(b, True, st), state)
        result = accum / total
        out_ref[s, :, columns] = result
        lse_ref[s, :, columns] = best + jnp.log(total)
        lanes = pl.ds(pl.multiple_of(s * 128, 128), 128)
        result = result.astype(BF16)
        low_ref[2 * t, :, lanes] = result[:, :128]
        low_ref[2 * t + 1, :, lanes] = result[:, 128:]
        return unused

    lax.fori_loop(0, 16, query_tile, 0)


def tall(wide):
    return jnp.concatenate([wide, jnp.zeros((128 - HD, 256), F32)], 0).T.astype(BF16)


def backward_kernel(
    bounds, qt_ref, raw_ref, ko_ref, kx_ref, vo_ref, vx_ref, kto_ref, ktx_ref, start_ref, out_ref, lse_ref, grad_ref, factor_ref,
    dq_ref, scale_ref, dko_ref, dvo_ref, dkx_ref, dvx_ref, dk_acc, dv_acc,
):
    core = bounds[32]
    key_base, query_base = tile_positions()
    for ref in (dko_ref, dvo_ref, dk_acc, dv_acc):
        ref[...] = jnp.zeros_like(ref)
    scale_ref[...] = jnp.zeros_like(scale_ref)

    def query_tile(index, unused):
        s, t = index // 8, index % 8
        columns = pl.ds(pl.multiple_of(t * 256, 256), 256)
        queries = qt_ref[s, :, columns]
        query_rows = tall(queries.astype(F32))
        query_pos = query_base + (512 * t + 128 * core)
        starts = start_ref[s, :, columns]
        lse = lse_ref[s, :, columns]
        lanes = pl.ds(pl.multiple_of(s * 128, 128), 128)
        grads = jnp.concatenate([grad_ref[2 * t, :, lanes], grad_ref[2 * t + 1, :, lanes]], 1)
        wide = grads.astype(F32)
        grad_rows = tall(wide)
        delta = jnp.sum(wide * out_ref[s, :, columns], 0, keepdims=True)

        def tile(block, masked, dq):
            rows = pl.ds(pl.multiple_of(block * 256, 256), 256)
            for k_ref, v_ref, kt_ref, dk_ref, dv_ref, which in (
                (ko_ref, vo_ref, kto_ref, dko_ref, dvo_ref, core),
                (kx_ref, vx_ref, ktx_ref, dk_acc, dv_acc, 1 - core),
            ):
                probs = jnp.exp(dot(k_ref[s, rows, :HD], queries) - lse)
                if masked:
                    shift = 512 * block + 128 * which
                    mask = (key_base <= query_pos - shift) & (key_base >= starts - shift)
                    probs = jnp.where(mask, probs, 0.0)
                dprobs = dot(v_ref[s, rows, :HD], grads)
                dscores = (probs * (dprobs - delta)).astype(BF16)
                dv_ref[s, rows, :] += dot(probs.astype(BF16), grad_rows)
                dk_ref[s, rows, :] += dot(dscores, query_rows)
                dq = dq + dot(kt_ref[s, :, rows], dscores)
            return dq

        dq = tile(t, True, jnp.zeros((HD, 256), F32))
        low, high = bounds[index], bounds[16 + index]
        dq = lax.fori_loop(high, t, lambda b, st: tile(b, False, st), dq)
        dq = lax.fori_loop(low, high, lambda b, st: tile(b, True, st), dq)
        scale_ref[...] += dq * raw_ref[s, :, columns]
        result = (dq * factor_ref[...]).astype(BF16)
        dq_ref[2 * t, :, lanes] = result[:, :128]
        dq_ref[2 * t + 1, :, lanes] = result[:, 128:]
        return unused

    lax.fori_loop(0, 16, query_tile, 0)
    dkx_ref[...] = dk_acc[...].astype(BF16)
    dvx_ref[...] = dv_acc[...].astype(BF16)


def whole_call(kernel, inputs, out_shape, scratch, name, cost):
    vmem = pl.BlockSpec(memory_space=pltpu.VMEM)
    return pl.pallas_call(
        kernel,
        in_specs=[pl.BlockSpec(memory_space=pltpu.SMEM)] + [vmem] * (len(inputs) - 1),
        out_specs=[vmem] * len(out_shape),
        out_shape=out_shape,
        scratch_shapes=scratch,
        compiler_params=pltpu.CompilerParams(vmem_limit_bytes=VMEM_LIMIT),
        cost_estimate=pl.CostEstimate(flops=cost, bytes_accessed=16 << 20, transcendentals=8 << 20),
        name=name,
    )(*inputs)


def weight_kernel(dq_ref, dko_ref, dkr_ref, dvo_ref, dvr_ref, first_ref, grad_ref, weight_ref, accum):
    g = pl.program_id(0)

    @pl.when(g == 0)
    def _():
        accum[...] = jnp.zeros_like(accum)

    grad_ref[0, :HD] = dq_ref[0]
    for base, own_ref, far_ref in ((HD, dko_ref, dkr_ref), (2 * HD, dvo_ref, dvr_ref)):
        for s in range(2):
            total = own_ref[s] + far_ref[s].astype(F32)
            grad_ref[0, base : base + HD, 128 * s : 128 * s + 128] = total.T[:HD].astype(BF16)
    accum[...] += dot(grad_ref[0], first_ref[...])

    @pl.when(g == 15)
    def _():
        weight_ref[...] = jnp.concatenate([accum[...], jnp.zeros((16, D), F32)], 0).T


def weight_call(dq, dko, dkr, dvo, dvr, first):
    tall = pl.BlockSpec((2, 128, 128), lambda g: (0, g, 0))
    return pl.pallas_call(
        weight_kernel,
        grid=(16,),
        in_specs=[
            pl.BlockSpec((1, HD, 256), lambda g: (g, 0, 0)),
            tall,
            tall,
            tall,
            tall,
            pl.BlockSpec((256, D), lambda g: (g, 0)),
        ],
        out_specs=[
            pl.BlockSpec((1, 3 * HD, 256), lambda g: (g, 0, 0)),
            pl.BlockSpec((D, 256), lambda g: (0, 0)),
        ],
        out_shape=[
            jax.ShapeDtypeStruct((16, 3 * HD, 256), BF16),
            jax.ShapeDtypeStruct((D, 256), F32),
        ],
        scratch_shapes=[pltpu.VMEM((3 * HD, D), F32)],
        compiler_params=pltpu.CompilerParams(vmem_limit_bytes=VMEM_LIMIT),
        name="weight",
    )(dq, dko, dkr, dvo, dvr, first)


def assemble_kernel(zero_ref, one_ref, out_ref, scale_ref):
    total = jnp.zeros((8, 256), F32)
    for c, ref in enumerate((zero_ref, one_ref)):
        for h in range(HEADS):
            total = total + ref[h, 160:168].astype(F32)
        for part in range(3):
            lanes = slice(HD * part, HD * part + HD)
            out_ref[160 * c : 160 * c + 160, D * part : D * part + D] = jnp.concatenate(
                [ref[h, :160, lanes].astype(F32) for h in range(HEADS)], 1
            )
    scale_ref[...] = total


def assemble_call(zero, one):
    return pl.pallas_call(
        assemble_kernel,
        out_shape=[jax.ShapeDtypeStruct((320, 3 * D), F32), jax.ShapeDtypeStruct((8, 256), F32)],
        compiler_params=pltpu.CompilerParams(vmem_limit_bytes=VMEM_LIMIT),
        name="assemble",
    )(zero, one)


def other_core(value):
    return lax.ppermute(value, "core", [(0, 1), (1, 0)])


def scatter_sum_y(parts):
    y = lax.axis_index("y")
    piece = lambda step: lax.dynamic_index_in_dim(parts, (y + step) % 4, 0, keepdims=False)
    total = piece(0).astype(F32)
    for step in (1, 3, 2):
        pairs = [(i, (i + step) % 4) for i in range(4)]
        total = total + lax.ppermute(piece(step).astype(BF16), "y", pairs).astype(F32)
    return total


def gather_y(value):
    return lax.all_gather(value, "y", axis=0, tiled=True)


def gather_rows(value):
    rows = value.shape[0] // 2
    half = lax.dynamic_slice_in_dim(value, lax.axis_index("core") * rows, rows, 0)
    return lax.all_gather(half, ("y", "core"), axis=0, tiled=True)


def swap(value):
    return lax.all_to_all(value, CHIPS, 0, 0, tiled=True)


def norm_scale(values):
    return lax.rsqrt(jnp.mean(values * values, -1, keepdims=True) + EPS)


def norm_back(values, scale, gain, grad):
    shaped = grad * gain
    inner = jnp.mean(shaped * values, -1, keepdims=True)
    return scale * shaped - values * scale * scale * scale * inner


def local(tokens, segment_ids, cotangent, attn_in, attn_out, ffn_in, ffn_out, gain_attn, gain_ffn, query_scale):
    core = lax.axis_index("core")
    head = lax.axis_index("x") * 4 + lax.axis_index("z")
    inputs_low = tokens.reshape(256, D)
    upstream = cotangent.reshape(256, D)

    gathered = lax.all_gather(inputs_low, CHIPS, axis=0, tiled=True)

    mine = lax.dynamic_index_in_dim(attn_in.reshape(320, 3, HEADS, HD), head, 2, keepdims=False).reshape(320, 3 * HD)
    small = jnp.concatenate([gain_attn[:, None], gain_ffn[:, None], jnp.pad(query_scale, (0, 300))[:, None]], 1)
    small = gather_y(jnp.concatenate([mine, jnp.pad(small, ((0, 0), (0, 13)))], 1))
    head_weights = small[:, : 3 * HD]
    gain_one = small[:, 240].reshape(1, D).astype(F32)
    gain_two = small[:, 241].reshape(1, D).astype(F32)
    scale_raw = small[:, 242].reshape(4, 320)[:, :20].reshape(HD).astype(F32)
    factor = jax.nn.softplus(scale_raw) * (QCONST / math.sqrt(HD))
    factor_column = factor[:, None]
    w_out, w_up, w_down = gather_rows(attn_out), gather_rows(ffn_in), gather_rows(ffn_out)

    segments = lax.all_gather(segment_ids, ("x", "z", "core"), axis=1, tiled=True)
    begins = [jnp.sum((segments < k).astype(jnp.int32), 1, keepdims=True) for k in range(1, 4)]
    own_segments = lax.dynamic_index_in_dim(segments.reshape(2, 16, 2, 128), core, 2, keepdims=False).reshape(2, 2048)
    starts = jnp.zeros_like(own_segments)
    for k in range(1, 4):
        starts = jnp.where(own_segments == k, begins[k - 1], starts)
    by_tile = starts.reshape(2, 8, 256)
    low = by_tile[:, :, 0] // 512
    high = jnp.minimum((by_tile[:, :, 255] + 511) // 512, jnp.arange(8, dtype=jnp.int32)[None])
    high = jnp.maximum(low, high)
    bounds = jnp.concatenate([low.reshape(16), high.reshape(16), core[None].astype(jnp.int32)])
    starts = starts[:, None, :]

    blank = jnp.zeros((D, 128 - HD), BF16)
    head_kv = jnp.concatenate([head_weights[:, HD : 2 * HD], blank, head_weights[:, 2 * HD :], blank], 1)
    first, qt, raw, k_own, v_own, kt_own, vt_own = qkv_call(gathered, gain_one, head_weights.T, head_kv, factor_column)
    k_far, vt_far, v_far, kt_far = other_core(k_own), other_core(vt_own), other_core(v_own), other_core(kt_own)

    shape = jax.ShapeDtypeStruct
    attended, attended_low, lse = whole_call(
        forward_kernel,
        (bounds, qt, k_own, k_far, vt_own, vt_far, starts),
        [shape((2, HD, 2048), F32), shape((16, HD, 256), BF16), shape((2, 1, 2048), F32)],
        [],
        "attention",
        8 << 30,
    )
    attended_t = swap(attended_low).reshape(D, 256)

    inputs = inputs_low.astype(F32)
    middle = inputs + dot_tn(attended_t, w_out)
    second_scale = norm_scale(middle)
    second = (middle * second_scale * gain_two).astype(BF16)
    hidden_pre = dot(second, w_up)
    gate = jax.nn.sigmoid(hidden_pre)
    hidden = jax.nn.silu(hidden_pre).astype(BF16)
    grad_hidden = dot_nt(upstream, w_down)
    grad_pre = (grad_hidden * gate * (1.0 + hidden_pre * (1.0 - gate))).astype(BF16)
    grad_second = dot_nt(grad_pre, w_up)
    grad_middle = upstream.astype(F32) + norm_back(middle, second_scale, gain_two, grad_second)
    grad_branch = grad_middle.astype(BF16)
    grad_attended = dot_nt(w_out, grad_branch).astype(BF16).reshape(16, HD, 256)
    grad_attended, hidden, second, attended_t = lax.optimization_barrier((grad_attended, hidden, second, attended_t))
    grad_attended = swap(grad_attended)
    outputs = (middle + dot(hidden, w_down)).astype(BF16)

    def half_columns(which):
        cut = lambda value: lax.dynamic_slice_in_dim(value, which * 640, 640, 1)
        parts = [dot(attended_t, cut(grad_branch)), dot_tn(second, cut(grad_pre)), dot_tn(hidden, cut(upstream))]
        return jnp.concatenate([part.astype(BF16) for part in parts], 1)

    give = half_columns(1 - core)
    summed = (half_columns(core).astype(F32) + other_core(give).astype(F32)).astype(BF16)
    summed = lax.psum_scatter(summed, "y", scatter_dimension=0, tiled=True)

    dq, scale_terms, dk_own, dv_own, dk_far, dv_far = whole_call(
        backward_kernel,
        (bounds, qt, raw, k_own, k_far, v_own, v_far, kt_own, kt_far, starts, attended, lse, grad_attended, factor_column),
        [
            shape((16, HD, 256), BF16),
            shape((HD, 256), F32),
            shape((2, 2048, 128), F32),
            shape((2, 2048, 128), F32),
            shape((2, 2048, 128), BF16),
            shape((2, 2048, 128), BF16),
        ],
        [pltpu.VMEM((2, 2048, 128), F32), pltpu.VMEM((2, 2048, 128), F32)],
        "attention_back",
        20 << 30,
    )
    grad_project, head_grad = weight_call(dq, dk_own, other_core(dk_far), dv_own, other_core(dv_far), first)

    scale_part = jnp.sum(scale_terms, 1).reshape(4, 1, 20)
    scale_part = jnp.pad(scale_part, ((0, 0), (0, 7), (0, 236)))
    head_parts = head_grad.reshape(4, 2, 160, 256)
    keep = lax.dynamic_index_in_dim(head_parts, core, 1, keepdims=False)
    give = lax.dynamic_index_in_dim(head_parts, 1 - core, 1, keepdims=False)
    head_sum = keep + other_core(give.astype(BF16)).astype(F32)
    head_sum = scatter_sum_y(jnp.concatenate([head_sum, scale_part], 1))

    grad_project = swap(grad_project)
    w_qkv = gather_rows(attn_in)
    columns = grad_project.reshape(HEADS, 3, HD, 256).transpose(1, 0, 2, 3).reshape(3 * D, 256)
    grad_first = lax.dot_general(columns, w_qkv, (((0,), (1,)), ((), ())), preferred_element_type=F32)
    input_grad = grad_middle + norm_back(inputs, norm_scale(inputs), gain_one, grad_first)

    square_sum = jnp.sum(swap(summed.reshape(16, 20, 3 * 640)).astype(F32), 0).astype(BF16)
    squares = swap(jnp.broadcast_to(square_sum[None], (16, 20, 3 * 640))).reshape(320, 3 * 640)
    far_squares = other_core(squares)
    squares = jnp.where(core == 0, squares, far_squares), jnp.where(core == 0, far_squares, squares)
    grad_out, grad_up, grad_down = (
        jnp.concatenate([part[:, 640 * i : 640 * i + 640] for part in squares], 1).astype(F32) for i in range(3)
    )
    heads = swap(jnp.broadcast_to(head_sum.astype(BF16)[None], (16, 168, 256)))
    far_heads = other_core(heads)
    heads = jnp.where(core == 0, heads, far_heads), jnp.where(core == 0, far_heads, heads)
    grad_attn_in, scale_sum = assemble_call(*heads)
    own_gain = lambda value: value.astype(F32)
    grad_gain_one = jnp.sum(grad_attn_in * attn_in.astype(F32), 1) / own_gain(gain_attn)
    grad_gain_two = jnp.sum(grad_up * ffn_in.astype(F32), 1) / own_gain(gain_ffn)
    own_scale = query_scale.astype(F32)
    grad_scale = scale_sum[0, :20] * jax.nn.sigmoid(own_scale) * (QCONST / math.sqrt(HD))
    return (
        outputs.reshape(2, 128, D),
        input_grad.reshape(2, 128, D),
        grad_attn_in,
        grad_out,
        grad_up,
        grad_down,
        grad_gain_one,
        grad_gain_two,
        grad_scale,
    )


def solution(mesh):
    split = Mesh(mesh.devices.reshape(4, 4, 2, 4), ("x", "z", "core", "y"))
    rows = P("y", ("x", "z", "core"), None)
    weight = P("y", None)
    vector = P("y")
    return jax.shard_map(
        local,
        mesh=split,
        in_specs=(rows, P("y", ("x", "z", "core")), rows) + (weight,) * 4 + (vector,) * 3,
        out_specs=(rows, rows) + (weight,) * 4 + (vector,) * 3,
        check_vma=False,
    )
```

```python
import math

import jax
import jax.numpy as jnp
from jax import lax
from jax.experimental import pallas as pl
from jax.experimental.pallas import tpu as pltpu
from jax.sharding import Mesh
from jax.sharding import PartitionSpec as P

D = 1280
HEADS = 16
HD = 80
EPS = 1e-06
QCONST = 1.442695041
NEG = -1e30
LOG2E = math.log2(math.e)
F32 = jnp.float32
BF16 = jnp.bfloat16
CHIPS = ("x", "z")
shape = jax.ShapeDtypeStruct


def dot(a, b):
    return jnp.dot(a, b, preferred_element_type=F32)


def dot_nt(a, b):
    return lax.dot_general(a, b, (((1,), (1,)), ((), ())), preferred_element_type=F32)


def dot_tn(a, b):
    return lax.dot_general(a, b, (((0,), (0,)), ((), ())), preferred_element_type=F32)


def norm_scale(values):
    return lax.rsqrt(jnp.mean(values * values, -1, keepdims=True) + EPS)


def norm_back(values, scale, gain, grad):
    shaped = grad * gain
    inner = jnp.mean(shaped * values, -1, keepdims=True)
    return scale * shaped - values * (scale * scale * scale * inner)


def whole_call(kernel, scalars, inputs, out_shape, scratch, name, flops, moved, vmem_mib):
    vmem = pl.BlockSpec(memory_space=pltpu.VMEM)
    return pl.pallas_call(
        kernel,
        in_specs=[pl.BlockSpec(memory_space=pltpu.SMEM)] + [vmem] * len(inputs),
        out_specs=[vmem] * len(out_shape),
        out_shape=out_shape,
        scratch_shapes=scratch,
        compiler_params=pltpu.CompilerParams(vmem_limit_bytes=vmem_mib << 20),
        cost_estimate=pl.CostEstimate(flops=flops, bytes_accessed=moved, transcendentals=0),
        name=name,
    )(scalars, *inputs)


def project_kernel(x_ref, gain_ref, weight_ref, factor_ref, first_ref, out_ref):
    blocks = range(x_ref.shape[0])
    for g in blocks:
        x = x_ref[g].astype(F32)
        first_ref[g] = (x * norm_scale(x) * gain_ref[...]).astype(BF16)
    flat = [dot_nt(weight_ref[...], first_ref[g]) for g in blocks]
    for g in blocks:
        out_ref[g, :HD] = (flat[g][:HD] * factor_ref[...]).astype(BF16)
        out_ref[g, HD:] = flat[g][HD:].astype(BF16)


def project_call(x, gain, weight, factor):
    step = 2
    whole = lambda *dims: pl.BlockSpec(dims, lambda g: (0,) * len(dims))
    block = lambda *dims: pl.BlockSpec((step,) + dims, lambda g: (g, 0, 0))
    return pl.pallas_call(
        project_kernel,
        grid=(16 // step,),
        in_specs=[block(256, D), whole(1, D), whole(3 * HD, D), whole(HD, 1)],
        out_specs=[block(256, D), block(3 * HD, 256)],
        out_shape=[shape((16, 256, D), BF16), shape((16, 3 * HD, 256), BF16)],
        compiler_params=pltpu.CompilerParams(vmem_limit_bytes=24 << 20),
        cost_estimate=pl.CostEstimate(flops=8 << 30, bytes_accessed=24 << 20, transcendentals=0),
        name="project",
    )(x, gain, weight, factor)


def rows_of(s):
    return pl.ds(pl.multiple_of(s * 128, 128), 128)


def wide_tile(ref, block, s, part=None):
    rows = slice(None) if part is None else slice(HD * part, HD * part + HD)
    return jnp.concatenate([ref[2 * block, rows, rows_of(s)], ref[2 * block + 1, rows, rows_of(s)]], 1)


def tall_tile(ref, which, block, s):
    return jnp.concatenate([ref[which, 2 * block, rows_of(s), :], ref[which, 2 * block + 1, rows_of(s), :]], 0)


def stand(out_ref, which, ref, part):
    row = lax.broadcasted_iota(jnp.int32, (128 - HD, 256), 0)
    ones = jnp.where(row < 3, 1.0, 0.0)

    def block(g, unused):
        wide = ref[g, HD * part : HD * part + HD].astype(F32)
        out_ref[which, g] = jnp.concatenate([wide, ones], 0).T.astype(BF16)
        return unused

    lax.fori_loop(0, 16, block, 0, unroll=4)


def put_wide(ref, block, s, value):
    ref[2 * block, :, rows_of(s)] = value[:, :128]
    ref[2 * block + 1, :, rows_of(s)] = value[:, 128:]


CHAINS = 4
GROUPS = 8 // CHAINS


def query_base():
    column = lax.broadcasted_iota(jnp.int32, (1, 256), 1)
    return column + jnp.where(column >= 128, 128, 0)


def fill_key_base(ref, core):
    row = lax.broadcasted_iota(jnp.int32, (512, 256), 0)
    inner = row % 256
    ref[...] = 128 * jnp.where(row < 256, core, 1 - core) + inner + jnp.where(inner >= 128, 128, 0)


def start_row(bounds, t, s):
    query_pos = 512 * t + 128 * bounds[32] + query_base()
    start = jnp.zeros_like(query_pos)
    for k in range(3):
        begin = bounds[33 + 3 * s + k]
        start = jnp.where(query_pos >= begin, begin, start)
    return start


def allowed(base_ref, bounds, starts, block, diagonal):
    keys = base_ref[...]
    mask = keys >= starts - 512 * block
    if diagonal:
        mask = mask & (keys <= query_base() + 128 * bounds[32])
    return mask


def group_loops(bounds, s, p, tile):
    first = CHAINS * p
    low, high = bounds[8 * s + first], bounds[16 + 8 * s + first + CHAINS - 1]

    def diagonal(masked):
        for j in reversed(range(CHAINS)):
            tile(first + j, j, masked, True)

    pl.when(high <= first)(lambda: diagonal(False))
    pl.when(high > first)(lambda: diagonal(True))
    high = jnp.maximum(low, jnp.minimum(high, first))

    def loop(masked):
        def body(block, unused):
            tile(block, 0, masked, False)
            return unused

        return body

    lax.fori_loop(high, first, loop(False), 0)
    lax.fori_loop(low, high, loop(True), 0)


def forward_kernel(
    bounds, own_ref, far_ref, out_ref, low_ref, lse_ref, keys_ref, base_ref, best_ref, total_ref, accum_ref
):
    fill_key_base(base_ref, bounds[32])
    stand(keys_ref, 0, own_ref, 1)
    stand(keys_ref, 1, far_ref, 0)

    def group(index, unused):
        s, p = index // GROUPS, index % GROUPS
        queries = [wide_tile(own_ref, CHAINS * p + c, s, 0) for c in range(CHAINS)]
        starts = [start_row(bounds, CHAINS * p + c, s) for c in range(CHAINS)]
        best_ref[...] = jnp.full_like(best_ref, NEG)
        total_ref[...] = jnp.zeros_like(total_ref)
        accum_ref[...] = jnp.zeros_like(accum_ref)

        def tile(block, least, masked, diagonal):
            keys = jnp.concatenate([tall_tile(keys_ref, c, block, s) for c in range(2)], 0)[:, :HD]
            values = jnp.concatenate([wide_tile(own_ref, block, s, 2), wide_tile(far_ref, block, s, 1)], 1)
            chains = range(least, CHAINS)
            scores = {c: dot(keys, queries[c]) for c in chains}
            weights, decay = {}, {}
            for c in chains:
                here = diagonal and c == least
                if masked or here:
                    scores[c] = jnp.where(allowed(base_ref, bounds, starts[c], block, here), scores[c], NEG)
                best = best_ref[c]
                newest = jnp.maximum(best, jnp.max(scores[c], 0, keepdims=True))
                best_ref[c] = newest
                weights[c] = jnp.exp2(scores[c] - newest)
                decay[c] = jnp.exp2(best - newest)
                total_ref[c] = total_ref[c] * decay[c] + jnp.sum(weights[c], 0, keepdims=True)
            for c in chains:
                accum_ref[c] = accum_ref[c] * decay[c] + dot(values, weights[c].astype(BF16))

        group_loops(bounds, s, p, tile)
        for c in range(CHAINS):
            t = CHAINS * p + c
            result = accum_ref[c] / total_ref[c]
            put_wide(out_ref, t, s, result)
            put_wide(low_ref, t, s, result.astype(BF16))
            put_wide(lse_ref, t, s, best_ref[c] + jnp.log2(total_ref[c]))
        return unused

    lax.fori_loop(0, 2 * GROUPS, group, 0)


def forward_call(bounds, *inputs):
    return whole_call(
        forward_kernel,
        bounds,
        inputs,
        [shape((16, HD, 256), F32), shape((16, HD, 256), BF16), shape((16, 1, 256), F32), shape((2, 16, 256, 128), BF16)],
        [
            pltpu.VMEM((512, 256), jnp.int32),
            pltpu.VMEM((CHAINS, 1, 256), F32),
            pltpu.VMEM((CHAINS, 1, 256), F32),
            pltpu.VMEM((CHAINS, HD, 256), F32),
        ],
        "attention",
        8 << 30,
        8 << 20,
        12,
    )


def tall(wide):
    return jnp.concatenate([wide, jnp.zeros((128 - HD, 256), F32)], 0).T.astype(BF16)


def with_row(wide, row):
    one = row.astype(BF16)
    rest = row - one.astype(F32)
    two = rest.astype(BF16)
    three = (rest - two.astype(F32)).astype(BF16)
    terms = jnp.concatenate([one.astype(F32), two.astype(F32), three.astype(F32), jnp.zeros((13, 256), F32)], 0)
    return jnp.concatenate([wide, terms.astype(BF16)], 0)


def backward_kernel(
    bounds, own_ref, far_ref, keys_ref, out_ref, lse_ref, grad_ref, factor_ref,
    dq_ref, scale_ref, dko_ref, dvo_ref, dkx_ref, dvx_ref,
    dk_acc, dv_acc, base_ref, dq_acc, queries_ref, query_rows_ref, grads_ref, grad_rows_ref, values_ref,
):
    fill_key_base(base_ref, bounds[32])
    stand(values_ref, 0, own_ref, 2)
    stand(values_ref, 1, far_ref, 1)
    for ref in (dko_ref, dvo_ref, dk_acc, dv_acc):
        ref[...] = jnp.zeros_like(ref)
    scale_ref[...] = jnp.zeros_like(scale_ref)

    def group(index, unused):
        s, p = index // GROUPS, index % GROUPS
        starts = []
        for c in range(CHAINS):
            t = CHAINS * p + c
            starts.append(start_row(bounds, t, s))
            own = wide_tile(own_ref, t, s, 0)
            queries_ref[c] = with_row(own, -wide_tile(lse_ref, t, s))
            query_rows_ref[256 * c : 256 * c + 256] = tall(own.astype(F32))
            own = wide_tile(grad_ref, t, s)
            wide = own.astype(F32)
            grads_ref[c] = with_row(own, -jnp.sum(wide * wide_tile(out_ref, t, s), 0, keepdims=True))
            grad_rows_ref[256 * c : 256 * c + 256] = tall(wide)
        dq_acc[...] = jnp.zeros_like(dq_acc)

        def tile(block, least, masked, diagonal):
            keys = jnp.concatenate([tall_tile(keys_ref, c, block, s) for c in range(2)], 0)[:, :96]
            values = jnp.concatenate([tall_tile(values_ref, c, block, s) for c in range(2)], 0)[:, :96]
            flat = jnp.concatenate([wide_tile(own_ref, block, s, 1), wide_tile(far_ref, block, s, 0)], 1)
            chains = range(least, CHAINS)
            scores = [dot(keys, queries_ref[c]) for c in chains]
            dprobs = [dot(values, grads_ref[c]) for c in chains]
            all_probs, all_dscores = [], []
            for c in chains:
                here = diagonal and c == least
                probs = jnp.exp2(scores[c - least])
                if masked or here:
                    probs = jnp.where(allowed(base_ref, bounds, starts[c], block, here), probs, 0.0)
                all_probs.append(probs.astype(BF16))
                all_dscores.append((probs * dprobs[c - least]).astype(BF16))
            for c in chains:
                dq_acc[c] += dot(flat, all_dscores[c - least])
            dv = dot(jnp.concatenate(all_probs, 1), grad_rows_ref[256 * least :])
            dk = dot(jnp.concatenate(all_dscores, 1), query_rows_ref[256 * least :])
            for j in range(2):
                dvo_ref[2 * block + j, rows_of(s), :] += dv[128 * j : 128 * j + 128]
                dko_ref[2 * block + j, rows_of(s), :] += dk[128 * j : 128 * j + 128]
                dv_acc[2 * block + j, rows_of(s), :] += dv[256 + 128 * j : 384 + 128 * j]
                dk_acc[2 * block + j, rows_of(s), :] += dk[256 + 128 * j : 384 + 128 * j]

        group_loops(bounds, s, p, tile)
        for c in range(CHAINS):
            t = CHAINS * p + c
            scale_ref[...] += dq_acc[c] * wide_tile(own_ref, t, s, 0).astype(F32)
            put_wide(dq_ref, t, s, (dq_acc[c] * factor_ref[...]).astype(BF16))
        return unused

    lax.fori_loop(0, 2 * GROUPS, group, 0)
    dkx_ref[...] = (dk_acc[...] * (1 / LOG2E)).astype(BF16)
    dvx_ref[...] = dv_acc[...].astype(BF16)
    dko_ref[...] = dko_ref[...] * (1 / LOG2E)


def backward_call(bounds, *inputs):
    rows = (16, 256, 128)
    return whole_call(
        backward_kernel,
        bounds,
        inputs,
        [shape((16, HD, 256), BF16), shape((HD, 256), F32)] + [shape(rows, F32)] * 2 + [shape(rows, BF16)] * 2,
        [
            pltpu.VMEM(rows, F32),
            pltpu.VMEM(rows, F32),
            pltpu.VMEM((512, 256), jnp.int32),
            pltpu.VMEM((CHAINS, HD, 256), F32),
            pltpu.VMEM((CHAINS, 96, 256), BF16),
            pltpu.VMEM((CHAINS * 256, 128), BF16),
            pltpu.VMEM((CHAINS, 96, 256), BF16),
            pltpu.VMEM((CHAINS * 256, 128), BF16),
            pltpu.VMEM((2, 16, 256, 128), BF16),
        ],
        "attention_back",
        100 << 30,
        16 << 20,
        20,
    )


def weight_kernel(unused, dq_ref, dko_ref, dkr_ref, dvo_ref, dvr_ref, first_ref, *refs):
    send_ref, weight_ref = refs

    def block(g, accum):
        send_ref[g, :HD] = dq_ref[g]
        for base, own_ref, far_ref in ((HD, dko_ref, dkr_ref), (2 * HD, dvo_ref, dvr_ref)):
            total = own_ref[g] + far_ref[g].astype(F32)
            send_ref[g, base : base + HD] = total.T[:HD].astype(BF16)
        return accum

    lax.fori_loop(0, 16, block, 0, unroll=2)
    rows = jnp.concatenate([send_ref[g] for g in range(16)], 1)
    first = first_ref[...].reshape(4096, D)
    parts = [dot(rows, first[:, 256 * n : 256 * n + 256]) for n in range(5)]
    for n in range(5):
        weight_ref[256 * n : 256 * n + 256, :] = jnp.concatenate([parts[n], jnp.zeros((16, 256), F32)], 0).T


def weight_call(*inputs):
    return whole_call(
        weight_kernel,
        jnp.zeros((1,), jnp.int32),
        inputs,
        [shape((16, 3 * HD, 256), BF16), shape((D, 256), F32)],
        [],
        "weight",
        12 << 30,
        24 << 20,
        14,
    )


def middle_kernel(unused, att_ref, x_ref, dy_ref, gain_ref, weights_ref, grad_ref, branch_ref, pre_ref, second_ref, hidden_ref, middle_ref, wide_ref):
    gain = gain_ref[...]
    out_ref, up_ref, down_ref = (weights_ref.at[:, D * i : D * i + D] for i in range(3))
    middle = x_ref[...].astype(F32) + dot_tn(att_ref[...], out_ref[...])
    middle_ref[...] = middle
    scale = norm_scale(middle)
    second = (middle * scale * gain).astype(BF16)
    second_ref[...] = second
    upstream = dy_ref[...]
    hidden_pre = dot(second, up_ref[...])
    gate = jax.nn.sigmoid(hidden_pre)
    hidden_ref[...] = (hidden_pre * gate).astype(BF16)
    grad_hidden = dot_nt(upstream, down_ref[...])
    grad_pre = (grad_hidden * gate * (1.0 + hidden_pre * (1.0 - gate))).astype(BF16)
    pre_ref[...] = grad_pre
    grad_second = dot_nt(grad_pre, up_ref[...])
    grad_middle = upstream.astype(F32) + norm_back(middle, scale, gain, grad_second)
    wide_ref[...] = grad_middle
    branch = grad_middle.astype(BF16)
    branch_ref[...] = branch
    grad_ref[...] = dot_nt(out_ref[...], branch).astype(BF16)


def middle_call(*inputs):
    rows = (256, D)
    return whole_call(
        middle_kernel,
        jnp.zeros((1,), jnp.int32),
        inputs,
        [shape((D, 256), BF16)] + [shape(rows, BF16)] * 4 + [shape(rows, F32)] * 2,
        [],
        "middle",
        5 << 30,
        20 << 20,
        16,
    )


def square_kernel(place, *refs):
    inputs, (grad_ref, output_ref, turned) = refs[:14], refs[14:]
    middle_ref, down_ref = inputs[12:]
    core = place[2]
    output_ref[...] = (middle_ref[...] + dot(inputs[2][...], down_ref[:, 2 * D :])).astype(BF16)
    for m in range(3):
        left_ref, right_ref, left_far, right_far = inputs[m], inputs[3 + m], inputs[6 + m], inputs[9 + m]
        if m:
            turned[:, :256] = left_ref[...].T
            turned[:, 256:] = left_far[...].T
        else:
            turned[:, :256] = left_ref[...]
            turned[:, 256:] = left_far[...]

        def block(k, unused, right_ref=right_ref, right_far=right_far, m=m):
            near = right_ref[:, pl.ds(pl.multiple_of(640 * core + 128 * k, 128), 128)]
            far = right_far[:, pl.ds(pl.multiple_of(128 * k, 128), 128)]
            grad_ref[:, 5 * m + k] = dot(turned[...], jnp.concatenate([near, far], 0)).astype(BF16).reshape(4, 320, 128)
            return unused

        lax.fori_loop(0, 5, block, 0)
    grad_ref[:, 15] = jnp.zeros((4, 320, 128), BF16)


def square_call(place, *inputs):
    return whole_call(
        square_kernel,
        place,
        inputs,
        [shape((4, 16, 320, 128), BF16), shape((256, D), BF16)],
        [pltpu.VMEM((D, 512), BF16)],
        "square",
        6 << 30,
        20 << 20,
        10,
    )


def assemble_kernel(place, mine_ref, far_ref, in_ref, up_ref, in_grad_ref, out_grad_ref, up_grad_ref, down_grad_ref, scale_ref, one_ref, two_ref):
    core = place[2]
    total = jnp.zeros((8, 256), F32)
    for c in range(2):
        own = core == c
        pick = lambda h, rows: jnp.where(own, mine_ref[h, rows].astype(F32), far_ref[h, rows].astype(F32))
        heads = []
        for h in range(HEADS):
            total = total + pick(h, slice(160, 168))
            heads.append(pick(h, slice(0, 160)))
        for part in range(3):
            in_grad_ref[160 * c : 160 * c + 160, D * part : D * part + D] = jnp.concatenate(
                [head[:, HD * part : HD * part + HD] for head in heads], 1
            )
        for k in range(15):
            block = pick(k, slice(176, 336))
            ref = (out_grad_ref, up_grad_ref, down_grad_ref)[k // 5]
            lanes = slice(640 * c + 128 * (k % 5), 640 * c + 128 * (k % 5) + 128)
            ref[:160, lanes] = block[:, :128]
            ref[160:, lanes] = block[:, 128:]
    scale_ref[...] = total
    one_ref[...] = jnp.sum(in_grad_ref[...] * in_ref[...].astype(F32), 1, keepdims=True)
    two_ref[...] = jnp.sum(up_grad_ref[...] * up_ref[...].astype(F32), 1, keepdims=True)


def assemble_call(place, *inputs):
    return whole_call(
        assemble_kernel,
        place,
        inputs,
        [shape((320, 3 * D), F32)] + [shape((320, D), F32)] * 3 + [shape((8, 256), F32)] + [shape((320, 1), F32)] * 2,
        [],
        "assemble",
        1 << 20,
        20 << 20,
        28,
    )


def shift(value, axis, step):
    return lax.ppermute(value, axis, [(i, (i + step) % 4) for i in range(4)])


def other_core(value):
    return lax.ppermute(value, "core", [(0, 1), (1, 0)])


def scatter_y(parts):
    y = lax.axis_index("y")
    piece = lambda step: lax.dynamic_index_in_dim(parts, (y + step) % 4, 0, keepdims=False)
    return [piece(0)] + [shift(piece(step).astype(BF16), "y", step) for step in (1, 3, 2)]


def total_of(parts):
    return sum(part.astype(F32) for part in parts)


def gather_rows(value):
    rows = value.shape[0] // 2
    half = lax.dynamic_slice_in_dim(value, lax.axis_index("core") * rows, rows, 0)
    return lax.all_gather(half, ("y", "core"), axis=0, tiled=True)


def swap(value):
    return lax.all_to_all(value, CHIPS, 0, 0, tiled=True)


def local(tokens, segment_ids, cotangent, attn_in, attn_out, ffn_in, ffn_out, gain_attn, gain_ffn, query_scale):
    core = lax.axis_index("core")
    place = jnp.stack([lax.axis_index("x"), lax.axis_index("z"), core]).astype(jnp.int32)
    head = place[0] * 4 + place[1]
    inputs_low = tokens.reshape(256, D)
    upstream = cotangent.reshape(256, D)

    gathered = lax.all_gather(inputs_low, CHIPS, axis=0, tiled=True).reshape(16, 256, D)

    small = jnp.stack([gain_attn, gain_ffn, jnp.pad(query_scale, (0, 300))], 1)
    mine = lax.dynamic_index_in_dim(attn_in.reshape(320, 3, HEADS, HD), head, 2, keepdims=False).reshape(320, 3 * HD)
    small = lax.all_gather(jnp.concatenate([mine, jnp.pad(small, ((0, 0), (0, 13)))], 1), "y", axis=0, tiled=True)
    head_weights = small[:, : 3 * HD].T
    gain_one = small[:, 240].reshape(1, D).astype(F32)
    gain_two = small[:, 241].reshape(1, D).astype(F32)
    scale_raw = small[:, 242].reshape(4, 320)[:, :20].reshape(HD).astype(F32)
    factor = (jax.nn.softplus(scale_raw) * (QCONST / math.sqrt(HD)))[:, None]

    segments = lax.all_gather(segment_ids, ("x", "z", "core"), axis=1, tiled=True)
    begins = jnp.stack([jnp.sum((segments < k).astype(jnp.int32), 1) for k in range(1, 4)], 1)
    first_row = 512 * jnp.arange(8, dtype=jnp.int32) + 128 * core.astype(jnp.int32)
    start_of = lambda pos: jnp.max(jnp.where(begins[:, None] <= pos[None, :, None], begins[:, None], 0), 2)
    low = start_of(first_row) // 512
    high = jnp.minimum((start_of(first_row + 383) + 511) // 512, jnp.arange(8, dtype=jnp.int32)[None])
    high = jnp.maximum(low, high)
    bounds = jnp.concatenate([low.reshape(16), high.reshape(16), core[None].astype(jnp.int32), begins.reshape(6)])

    square_weights = jnp.concatenate([attn_out, ffn_in, ffn_out], 1)
    gathered, head_weights, bounds, gain_one, gain_two, factor, square_weights = lax.optimization_barrier(
        (gathered, head_weights, bounds, gain_one, gain_two, factor, square_weights)
    )
    weights = gather_rows(square_weights)
    first, own = project_call(gathered, gain_one, head_weights, factor * LOG2E)
    far = other_core(own[:, HD:])
    attended, attended_low, lse, keys = forward_call(bounds, own, far)
    attended_t = swap(attended_low).reshape(D, 256)
    grad_attended, branch, grad_pre, second, hidden, middle, grad_middle = middle_call(
        attended_t, inputs_low, upstream, gain_two, weights
    )
    grad_attended = swap(grad_attended.reshape(16, HD, 256))

    lefts, rights = (attended_t, second, hidden), (branch, grad_pre, upstream)
    traded = [other_core(value) for value in lefts]
    traded += [other_core(lax.dynamic_slice_in_dim(value, 640 * (1 - core), 640, 1)) for value in rights]
    squares, outputs = square_call(place, *lefts, *rights, *traded, middle, weights)

    grad_attended, squares, outputs = lax.optimization_barrier((grad_attended, squares, outputs))
    squares = lax.psum_scatter(squares, "y", scatter_dimension=0, tiled=True)[0]
    dq, scale_terms, dk_own, dv_own, dk_far, dv_far = backward_call(
        bounds, own, far, keys, attended, lse, grad_attended, factor
    )
    send, head_grad = weight_call(dq, dk_own, other_core(dk_far), dv_own, other_core(dv_far), first)
    send, head_grad, squares = lax.optimization_barrier((send, head_grad, squares))
    grad_project = swap(send)
    scale_part = jnp.pad(jnp.sum(scale_terms, 1).reshape(4, 1, 20), ((0, 0), (0, 15), (0, 236)))
    head_parts = head_grad.reshape(4, 2, 160, 256)
    give = lax.dynamic_index_in_dim(head_parts, 1 - core, 1, keepdims=False).astype(BF16)
    head_sum = lax.dynamic_index_in_dim(head_parts, core, 1, keepdims=False) + other_core(give).astype(F32)
    head_sum = total_of(scatter_y(jnp.concatenate([head_sum, scale_part], 1)))
    w_qkv = gather_rows(attn_in)
    columns = grad_project.reshape(HEADS, 3, HD, 256).transpose(1, 0, 2, 3).reshape(3 * D, 256)
    grad_first = lax.dot_general(columns, w_qkv, (((0,), (1,)), ((), ())), preferred_element_type=F32)
    inputs = inputs_low.astype(F32)
    input_grad = grad_middle + norm_back(inputs, norm_scale(inputs), gain_one, grad_first)
    squares = jnp.sum(swap(squares).astype(F32), 0)
    payload = jnp.concatenate([head_sum, jnp.concatenate([squares[:160], squares[160:]], 1)], 0).astype(BF16)
    payload = swap(jnp.broadcast_to(payload[None], (16, 336, 256)))
    payload, input_grad = lax.optimization_barrier((payload, input_grad))
    grad_in, grad_out, grad_up, grad_down, scale_sum, one, two = assemble_call(
        place, payload, other_core(payload), attn_in, ffn_in
    )
    own_scale = query_scale.astype(F32)
    slope = jax.nn.sigmoid(own_scale) / (jax.nn.softplus(own_scale) * LOG2E)
    return (
        outputs.reshape(2, 128, D),
        input_grad.reshape(2, 128, D),
        grad_in,
        grad_out,
        grad_up,
        grad_down,
        one[:, 0] / gain_attn.astype(F32),
        two[:, 0] / gain_ffn.astype(F32),
        scale_sum[0, :20] * slope,
    )


def solution(mesh):
    split = Mesh(mesh.devices.reshape(4, 4, 2, 4), ("x", "z", "core", "y"))
    rows = P("y", ("x", "z", "core"), None)
    weight = P("y", None)
    vector = P("y")
    return jax.shard_map(
        local,
        mesh=split,
        in_specs=(rows, P("y", ("x", "z", "core")), rows) + (weight,) * 4 + (vector,) * 3,
        out_specs=(rows, rows) + (weight,) * 4 + (vector,) * 3,
        check_vma=False,
    )
```

```python
import math

import jax
import jax.numpy as jnp
from jax import lax
from jax.experimental import pallas as pl
from jax.experimental.pallas import tpu as pltpu
from jax.sharding import Mesh
from jax.sharding import PartitionSpec as P

D = 1280
HEADS = 16
HD = 80
EPS = 1e-06
QCONST = 1.442695041
NEG = -1e30
LOG2E = math.log2(math.e)
F32 = jnp.float32
BF16 = jnp.bfloat16
CHIPS = ("x", "z")
shape = jax.ShapeDtypeStruct


def dot(a, b):
    return jnp.dot(a, b, preferred_element_type=F32)


def dot_nt(a, b):
    return lax.dot_general(a, b, (((1,), (1,)), ((), ())), preferred_element_type=F32)


def dot_tn(a, b):
    return lax.dot_general(a, b, (((0,), (0,)), ((), ())), preferred_element_type=F32)


def norm_scale(values):
    return lax.rsqrt(jnp.mean(values * values, -1, keepdims=True) + EPS)


def norm_back(values, scale, gain, grad):
    shaped = grad * gain
    inner = jnp.mean(shaped * values, -1, keepdims=True)
    return scale * shaped - values * (scale * scale * scale * inner)


def whole_call(kernel, scalars, inputs, out_shape, scratch, name, flops, moved, vmem_mib, left_out=()):
    def spec(index, array):
        if index in left_out:
            return pl.BlockSpec(memory_space=pl.ANY)
        return pl.BlockSpec(array.shape, lambda unused: (0,) * len(array.shape), pipeline_mode=pl.Buffered(1))

    return pl.pallas_call(
        kernel,
        grid=(1,),
        in_specs=[pl.BlockSpec(memory_space=pltpu.SMEM)] + [spec(i, array) for i, array in enumerate(inputs)],
        out_specs=[spec(None, array) for array in out_shape],
        out_shape=out_shape,
        scratch_shapes=scratch,
        compiler_params=pltpu.CompilerParams(vmem_limit_bytes=vmem_mib << 20),
        cost_estimate=pl.CostEstimate(flops=flops, bytes_accessed=moved, transcendentals=0),
        name=name,
    )(scalars, *inputs)


def project_kernel(x_ref, gain_ref, weight_ref, factor_ref, first_ref, out_ref, trade_ref):
    blocks = range(x_ref.shape[0])
    for g in blocks:
        x = x_ref[g].astype(F32)
        first_ref[g] = (x * norm_scale(x) * gain_ref[...]).astype(BF16)
    flat = [dot_nt(weight_ref[...], first_ref[g]) for g in blocks]
    for g in blocks:
        out_ref[g, :HD] = (flat[g][:HD] * factor_ref[...]).astype(BF16)
        low = flat[g][HD:].astype(BF16)
        out_ref[g, HD:] = low
        trade_ref[g] = low


def project_call(x, gain, weight, factor):
    step = 4
    whole = lambda *dims: pl.BlockSpec(dims, lambda g: (0,) * len(dims))
    block = lambda *dims: pl.BlockSpec((step,) + dims, lambda g: (g, 0, 0))
    return pl.pallas_call(
        project_kernel,
        grid=(16 // step,),
        in_specs=[block(256, D), whole(1, D), whole(3 * HD, D), whole(HD, 1)],
        out_specs=[block(256, D), block(3 * HD, 256), block(2 * HD, 256)],
        out_shape=[shape((16, 256, D), BF16), shape((16, 3 * HD, 256), BF16), shape((16, 2 * HD, 256), BF16)],
        compiler_params=pltpu.CompilerParams(vmem_limit_bytes=58 << 20),
        cost_estimate=pl.CostEstimate(flops=8 << 30, bytes_accessed=24 << 20, transcendentals=0),
        name="project",
    )(x, gain, weight, factor)


def rows_of(s):
    return pl.ds(pl.multiple_of(s * 128, 128), 128)


def wide_tile(ref, block, s, part=None):
    rows = slice(None) if part is None else slice(HD * part, HD * part + HD)
    return jnp.concatenate([ref[2 * block, rows, rows_of(s)], ref[2 * block + 1, rows, rows_of(s)]], 1)


def tall_tile(ref, which, block, s):
    return jnp.concatenate([ref[which, 2 * block, rows_of(s), :], ref[which, 2 * block + 1, rows_of(s), :]], 0)


def stand(out_ref, which, ref, part):
    row = lax.broadcasted_iota(jnp.int32, (128 - HD, 256), 0)
    ones = jnp.where(row < 3, 1.0, 0.0)

    def block(g, unused):
        wide = ref[g, HD * part : HD * part + HD].astype(F32)
        out_ref[which, g] = jnp.concatenate([wide, ones], 0).T.astype(BF16)
        return unused

    lax.fori_loop(0, 16, block, 0, unroll=4)


def put_wide(ref, block, s, value):
    ref[2 * block, :, rows_of(s)] = value[:, :128]
    ref[2 * block + 1, :, rows_of(s)] = value[:, 128:]


CHAINS = 4
GROUPS = 8 // CHAINS


def query_base():
    column = lax.broadcasted_iota(jnp.int32, (1, 256), 1)
    return column + jnp.where(column >= 128, 128, 0)


def fill_key_base(ref, core):
    row = lax.broadcasted_iota(jnp.int32, (512, 256), 0)
    inner = row % 256
    ref[...] = 128 * jnp.where(row < 256, core, 1 - core) + inner + jnp.where(inner >= 128, 128, 0)


def start_row(bounds, t, s):
    query_pos = 512 * t + 128 * bounds[32] + query_base()
    start = jnp.zeros_like(query_pos)
    for k in range(3):
        begin = bounds[33 + 3 * s + k]
        start = jnp.where(query_pos >= begin, begin, start)
    return start


def allowed(base_ref, bounds, starts, block, diagonal):
    keys = base_ref[...]
    mask = keys >= starts - 512 * block
    if diagonal:
        mask = mask & (keys <= query_base() + 128 * bounds[32])
    return mask


def group_loops(bounds, s, p, last, tile):
    first = CHAINS * p
    low, high = bounds[8 * s + first], bounds[16 + 8 * s + first + CHAINS - 1]
    pl.when(high <= first)(lambda: last(first, False))
    pl.when(high > first)(lambda: last(first, True))
    high = jnp.maximum(low, jnp.minimum(high, first))

    def loop(masked):
        def body(block, unused):
            tile(block, masked)
            return unused

        return body

    lax.fori_loop(high, first, loop(False), 0)
    lax.fori_loop(low, high, loop(True), 0)


LAST = [(j, c) for c in range(CHAINS) for j in range(c + 1)]


def forward_kernel(
    bounds, own_ref, far_ref, out_ref, low_ref, lse_ref, keys_ref, base_ref, best_ref, total_ref, accum_ref
):
    fill_key_base(base_ref, bounds[32])
    stand(keys_ref, 0, own_ref, 1)
    stand(keys_ref, 1, far_ref, 0)

    def group(index, unused):
        s, p = index // GROUPS, index % GROUPS
        queries = [wide_tile(own_ref, CHAINS * p + c, s, 0) for c in range(CHAINS)]
        starts = [start_row(bounds, CHAINS * p + c, s) for c in range(CHAINS)]
        keys_of = lambda block: jnp.concatenate([tall_tile(keys_ref, c, block, s) for c in range(2)], 0)[:, :HD]
        values_of = lambda block: jnp.concatenate([wide_tile(own_ref, block, s, 2), wide_tile(far_ref, block, s, 1)], 1)

        def last(first, masked):
            scores = {(j, c): dot(keys_of(first + j), queries[c]) for j, c in LAST}
            for j, c in LAST:
                if masked or j == c:
                    mask = allowed(base_ref, bounds, starts[c], first + j, j == c)
                    scores[j, c] = jnp.where(mask, scores[j, c], NEG)
            weights = []
            for c in range(CHAINS):
                best = jnp.max(scores[0, c], 0, keepdims=True)
                for j in range(1, c + 1):
                    best = jnp.maximum(best, jnp.max(scores[j, c], 0, keepdims=True))
                parts = [jnp.exp2(scores[j, c] - best) for j in range(c + 1)]
                best_ref[c] = best
                total_ref[c] = sum(jnp.sum(part, 0, keepdims=True) for part in parts)
                weights.append(jnp.concatenate([part.astype(BF16) for part in parts], 0))
            values = jnp.concatenate([values_of(first + j) for j in range(CHAINS)], 1)
            for c in range(CHAINS):
                accum_ref[c] = dot(values[:, : 512 * c + 512], weights[c])

        def tile(block, masked):
            keys, values = keys_of(block), values_of(block)
            scores = [dot(keys, queries[c]) for c in range(CHAINS)]
            weights, decay = [], []
            for c in range(CHAINS):
                if masked:
                    scores[c] = jnp.where(allowed(base_ref, bounds, starts[c], block, False), scores[c], NEG)
                best = best_ref[c]
                newest = jnp.maximum(best, jnp.max(scores[c], 0, keepdims=True))
                best_ref[c] = newest
                weights.append(jnp.exp2(scores[c] - newest))
                decay.append(jnp.exp2(best - newest))
                total_ref[c] = total_ref[c] * decay[c] + jnp.sum(weights[c], 0, keepdims=True)
            for c in range(CHAINS):
                accum_ref[c] = accum_ref[c] * decay[c] + dot(values, weights[c].astype(BF16))

        group_loops(bounds, s, p, last, tile)
        for c in range(CHAINS):
            t = CHAINS * p + c
            result = accum_ref[c] / total_ref[c]
            put_wide(out_ref, t, s, result)
            put_wide(low_ref, t, s, result.astype(BF16))
            put_wide(lse_ref, t, s, best_ref[c] + jnp.log2(total_ref[c]))
        return unused

    lax.fori_loop(0, 2 * GROUPS, group, 0)


def forward_call(bounds, *inputs):
    return whole_call(
        forward_kernel,
        bounds,
        inputs,
        [shape((16, HD, 256), F32), shape((16, HD, 256), BF16), shape((16, 1, 256), F32), shape((2, 16, 256, 128), BF16)],
        [
            pltpu.VMEM((512, 256), jnp.int32),
            pltpu.VMEM((CHAINS, 1, 256), F32),
            pltpu.VMEM((CHAINS, 1, 256), F32),
            pltpu.VMEM((CHAINS, HD, 256), F32),
        ],
        "attention",
        8 << 30,
        8 << 20,
        58,
    )


def tall(wide):
    return jnp.concatenate([wide, jnp.zeros((128 - HD, 256), F32)], 0).T.astype(BF16)


def with_row(wide, row):
    one = row.astype(BF16)
    rest = row - one.astype(F32)
    two = rest.astype(BF16)
    three = (rest - two.astype(F32)).astype(BF16)
    terms = jnp.concatenate([one.astype(F32), two.astype(F32), three.astype(F32), jnp.zeros((13, 256), F32)], 0)
    return jnp.concatenate([wide, terms.astype(BF16)], 0)


def backward_kernel(
    bounds, own_ref, far_ref, keys_ref, out_ref, lse_ref, grad_ref, factor_ref,
    dq_ref, scale_ref, dko_ref, dvo_ref, dkx_ref, dvx_ref,
    dko_acc, dvo_acc, dkx_acc, dvx_acc, base_ref, dq_acc, queries_ref, query_rows_ref, grads_ref, grad_rows_ref, values_ref,
):
    fill_key_base(base_ref, bounds[32])
    stand(values_ref, 0, own_ref, 2)
    stand(values_ref, 1, far_ref, 1)
    for ref in (dko_acc, dvo_acc, dkx_acc, dvx_acc):
        ref[...] = jnp.zeros_like(ref)
    scale_ref[...] = jnp.zeros_like(scale_ref)

    def group(index, unused):
        s, p = index // GROUPS, index % GROUPS
        starts = []
        for c in range(CHAINS):
            t = CHAINS * p + c
            starts.append(start_row(bounds, t, s))
            own = wide_tile(own_ref, t, s, 0)
            queries_ref[c] = with_row(own, -wide_tile(lse_ref, t, s))
            query_rows_ref[256 * c : 256 * c + 256] = tall(own.astype(F32))
            own = wide_tile(grad_ref, t, s)
            wide = own.astype(F32)
            grads_ref[c] = with_row(own, -jnp.sum(wide * wide_tile(out_ref, t, s), 0, keepdims=True))
            grad_rows_ref[256 * c : 256 * c + 256] = tall(wide)
        keys_of = lambda block: jnp.concatenate([tall_tile(keys_ref, c, block, s) for c in range(2)], 0)[:, :96]
        values_of = lambda block: jnp.concatenate([tall_tile(values_ref, c, block, s) for c in range(2)], 0)[:, :96]
        flat_of = lambda block: jnp.concatenate([wide_tile(own_ref, block, s, 1), wide_tile(far_ref, block, s, 0)], 1)

        def add(block, probs, dscores, least):
            dv = dot(jnp.concatenate(probs, 1), grad_rows_ref[256 * least :])
            dk = dot(jnp.concatenate(dscores, 1), query_rows_ref[256 * least :])
            for j in range(2):
                near, far = slice(128 * j, 128 * j + 128), slice(256 + 128 * j, 384 + 128 * j)
                dvo_acc[2 * block + j, rows_of(s), :] += dv[near]
                dko_acc[2 * block + j, rows_of(s), :] += dk[near]
                dvx_acc[2 * block + j, rows_of(s), :] += dv[far]
                dkx_acc[2 * block + j, rows_of(s), :] += dk[far]

        def weigh(scores, dprobs, mask):
            probs = jnp.exp2(scores)
            if mask is not None:
                probs = jnp.where(mask, probs, 0.0)
            return probs.astype(BF16), (probs * dprobs).astype(BF16)

        def last(first, masked):
            scores = {(j, c): dot(keys_of(first + j), queries_ref[c]) for j, c in LAST}
            dprobs = {(j, c): dot(values_of(first + j), grads_ref[c]) for j, c in LAST}
            pair = {}
            for j, c in LAST:
                mask = allowed(base_ref, bounds, starts[c], first + j, j == c) if masked or j == c else None
                pair[j, c] = weigh(scores[j, c], dprobs[j, c], mask)
            flat = jnp.concatenate([flat_of(first + j) for j in range(CHAINS)], 1)
            for c in range(CHAINS):
                dq_acc[c] = dot(flat[:, : 512 * c + 512], jnp.concatenate([pair[j, c][1] for j in range(c + 1)], 0))
            for j in range(CHAINS):
                probs, dscores = zip(*(pair[j, c] for c in range(j, CHAINS)))
                add(first + j, probs, dscores, j)

        def tile(block, masked):
            keys, values, flat = keys_of(block), values_of(block), flat_of(block)
            scores = [dot(keys, queries_ref[c]) for c in range(CHAINS)]
            dprobs = [dot(values, grads_ref[c]) for c in range(CHAINS)]
            masks = [allowed(base_ref, bounds, starts[c], block, False) if masked else None for c in range(CHAINS)]
            probs, dscores = zip(*(weigh(scores[c], dprobs[c], masks[c]) for c in range(CHAINS)))
            for c in range(CHAINS):
                dq_acc[c] += dot(flat, dscores[c])
            add(block, probs, dscores, 0)

        group_loops(bounds, s, p, last, tile)
        for c in range(CHAINS):
            t = CHAINS * p + c
            scale_ref[...] += dq_acc[c] * wide_tile(own_ref, t, s, 0).astype(F32)
            put_wide(dq_ref, t, s, (dq_acc[c] * factor_ref[...]).astype(BF16))
        return unused

    lax.fori_loop(0, 2 * GROUPS, group, 0)
    for ref, total in ((dkx_ref, dkx_acc), (dko_ref, dko_acc)):
        ref[...] = (total[...] * (1 / LOG2E)).astype(BF16)
    for ref, total in ((dvx_ref, dvx_acc), (dvo_ref, dvo_acc)):
        ref[...] = total[...].astype(BF16)


def backward_call(bounds, *inputs):
    rows = (16, 256, 128)
    return whole_call(
        backward_kernel,
        bounds,
        inputs,
        [shape((16, HD, 256), BF16), shape((HD, 256), F32)] + [shape(rows, BF16)] * 4,
        [
            *[pltpu.VMEM(rows, F32)] * 4,
            pltpu.VMEM((512, 256), jnp.int32),
            pltpu.VMEM((CHAINS, HD, 256), F32),
            pltpu.VMEM((CHAINS, 96, 256), BF16),
            pltpu.VMEM((CHAINS * 256, 128), BF16),
            pltpu.VMEM((CHAINS, 96, 256), BF16),
            pltpu.VMEM((CHAINS * 256, 128), BF16),
            pltpu.VMEM((2, 16, 256, 128), BF16),
        ],
        "attention_back",
        100 << 30,
        16 << 20,
        58,
    )


def weight_kernel(
    unused, dq_ref, dko_ref, dkr_ref, dvo_ref, dvr_ref, first_ref, send_ref, weight_ref, held, arrived
):
    copies = [pltpu.make_async_copy(first_ref.at[pl.ds(4 * i, 4)], held.at[pl.ds(4 * i, 4)], arrived.at[i]) for i in range(4)]
    for copy in copies:
        copy.start()

    def block(g, unused):
        send_ref[g, :HD] = dq_ref[g]
        for base, own_ref, far_ref in ((HD, dko_ref, dkr_ref), (2 * HD, dvo_ref, dvr_ref)):
            total = own_ref[g].astype(F32) + far_ref[g].astype(F32)
            send_ref[g, base : base + HD] = total.T[:HD].astype(BF16)
        return unused

    lax.fori_loop(0, 16, block, 0, unroll=2)
    total = 0.0
    for i in range(4):
        rows = jnp.concatenate([send_ref[g] for g in range(4 * i, 4 * i + 4)], 1)
        copies[i].wait()
        total = total + dot(rows, held[4 * i : 4 * i + 4].reshape(1024, D))
    weight_ref[...] = jnp.concatenate([total, jnp.zeros((16, D), F32)], 0).T


def weight_call(*inputs):
    return whole_call(
        weight_kernel,
        jnp.zeros((1,), jnp.int32),
        inputs,
        [shape((16, 3 * HD, 256), BF16), shape((D, 256), F32)],
        [pltpu.VMEM((16, 256, D), BF16), pltpu.SemaphoreType.DMA((4,))],
        "weight",
        12 << 30,
        24 << 20,
        58,
        (5,),
    )


def middle_kernel(
    unused, att_ref, x_ref, dy_ref, gain_ref, weights_ref,
    grad_ref, branch_ref, pre_ref, second_ref, hidden_ref, output_ref, wide_ref, held, arrived,
):
    gain = gain_ref[...]
    copies = [pltpu.make_async_copy(weights_ref.at[:, D * i : D * i + D], held.at[i], arrived.at[i]) for i in range(3)]
    for copy in copies:
        copy.start()
    out_ref, up_ref, down_ref = (held.at[i] for i in range(3))
    copies[0].wait()
    middle = x_ref[...].astype(F32) + dot_tn(att_ref[...], out_ref[...])
    scale = norm_scale(middle)
    second = (middle * scale * gain).astype(BF16)
    second_ref[...] = second
    upstream = dy_ref[...]
    copies[1].wait()
    hidden_pre = dot(second, up_ref[...])
    gate = jax.nn.sigmoid(hidden_pre)
    hidden_ref[...] = (hidden_pre * gate).astype(BF16)
    copies[2].wait()
    grad_hidden = dot_nt(upstream, down_ref[...])
    grad_pre = (grad_hidden * gate * (1.0 + hidden_pre * (1.0 - gate))).astype(BF16)
    pre_ref[...] = grad_pre
    grad_second = dot_nt(grad_pre, up_ref[...])
    grad_middle = upstream.astype(F32) + norm_back(middle, scale, gain, grad_second)
    wide_ref[...] = grad_middle
    branch = grad_middle.astype(BF16)
    branch_ref[...] = branch
    grad_ref[...] = dot_nt(out_ref[...], branch).astype(BF16)
    output_ref[...] = (middle + dot(hidden_ref[...], down_ref[...])).astype(BF16)


def middle_call(*inputs):
    rows = (256, D)
    return whole_call(
        middle_kernel,
        jnp.zeros((1,), jnp.int32),
        inputs,
        [shape((D, 256), BF16)] + [shape(rows, BF16)] * 5 + [shape(rows, F32)],
        [pltpu.VMEM((3, D, D), BF16), pltpu.SemaphoreType.DMA((3,))],
        "middle",
        5 << 30,
        20 << 20,
        58,
        (4,),
    )


def square_kernel(place, *refs):
    inputs, (grad_ref, turned) = refs[:12], refs[12:]
    core = place[2]
    for m in range(3):
        left_ref, right_ref, left_far, right_far = inputs[m], inputs[3 + m], inputs[6 + m], inputs[9 + m]
        if m:
            turned[:, :256] = left_ref[...].T
            turned[:, 256:] = left_far[...].T
        else:
            turned[:, :256] = left_ref[...]
            turned[:, 256:] = left_far[...]

        near = right_ref[:, pl.ds(pl.multiple_of(640 * core, 128), 640)]
        right = jnp.concatenate([near, right_far[...]], 0)
        parts = [dot(turned[320 * i : 320 * i + 320], right).astype(BF16) for i in range(4)]
        for i in range(4):
            for k in range(5):
                grad_ref[i, 5 * m + k] = parts[i][:, 128 * k : 128 * k + 128]
    grad_ref[:, 15] = jnp.zeros((4, 320, 128), BF16)


def square_call(place, *inputs):
    return whole_call(
        square_kernel,
        place,
        inputs,
        [shape((4, 16, 320, 128), BF16)],
        [pltpu.VMEM((D, 512), BF16)],
        "square",
        6 << 30,
        20 << 20,
        58,
    )


def assemble_kernel(place, mine_ref, far_ref, in_ref, up_ref, gain_ref, in_grad_ref, out_grad_ref, up_grad_ref, down_grad_ref, scale_ref, one_ref, two_ref):
    core = place[2]
    total = jnp.zeros((8, 256), F32)
    for c in range(2):
        own = core == c
        pick = lambda h, rows: jnp.where(own, mine_ref[h, rows].astype(F32), far_ref[h, rows].astype(F32))
        heads = []
        for h in range(HEADS):
            total = total + pick(h, slice(160, 168))
            heads.append(pick(h, slice(0, 160)))
        for part in range(3):
            in_grad_ref[160 * c : 160 * c + 160, D * part : D * part + D] = jnp.concatenate(
                [head[:, HD * part : HD * part + HD] for head in heads], 1
            )
        for k in range(15):
            block = pick(k, slice(176, 336))
            ref = (out_grad_ref, up_grad_ref, down_grad_ref)[k // 5]
            lanes = slice(640 * c + 128 * (k % 5), 640 * c + 128 * (k % 5) + 128)
            ref[:160, lanes] = block[:, :128]
            ref[160:, lanes] = block[:, 128:]
    scale_ref[...] = total
    for row, (total_ref, grad_ref, ref) in enumerate(((one_ref, in_grad_ref, in_ref), (two_ref, up_grad_ref, up_ref))):
        terms = grad_ref[...] * ref[...].astype(F32)
        terms = sum(terms[:, 128 * k : 128 * k + 128] for k in range(terms.shape[1] // 128))
        total_ref[...] = jnp.sum(terms.T, 0, keepdims=True) / gain_ref[row : row + 1, :320]


def assemble_call(place, *inputs):
    return whole_call(
        assemble_kernel,
        place,
        inputs,
        [shape((320, 3 * D), F32)] + [shape((320, D), F32)] * 3 + [shape((8, 256), F32)] + [shape((1, 320), F32)] * 2,
        [],
        "assemble",
        1 << 20,
        20 << 20,
        58,
    )


def shift(value, axis, step):
    return lax.ppermute(value, axis, [(i, (i + step) % 4) for i in range(4)])


def other_core(value):
    return lax.ppermute(value, "core", [(0, 1), (1, 0)])


def scatter_y(parts):
    y = lax.axis_index("y")
    piece = lambda step: lax.dynamic_index_in_dim(parts, (y + step) % 4, 0, keepdims=False)
    return [piece(0)] + [shift(piece(step).astype(BF16), "y", step) for step in (1, 3, 2)]


def total_of(parts):
    return sum(part.astype(F32) for part in parts)


def gather_rows(value):
    rows = value.shape[0] // 2
    half = lax.dynamic_slice_in_dim(value, lax.axis_index("core") * rows, rows, 0)
    return lax.all_gather(half, ("y", "core"), axis=0, tiled=True)


def swap(value):
    return lax.all_to_all(value, CHIPS, 0, 0, tiled=True)


def local(tokens, segment_ids, cotangent, attn_in, attn_out, ffn_in, ffn_out, gain_attn, gain_ffn, query_scale):
    core = lax.axis_index("core")
    place = jnp.stack([lax.axis_index("x"), lax.axis_index("z"), core]).astype(jnp.int32)
    head = place[0] * 4 + place[1]
    inputs_low = tokens.reshape(256, D)
    upstream = cotangent.reshape(256, D)

    gathered = lax.all_gather(inputs_low, CHIPS, axis=0, tiled=True).reshape(16, 256, D)

    small = jnp.stack([gain_attn, gain_ffn, jnp.pad(query_scale, (0, 300))], 1)
    mine = lax.dynamic_index_in_dim(attn_in.reshape(320, 3, HEADS, HD), head, 2, keepdims=False).reshape(320, 3 * HD)
    small = lax.all_gather(jnp.concatenate([mine, jnp.pad(small, ((0, 0), (0, 13)))], 1), "y", axis=0, tiled=True)
    head_weights = small[:, : 3 * HD].T
    gain_one = small[:, 240].reshape(1, D).astype(F32)
    gain_two = small[:, 241].reshape(1, D).astype(F32)
    scale_raw = small[:, 242].reshape(4, 320)[:, :20].reshape(HD).astype(F32)
    factor = (jax.nn.softplus(scale_raw) * (QCONST / math.sqrt(HD)))[:, None]

    segments = lax.all_gather(segment_ids, ("x", "z", "core"), axis=1, tiled=True)
    begins = jnp.stack([jnp.sum((segments < k).astype(jnp.int32), 1) for k in range(1, 4)], 1)
    first_row = 512 * jnp.arange(8, dtype=jnp.int32) + 128 * core.astype(jnp.int32)
    start_of = lambda pos: jnp.max(jnp.where(begins[:, None] <= pos[None, :, None], begins[:, None], 0), 2)
    low = start_of(first_row) // 512
    high = jnp.minimum((start_of(first_row + 383) + 511) // 512, jnp.arange(8, dtype=jnp.int32)[None])
    high = jnp.maximum(low, high)
    bounds = jnp.concatenate([low.reshape(16), high.reshape(16), core[None].astype(jnp.int32), begins.reshape(6)])

    square_weights = jnp.concatenate([attn_out, ffn_in, ffn_out], 1)
    gathered, head_weights, bounds, gain_one, gain_two, factor, square_weights = lax.optimization_barrier(
        (gathered, head_weights, bounds, gain_one, gain_two, factor, square_weights)
    )
    weights = gather_rows(square_weights)
    first, own, trade = project_call(gathered, gain_one, head_weights, factor * LOG2E)
    far = other_core(trade)
    attended, attended_low, lse, keys = forward_call(bounds, own, far)
    attended_t = swap(attended_low).reshape(D, 256)
    grad_attended, branch, grad_pre, second, hidden, outputs, grad_middle = middle_call(
        attended_t, inputs_low, upstream, gain_two, weights
    )
    grad_attended = swap(grad_attended.reshape(16, HD, 256))

    lefts, rights = (attended_t, second, hidden), (branch, grad_pre, upstream)
    traded = [other_core(value) for value in lefts]
    traded += [other_core(lax.dynamic_slice_in_dim(value, 640 * (1 - core), 640, 1)) for value in rights]
    (squares,) = square_call(place, *lefts, *rights, *traded)

    grad_attended, squares = lax.optimization_barrier((grad_attended, squares))
    squares = lax.psum_scatter(squares, "y", scatter_dimension=0, tiled=True)[0]
    dq, scale_terms, dk_own, dv_own, dk_far, dv_far = backward_call(
        bounds, own, far, keys, attended, lse, grad_attended, factor
    )
    send, head_grad = weight_call(dq, dk_own, other_core(dk_far), dv_own, other_core(dv_far), first)
    scale_part = jnp.pad(jnp.sum(scale_terms, 1).reshape(4, 1, 20), ((0, 0), (0, 15), (0, 236)))
    head_parts = head_grad.reshape(4, 2, 160, 256)
    give = lax.dynamic_index_in_dim(head_parts, 1 - core, 1, keepdims=False).astype(BF16)
    head_sum = lax.dynamic_index_in_dim(head_parts, core, 1, keepdims=False) + other_core(give).astype(F32)
    head_sum = total_of(scatter_y(jnp.concatenate([head_sum, scale_part], 1)))
    grad_project, head_sum, squares = lax.optimization_barrier((swap(send), head_sum, squares))
    squares = jnp.sum(swap(squares).astype(F32), 0)
    payload = jnp.concatenate([head_sum, jnp.concatenate([squares[:160], squares[160:]], 1)], 0).astype(BF16)
    w_qkv = gather_rows(attn_in)
    columns = grad_project.reshape(HEADS, 3, HD, 256).transpose(1, 0, 2, 3).reshape(3 * D, 256)
    grad_first = lax.dot_general(columns, w_qkv, (((0,), (1,)), ((), ())), preferred_element_type=F32)
    inputs = inputs_low.astype(F32)
    input_grad = grad_middle + norm_back(inputs, norm_scale(inputs), gain_one, grad_first)
    payload = swap(jnp.broadcast_to(payload[None], (16, 336, 256)))
    payload, input_grad = lax.optimization_barrier((payload, input_grad))
    own_gains = jnp.stack([gain_attn, gain_ffn]).astype(F32)
    grad_in, grad_out, grad_up, grad_down, scale_sum, one, two = assemble_call(
        place, payload, other_core(payload), attn_in, ffn_in, own_gains
    )
    own_scale = query_scale.astype(F32)
    slope = jax.nn.sigmoid(own_scale) / (jax.nn.softplus(own_scale) * LOG2E)
    return (
        outputs.reshape(2, 128, D),
        input_grad.reshape(2, 128, D),
        grad_in,
        grad_out,
        grad_up,
        grad_down,
        one[0],
        two[0],
        scale_sum[0, :20] * slope,
    )


def solution(mesh):
    split = Mesh(mesh.devices.reshape(4, 4, 2, 4), ("x", "z", "core", "y"))
    rows = P("y", ("x", "z", "core"), None)
    weight = P("y", None)
    vector = P("y")
    return jax.shard_map(
        local,
        mesh=split,
        in_specs=(rows, P("y", ("x", "z", "core")), rows) + (weight,) * 4 + (vector,) * 3,
        out_specs=(rows, rows) + (weight,) * 4 + (vector,) * 3,
        check_vma=False,
    )
```

```python
import math

import jax
import jax.numpy as jnp
from jax import lax
from jax.experimental import pallas as pl
from jax.experimental.pallas import tpu as pltpu
from jax.sharding import Mesh
from jax.sharding import PartitionSpec as P

D = 1280
HEADS = 16
HD = 80
EPS = 1e-06
QCONST = 1.442695041
NEG = -1e30
LOG2E = math.log2(math.e)
F32 = jnp.float32
BF16 = jnp.bfloat16
CHIPS = ("x", "z")
shape = jax.ShapeDtypeStruct


def dot(a, b):
    return jnp.dot(a, b, preferred_element_type=F32)


def dot_nt(a, b):
    return lax.dot_general(a, b, (((1,), (1,)), ((), ())), preferred_element_type=F32)


def dot_tn(a, b):
    return lax.dot_general(a, b, (((0,), (0,)), ((), ())), preferred_element_type=F32)


def norm_scale(values):
    return lax.rsqrt(jnp.mean(values * values, -1, keepdims=True) + EPS)


def norm_back(values, scale, gain, grad):
    shaped = grad * gain
    inner = jnp.mean(shaped * values, -1, keepdims=True)
    return scale * shaped - values * (scale * scale * scale * inner)


def whole_call(kernel, scalars, inputs, out_shape, scratch, name, flops, moved, vmem_mib, left_out=()):
    def spec(index, array):
        if index in left_out:
            return pl.BlockSpec(memory_space=pl.ANY)
        return pl.BlockSpec(array.shape, lambda unused: (0,) * len(array.shape), pipeline_mode=pl.Buffered(1))

    return pl.pallas_call(
        kernel,
        grid=(1,),
        in_specs=[pl.BlockSpec(memory_space=pltpu.SMEM)] + [spec(i, array) for i, array in enumerate(inputs)],
        out_specs=[spec(None, array) for array in out_shape],
        out_shape=out_shape,
        scratch_shapes=scratch,
        compiler_params=pltpu.CompilerParams(vmem_limit_bytes=vmem_mib << 20),
        cost_estimate=pl.CostEstimate(flops=flops, bytes_accessed=moved, transcendentals=0),
        name=name,
    )(scalars, *inputs)


def project_kernel(x_ref, gain_ref, weight_ref, factor_ref, first_ref, out_ref, trade_ref):
    blocks = range(x_ref.shape[0])
    for g in blocks:
        x = x_ref[g].astype(F32)
        first_ref[g] = (x * norm_scale(x) * gain_ref[...]).astype(BF16)
    flat = [dot_nt(weight_ref[...], first_ref[g]) for g in blocks]
    for g in blocks:
        out_ref[g, :HD] = (flat[g][:HD] * factor_ref[...]).astype(BF16)
        low = flat[g][HD:].astype(BF16)
        out_ref[g, HD:] = low
        trade_ref[g] = low


def project_call(x, gain, weight, factor):
    step = 4
    whole = lambda *dims: pl.BlockSpec(dims, lambda g: (0,) * len(dims))
    block = lambda *dims: pl.BlockSpec((step,) + dims, lambda g: (g, 0, 0))
    return pl.pallas_call(
        project_kernel,
        grid=(16 // step,),
        in_specs=[block(256, D), whole(1, D), whole(3 * HD, D), whole(HD, 1)],
        out_specs=[block(256, D), block(3 * HD, 256), block(2 * HD, 256)],
        out_shape=[shape((16, 256, D), BF16), shape((16, 3 * HD, 256), BF16), shape((16, 2 * HD, 256), BF16)],
        compiler_params=pltpu.CompilerParams(vmem_limit_bytes=58 << 20),
        cost_estimate=pl.CostEstimate(flops=8 << 30, bytes_accessed=24 << 20, transcendentals=0),
        name="project",
    )(x, gain, weight, factor)


def rows_of(s):
    return pl.ds(pl.multiple_of(s * 128, 128), 128)


def wide_tile(ref, block, s, part=None):
    rows = slice(None) if part is None else slice(HD * part, HD * part + HD)
    return jnp.concatenate([ref[2 * block, rows, rows_of(s)], ref[2 * block + 1, rows, rows_of(s)]], 1)


def tall_tile(ref, which, block, s):
    return jnp.concatenate([ref[which, 2 * block, rows_of(s), :], ref[which, 2 * block + 1, rows_of(s), :]], 0)


def stand(out_ref, which, ref, part):
    row = lax.broadcasted_iota(jnp.int32, (128 - HD, 256), 0)
    ones = jnp.where(row < 3, 1.0, 0.0)

    def block(g, unused):
        wide = ref[g, HD * part : HD * part + HD].astype(F32)
        out_ref[which, g] = jnp.concatenate([wide, ones], 0).T.astype(BF16)
        return unused

    lax.fori_loop(0, 16, block, 0, unroll=4)


def put_wide(ref, block, s, value):
    ref[2 * block, :, rows_of(s)] = value[:, :128]
    ref[2 * block + 1, :, rows_of(s)] = value[:, 128:]


CHAINS = 4
GROUPS = 8 // CHAINS


def query_base():
    column = lax.broadcasted_iota(jnp.int32, (1, 256), 1)
    return column + jnp.where(column >= 128, 128, 0)


def fill_key_base(ref, core):
    row = lax.broadcasted_iota(jnp.int32, (512, 256), 0)
    inner = row % 256
    ref[...] = 128 * jnp.where(row < 256, core, 1 - core) + inner + jnp.where(inner >= 128, 128, 0)


def start_row(bounds, t, s):
    query_pos = 512 * t + 128 * bounds[32] + query_base()
    start = jnp.zeros_like(query_pos)
    for k in range(3):
        begin = bounds[33 + 3 * s + k]
        start = jnp.where(query_pos >= begin, begin, start)
    return start


def allowed(base_ref, bounds, starts, block, diagonal):
    keys = base_ref[...]
    mask = keys >= starts - 512 * block
    if diagonal:
        mask = mask & (keys <= query_base() + 128 * bounds[32])
    return mask


def group_loops(bounds, s, p, last, tile):
    first = CHAINS * p
    low, high = bounds[8 * s + first], bounds[16 + 8 * s + first + CHAINS - 1]
    pl.when(high <= first)(lambda: last(first, False))
    pl.when(high > first)(lambda: last(first, True))
    high = jnp.maximum(low, jnp.minimum(high, first))

    def loop(masked):
        def body(block, unused):
            tile(block, masked)
            return unused

        return body

    lax.fori_loop(high, first, loop(False), 0)
    lax.fori_loop(low, high, loop(True), 0)


LAST = [(j, c) for c in range(CHAINS) for j in range(c + 1)]


def forward_kernel(
    bounds, own_ref, far_ref, out_ref, low_ref, lse_ref, keys_ref, base_ref, best_ref, total_ref, accum_ref
):
    fill_key_base(base_ref, bounds[32])
    stand(keys_ref, 0, own_ref, 1)
    stand(keys_ref, 1, far_ref, 0)

    def group(index, unused):
        s, p = index // GROUPS, index % GROUPS
        queries = [wide_tile(own_ref, CHAINS * p + c, s, 0) for c in range(CHAINS)]
        starts = [start_row(bounds, CHAINS * p + c, s) for c in range(CHAINS)]
        keys_of = lambda block: jnp.concatenate([tall_tile(keys_ref, c, block, s) for c in range(2)], 0)[:, :HD]
        values_of = lambda block: jnp.concatenate([wide_tile(own_ref, block, s, 2), wide_tile(far_ref, block, s, 1)], 1)

        def last(first, masked):
            scores = {(j, c): dot(keys_of(first + j), queries[c]) for j, c in LAST}
            for j, c in LAST:
                if masked or j == c:
                    mask = allowed(base_ref, bounds, starts[c], first + j, j == c)
                    scores[j, c] = jnp.where(mask, scores[j, c], NEG)
            weights = []
            for c in range(CHAINS):
                best = jnp.max(scores[0, c], 0, keepdims=True)
                for j in range(1, c + 1):
                    best = jnp.maximum(best, jnp.max(scores[j, c], 0, keepdims=True))
                parts = [jnp.exp2(scores[j, c] - best) for j in range(c + 1)]
                best_ref[c] = best
                total_ref[c] = sum(jnp.sum(part, 0, keepdims=True) for part in parts)
                weights.append(jnp.concatenate([part.astype(BF16) for part in parts], 0))
            values = jnp.concatenate([values_of(first + j) for j in range(CHAINS)], 1)
            for c in range(CHAINS):
                accum_ref[c] = dot(values[:, : 512 * c + 512], weights[c])

        def tile(block, masked):
            keys, values = keys_of(block), values_of(block)
            scores = [dot(keys, queries[c]) for c in range(CHAINS)]
            weights, decay = [], []
            for c in range(CHAINS):
                if masked:
                    scores[c] = jnp.where(allowed(base_ref, bounds, starts[c], block, False), scores[c], NEG)
                best = best_ref[c]
                newest = jnp.maximum(best, jnp.max(scores[c], 0, keepdims=True))
                best_ref[c] = newest
                weights.append(jnp.exp2(scores[c] - newest))
                decay.append(jnp.exp2(best - newest))
                total_ref[c] = total_ref[c] * decay[c] + jnp.sum(weights[c], 0, keepdims=True)
            for c in range(CHAINS):
                accum_ref[c] = accum_ref[c] * decay[c] + dot(values, weights[c].astype(BF16))

        group_loops(bounds, s, p, last, tile)
        for c in range(CHAINS):
            t = CHAINS * p + c
            result = accum_ref[c] / total_ref[c]
            put_wide(out_ref, t, s, result)
            put_wide(low_ref, t, s, result.astype(BF16))
            put_wide(lse_ref, t, s, best_ref[c] + jnp.log2(total_ref[c]))
        return unused

    lax.fori_loop(0, 2 * GROUPS, group, 0)


def forward_call(bounds, *inputs):
    return whole_call(
        forward_kernel,
        bounds,
        inputs,
        [shape((16, HD, 256), F32), shape((16, HD, 256), BF16), shape((16, 1, 256), F32), shape((2, 16, 256, 128), BF16)],
        [
            pltpu.VMEM((512, 256), jnp.int32),
            pltpu.VMEM((CHAINS, 1, 256), F32),
            pltpu.VMEM((CHAINS, 1, 256), F32),
            pltpu.VMEM((CHAINS, HD, 256), F32),
        ],
        "attention",
        8 << 30,
        8 << 20,
        58,
    )


def tall(wide):
    return jnp.concatenate([wide, jnp.zeros((128 - HD, 256), F32)], 0).T.astype(BF16)


def with_row(wide, row):
    one = row.astype(BF16)
    rest = row - one.astype(F32)
    two = rest.astype(BF16)
    three = (rest - two.astype(F32)).astype(BF16)
    terms = jnp.concatenate([one.astype(F32), two.astype(F32), three.astype(F32), jnp.zeros((13, 256), F32)], 0)
    return jnp.concatenate([wide, terms.astype(BF16)], 0)


def backward_kernel(
    bounds, own_ref, far_ref, keys_ref, out_ref, lse_ref, grad_ref, factor_ref,
    dq_ref, scale_ref, dko_ref, dvo_ref, dkx_ref, dvx_ref,
    dko_acc, dvo_acc, dkx_acc, dvx_acc, base_ref, dq_acc, queries_ref, query_rows_ref, grads_ref, grad_rows_ref, values_ref,
):
    fill_key_base(base_ref, bounds[32])
    stand(values_ref, 0, own_ref, 2)
    stand(values_ref, 1, far_ref, 1)
    for ref in (dko_acc, dvo_acc, dkx_acc, dvx_acc):
        ref[...] = jnp.zeros_like(ref)
    scale_ref[...] = jnp.zeros_like(scale_ref)

    def group(index, unused):
        s, p = index // GROUPS, index % GROUPS
        starts = []
        for c in range(CHAINS):
            t = CHAINS * p + c
            starts.append(start_row(bounds, t, s))
            own = wide_tile(own_ref, t, s, 0)
            queries_ref[c] = with_row(own, -wide_tile(lse_ref, t, s))
            query_rows_ref[256 * c : 256 * c + 256] = tall(own.astype(F32))
            own = wide_tile(grad_ref, t, s)
            wide = own.astype(F32)
            grads_ref[c] = with_row(own, -jnp.sum(wide * wide_tile(out_ref, t, s), 0, keepdims=True))
            grad_rows_ref[256 * c : 256 * c + 256] = tall(wide)
        keys_of = lambda block: jnp.concatenate([tall_tile(keys_ref, c, block, s) for c in range(2)], 0)[:, :96]
        values_of = lambda block: jnp.concatenate([tall_tile(values_ref, c, block, s) for c in range(2)], 0)[:, :96]
        flat_of = lambda block: jnp.concatenate([wide_tile(own_ref, block, s, 1), wide_tile(far_ref, block, s, 0)], 1)

        def add(block, probs, dscores, least):
            dv = dot(jnp.concatenate(probs, 1), grad_rows_ref[256 * least :])
            dk = dot(jnp.concatenate(dscores, 1), query_rows_ref[256 * least :])
            for j in range(2):
                near, far = slice(128 * j, 128 * j + 128), slice(256 + 128 * j, 384 + 128 * j)
                dvo_acc[2 * block + j, rows_of(s), :] += dv[near]
                dko_acc[2 * block + j, rows_of(s), :] += dk[near]
                dvx_acc[2 * block + j, rows_of(s), :] += dv[far]
                dkx_acc[2 * block + j, rows_of(s), :] += dk[far]

        def weigh(scores, dprobs, mask):
            probs = jnp.exp2(scores)
            if mask is not None:
                probs = jnp.where(mask, probs, 0.0)
            return probs.astype(BF16), (probs * dprobs).astype(BF16)

        def last(first, masked):
            scores = {(j, c): dot(keys_of(first + j), queries_ref[c]) for j, c in LAST}
            dprobs = {(j, c): dot(values_of(first + j), grads_ref[c]) for j, c in LAST}
            pair = {}
            for j, c in LAST:
                mask = allowed(base_ref, bounds, starts[c], first + j, j == c) if masked or j == c else None
                pair[j, c] = weigh(scores[j, c], dprobs[j, c], mask)
            flat = jnp.concatenate([flat_of(first + j) for j in range(CHAINS)], 1)
            for c in range(CHAINS):
                dq_acc[c] = dot(flat[:, : 512 * c + 512], jnp.concatenate([pair[j, c][1] for j in range(c + 1)], 0))
            for j in range(CHAINS):
                probs, dscores = zip(*(pair[j, c] for c in range(j, CHAINS)))
                add(first + j, probs, dscores, j)

        def tile(block, masked):
            keys, values, flat = keys_of(block), values_of(block), flat_of(block)
            scores = [dot(keys, queries_ref[c]) for c in range(CHAINS)]
            dprobs = [dot(values, grads_ref[c]) for c in range(CHAINS)]
            masks = [allowed(base_ref, bounds, starts[c], block, False) if masked else None for c in range(CHAINS)]
            probs, dscores = zip(*(weigh(scores[c], dprobs[c], masks[c]) for c in range(CHAINS)))
            for c in range(CHAINS):
                dq_acc[c] += dot(flat, dscores[c])
            add(block, probs, dscores, 0)

        group_loops(bounds, s, p, last, tile)
        for c in range(CHAINS):
            t = CHAINS * p + c
            scale_ref[...] += dq_acc[c] * wide_tile(own_ref, t, s, 0).astype(F32)
            put_wide(dq_ref, t, s, (dq_acc[c] * factor_ref[...]).astype(BF16))
        return unused

    lax.fori_loop(0, 2 * GROUPS, group, 0)
    for ref, total in ((dkx_ref, dkx_acc), (dko_ref, dko_acc)):
        ref[...] = (total[...] * (1 / LOG2E)).astype(BF16)
    for ref, total in ((dvx_ref, dvx_acc), (dvo_ref, dvo_acc)):
        ref[...] = total[...].astype(BF16)


def backward_call(bounds, *inputs):
    rows = (16, 256, 128)
    return whole_call(
        backward_kernel,
        bounds,
        inputs,
        [shape((16, HD, 256), BF16), shape((HD, 256), F32)] + [shape(rows, BF16)] * 4,
        [
            *[pltpu.VMEM(rows, F32)] * 4,
            pltpu.VMEM((512, 256), jnp.int32),
            pltpu.VMEM((CHAINS, HD, 256), F32),
            pltpu.VMEM((CHAINS, 96, 256), BF16),
            pltpu.VMEM((CHAINS * 256, 128), BF16),
            pltpu.VMEM((CHAINS, 96, 256), BF16),
            pltpu.VMEM((CHAINS * 256, 128), BF16),
            pltpu.VMEM((2, 16, 256, 128), BF16),
        ],
        "attention_back",
        60 << 30,
        16 << 20,
        58,
    )


def weight_kernel(
    unused, dq_ref, dko_ref, dkr_ref, dvo_ref, dvr_ref, first_ref, send_ref, weight_ref, held, arrived
):
    copies = [pltpu.make_async_copy(first_ref.at[pl.ds(4 * i, 4)], held.at[pl.ds(4 * i, 4)], arrived.at[i]) for i in range(4)]
    for copy in copies:
        copy.start()

    def block(g, unused):
        send_ref[g, :HD] = dq_ref[g]
        for base, own_ref, far_ref in ((HD, dko_ref, dkr_ref), (2 * HD, dvo_ref, dvr_ref)):
            total = own_ref[g].astype(F32) + far_ref[g].astype(F32)
            send_ref[g, base : base + HD] = total.T[:HD].astype(BF16)
        return unused

    lax.fori_loop(0, 16, block, 0, unroll=2)
    total = 0.0
    for i in range(4):
        rows = jnp.concatenate([send_ref[g] for g in range(4 * i, 4 * i + 4)], 1)
        copies[i].wait()
        total = total + dot(rows, held[4 * i : 4 * i + 4].reshape(1024, D))
    weight_ref[...] = jnp.concatenate([total, jnp.zeros((16, D), F32)], 0).T


def weight_call(*inputs):
    return whole_call(
        weight_kernel,
        jnp.zeros((1,), jnp.int32),
        inputs,
        [shape((16, 3 * HD, 256), BF16), shape((D, 256), F32)],
        [pltpu.VMEM((16, 256, D), BF16), pltpu.SemaphoreType.DMA((4,))],
        "weight",
        12 << 30,
        24 << 20,
        58,
        (5,),
    )


def middle_kernel(
    place, att_ref, x_ref, dy_ref, gain_ref, weights_ref,
    grad_ref, branch_ref, pre_ref, second_ref, hidden_ref, output_ref, wide_ref, branch_half, pre_half, held, arrived,
):
    far = pl.ds(pl.multiple_of(640 * (1 - place[2]), 128), 640)
    gain = gain_ref[...]
    copies = [pltpu.make_async_copy(weights_ref.at[:, D * i : D * i + D], held.at[i], arrived.at[i]) for i in range(3)]
    for copy in copies:
        copy.start()
    out_ref, up_ref, down_ref = (held.at[i] for i in range(3))
    copies[0].wait()
    middle = x_ref[...].astype(F32) + dot_tn(att_ref[...], out_ref[...])
    scale = norm_scale(middle)
    second = (middle * scale * gain).astype(BF16)
    second_ref[...] = second
    upstream = dy_ref[...]
    copies[1].wait()
    hidden_pre = dot(second, up_ref[...])
    gate = jax.nn.sigmoid(hidden_pre)
    hidden_ref[...] = (hidden_pre * gate).astype(BF16)
    copies[2].wait()
    grad_hidden = dot_nt(upstream, down_ref[...])
    grad_pre = (grad_hidden * gate * (1.0 + hidden_pre * (1.0 - gate))).astype(BF16)
    pre_ref[...] = grad_pre
    grad_second = dot_nt(grad_pre, up_ref[...])
    grad_middle = upstream.astype(F32) + norm_back(middle, scale, gain, grad_second)
    wide_ref[...] = grad_middle
    branch = grad_middle.astype(BF16)
    branch_ref[...] = branch
    branch_half[...] = branch_ref[:, far]
    pre_half[...] = pre_ref[:, far]
    grad_ref[...] = dot_nt(out_ref[...], branch).astype(BF16)
    output_ref[...] = (middle + dot(hidden_ref[...], down_ref[...])).astype(BF16)


def middle_call(place, *inputs):
    rows = (256, D)
    return whole_call(
        middle_kernel,
        place,
        inputs,
        [shape((D, 256), BF16)] + [shape(rows, BF16)] * 5 + [shape(rows, F32)] + [shape((256, 640), BF16)] * 2,
        [pltpu.VMEM((3, D, D), BF16), pltpu.SemaphoreType.DMA((3,))],
        "middle",
        5 << 30,
        20 << 20,
        58,
        (4,),
    )


def square_kernel(place, *refs):
    inputs, (early_ref, late_ref, turned) = refs[:12], refs[12:]
    core = place[2]
    for m in range(3):
        left_ref, right_ref, left_far, right_far = inputs[m], inputs[3 + m], inputs[6 + m], inputs[9 + m]
        if m:
            turned[:, :256] = left_ref[...].T
            turned[:, 256:] = left_far[...].T
        else:
            turned[:, :256] = left_ref[...]
            turned[:, 256:] = left_far[...]
        near = right_ref[:, pl.ds(pl.multiple_of(640 * core, 128), 640)]
        right = jnp.concatenate([near, right_far[...]], 0)
        parts = [dot(turned[320 * i : 320 * i + 320], right).astype(BF16) for i in range(4)]
        for i in range(4):
            for k in range(5):
                block = parts[i][:, 128 * k : 128 * k + 128]
                index = 5 * m + k
                if index < 8:
                    early_ref[i, index] = block
                else:
                    late_ref[2 * index - 16, i] = block[:160]
                    late_ref[2 * index - 15, i] = block[160:]
    for index in (14, 15):
        late_ref[index] = jnp.zeros((4, 160, 128), BF16)


def square_call(place, *inputs):
    return whole_call(
        square_kernel,
        place,
        inputs,
        [shape((4, 8, 320, 128), BF16), shape((16, 4, 160, 128), BF16)],
        [pltpu.VMEM((D, 512), BF16)],
        "square",
        6 << 30,
        20 << 20,
        58,
    )


def row_totals(grad, weight):
    terms = grad * weight.astype(F32)
    terms = sum(terms[:, 128 * k : 128 * k + 128] for k in range(terms.shape[1] // 128))
    return jnp.sum(terms.T, 0, keepdims=True)


def assemble_kernel(which, part_ref, in_ref, up_ref, *refs):
    before, (in_grad_ref, out_grad_ref, up_grad_ref, down_grad_ref, one_ref, scale_ref, two_ref) = refs[:-7], refs[-7:]
    heads = [part_ref[h, :160].astype(F32) for h in range(HEADS)]
    for part in range(3):
        in_grad_ref[:, D * part : D * part + D] = jnp.concatenate([head[:, HD * part : HD * part + HD] for head in heads], 1)
    for k in range(15):
        ref = (out_grad_ref, up_grad_ref, down_grad_ref)[k // 5]
        for i in range(2):
            block = part_ref[2 * (k % 8) + i, 160:, 128 * (k // 8) : 128 * (k // 8) + 128]
            ref[160 * i : 160 * i + 160, 128 * (k % 5) : 128 * (k % 5) + 128] = block.astype(F32)
    one_ref[0] = row_totals(in_grad_ref[...], in_ref[...])
    scale = sum(head[:8] for head in heads)
    two = row_totals(up_grad_ref[...], up_ref[...])
    if before:
        scale, two = scale + before[-2][...], two + before[-1][...]
    scale_ref[...] = scale
    two_ref[...] = two


def assemble_call(which, part, attn_in, ffn_in, before=()):
    one = pl.Buffered(1)
    whole = lambda *dims: pl.BlockSpec(dims, lambda i, which: (0,) * len(dims), pipeline_mode=one)
    rows = pl.BlockSpec((160, 3 * D), lambda i, which: (which[0], 0), pipeline_mode=one)
    columns = pl.BlockSpec((320, 640), lambda i, which: (0, which[0]), pipeline_mode=one)
    row = pl.BlockSpec((1, 1, 160), lambda i, which: (which[0], 0, 0), pipeline_mode=one)
    kept = [pl.BlockSpec(memory_space=pl.ANY)] * 5 if before else []
    return pl.pallas_call(
        assemble_kernel,
        grid_spec=pltpu.PrefetchScalarGridSpec(
            num_scalar_prefetch=1,
            grid=(1,),
            in_specs=[whole(16, 320, 256), rows, columns] + kept + ([whole(8, 256), whole(1, 320)] if before else []),
            out_specs=[rows, columns, columns, columns, row, whole(8, 256), whole(1, 320)],
        ),
        out_shape=[shape((320, 3 * D), F32)] + [shape((320, D), F32)] * 3
        + [shape((2, 1, 160), F32), shape((8, 256), F32), shape((1, 320), F32)],
        input_output_aliases={4 + i: i for i in range(5)} if before else {},
        compiler_params=pltpu.CompilerParams(vmem_limit_bytes=58 << 20),
        cost_estimate=pl.CostEstimate(flops=1 << 20, bytes_accessed=10 << 20, transcendentals=0),
        name="assemble",
    )(which, part, attn_in, ffn_in, *before)


def shift(value, axis, step):
    return lax.ppermute(value, axis, [(i, (i + step) % 4) for i in range(4)])


def other_core(value):
    return lax.ppermute(value, "core", [(0, 1), (1, 0)])


def scatter_y(parts):
    y = lax.axis_index("y")
    piece = lambda step: lax.dynamic_index_in_dim(parts, (y + step) % 4, 0, keepdims=False)
    return [piece(0)] + [shift(piece(step).astype(BF16), "y", step) for step in (1, 3, 2)]


def total_of(parts):
    return sum(part.astype(F32) for part in parts)


def half_rows(value):
    rows = value.shape[0] // 2
    return lax.dynamic_slice_in_dim(value, lax.axis_index("core") * rows, rows, 0)


def gather_rows(half):
    return lax.all_gather(half, ("y", "core"), axis=0, tiled=True)


def swap(value):
    return lax.all_to_all(value, CHIPS, 0, 0, tiled=True)


def local(tokens, segment_ids, cotangent, attn_in, attn_out, ffn_in, ffn_out, gain_attn, gain_ffn, query_scale):
    core = lax.axis_index("core")
    place = jnp.stack([lax.axis_index("x"), lax.axis_index("z"), core]).astype(jnp.int32)
    head = place[0] * 4 + place[1]
    inputs_low = tokens.reshape(256, D)
    upstream = cotangent.reshape(256, D)

    gathered = lax.all_gather(inputs_low, CHIPS, axis=0, tiled=True).reshape(16, 256, D)

    small = jnp.stack([gain_attn, gain_ffn, jnp.pad(query_scale, (0, 300))], 1)
    mine = lax.dynamic_index_in_dim(attn_in.reshape(320, 3, HEADS, HD), head, 2, keepdims=False).reshape(320, 3 * HD)
    small = lax.all_gather(jnp.concatenate([mine, jnp.pad(small, ((0, 0), (0, 13)))], 1), "y", axis=0, tiled=True)
    head_weights = small[:, : 3 * HD].T
    gain_one = small[:, 240].reshape(1, D).astype(F32)
    gain_two = small[:, 241].reshape(1, D).astype(F32)
    scale_raw = small[:, 242].reshape(4, 320)[:, :20].reshape(HD).astype(F32)
    factor = (jax.nn.softplus(scale_raw) * (QCONST / math.sqrt(HD)))[:, None]

    segments = lax.all_gather(segment_ids, ("x", "z", "core"), axis=1, tiled=True)
    begins = jnp.stack([jnp.sum((segments < k).astype(jnp.int32), 1) for k in range(1, 4)], 1)
    first_row = 512 * jnp.arange(8, dtype=jnp.int32) + 128 * core.astype(jnp.int32)
    start_of = lambda pos: jnp.max(jnp.where(begins[:, None] <= pos[None, :, None], begins[:, None], 0), 2)
    low = start_of(first_row) // 512
    high = jnp.minimum((start_of(first_row + 383) + 511) // 512, jnp.arange(8, dtype=jnp.int32)[None])
    high = jnp.maximum(low, high)
    bounds = jnp.concatenate([low.reshape(16), high.reshape(16), core[None].astype(jnp.int32), begins.reshape(6)])

    square_weights = half_rows(jnp.concatenate([attn_out, ffn_in, ffn_out], 1))
    qkv_half, upstream_half = half_rows(attn_in), lax.dynamic_slice_in_dim(upstream, 640 * (1 - core), 640, 1)
    gathered, head_weights, bounds, gain_one, gain_two, factor, square_weights, qkv_half, upstream_half = lax.optimization_barrier(
        (gathered, head_weights, bounds, gain_one, gain_two, factor, square_weights, qkv_half, upstream_half)
    )
    weights = gather_rows(square_weights)
    first, own, trade = project_call(gathered, gain_one, head_weights, factor * LOG2E)
    far = other_core(trade)
    attended, attended_low, lse, keys = forward_call(bounds, own, far)
    attended_t = swap(attended_low).reshape(D, 256)
    grad_attended, branch, grad_pre, second, hidden, outputs, grad_middle, branch_half, pre_half = middle_call(
        place, attended_t, inputs_low, upstream, gain_two, weights
    )
    grad_attended = swap(grad_attended.reshape(16, HD, 256))

    lefts, rights = (attended_t, second, hidden), (branch, grad_pre, upstream)
    traded = [other_core(value) for value in lefts]
    traded += [other_core(value) for value in (branch_half, pre_half, upstream_half)]
    early, late = square_call(place, *lefts, *rights, *traded)

    grad_attended, early, late = lax.optimization_barrier((grad_attended, early, late))
    early = lax.psum_scatter(early, "y", scatter_dimension=0, tiled=True)[0]
    dq, scale_terms, dk_own, dv_own, dk_far, dv_far = backward_call(
        bounds, own, far, keys, attended, lse, grad_attended, factor
    )
    late, dq = lax.optimization_barrier((swap(late), dq))
    send, head_grad = weight_call(dq, dk_own, other_core(dk_far), dv_own, other_core(dv_far), first)
    early, send, head_grad = lax.optimization_barrier((swap(early.reshape(16, 160, 128)), send, head_grad))

    scale_part = jnp.sum(scale_terms, 1).reshape(4, 2, 10)
    head_parts = head_grad.reshape(4, 2, 160, 256)
    give = lax.dynamic_index_in_dim(head_parts, 1 - core, 1, keepdims=False).astype(BF16)
    head_sum = lax.dynamic_index_in_dim(head_parts, core, 1, keepdims=False) + other_core(give).astype(F32)
    head_sum = head_sum + jnp.pad(scale_part, ((0, 0), (0, 158), (240, 6)))
    late = jnp.sum(late.astype(F32), 0)
    late = jnp.concatenate([late[:, :80], late[:, 80:]], 2)
    total = total_of(scatter_y(jnp.concatenate([head_sum, late], 1)))
    grad_project, total = lax.optimization_barrier((swap(send), total))
    late = jnp.concatenate([total[160:, :128], total[160:, 128:]], 0)
    squares = jnp.concatenate([jnp.sum(early.astype(F32), 0), late], 1)
    payload = jnp.concatenate([total[:160], squares], 0).astype(BF16)
    w_qkv = gather_rows(qkv_half)
    columns = grad_project.reshape(HEADS, 3, HD, 256).transpose(1, 0, 2, 3).reshape(3 * D, 256)
    grad_first = lax.dot_general(columns, w_qkv, (((0,), (1,)), ((), ())), preferred_element_type=F32)
    inputs = inputs_low.astype(F32)
    input_grad = grad_middle + norm_back(inputs, norm_scale(inputs), gain_one, grad_first)
    payload = swap(jnp.broadcast_to(payload[None], (16, 320, 256)))
    payload, input_grad = lax.optimization_barrier((payload, input_grad))
    parts = assemble_call(place[2:], payload, attn_in, ffn_in)
    far_payload = other_core(payload)
    grad_in, grad_out, grad_up, grad_down, one, scale_sum, two = assemble_call(
        1 - place[2:], far_payload, attn_in, ffn_in, parts
    )
    own_scale = query_scale.astype(F32)
    slope = jax.nn.sigmoid(own_scale) / (jax.nn.softplus(own_scale) * LOG2E)
    return (
        outputs.reshape(2, 128, D),
        input_grad.reshape(2, 128, D),
        grad_in,
        grad_out,
        grad_up,
        grad_down,
        one.reshape(320) / gain_attn.astype(F32),
        two.reshape(320) / gain_ffn.astype(F32),
        scale_sum[:2, 240:250].reshape(20) * slope,
    )


def solution(mesh):
    split = Mesh(mesh.devices.reshape(4, 4, 2, 4), ("x", "z", "core", "y"))
    rows = P("y", ("x", "z", "core"), None)
    weight = P("y", None)
    vector = P("y")
    return jax.shard_map(
        local,
        mesh=split,
        in_specs=(rows, P("y", ("x", "z", "core")), rows) + (weight,) * 4 + (vector,) * 3,
        out_specs=(rows, rows) + (weight,) * 4 + (vector,) * 3,
        check_vma=False,
    )
```

```python
import math

import jax
import jax.numpy as jnp
from jax import lax
from jax.experimental import pallas as pl
from jax.experimental.pallas import tpu as pltpu
from jax.sharding import Mesh
from jax.sharding import PartitionSpec as P

D = 1280
HEADS = 16
HD = 80
EPS = 1e-06
QCONST = 1.442695041
NEG = -1e30
LOG2E = math.log2(math.e)
F32 = jnp.float32
BF16 = jnp.bfloat16
CHIPS = ("x", "z")
shape = jax.ShapeDtypeStruct


def dot(a, b):
    return jnp.dot(a, b, preferred_element_type=F32)


def dot_nt(a, b):
    return lax.dot_general(a, b, (((1,), (1,)), ((), ())), preferred_element_type=F32)


def dot_tn(a, b):
    return lax.dot_general(a, b, (((0,), (0,)), ((), ())), preferred_element_type=F32)


def norm_scale(values):
    return lax.rsqrt(jnp.mean(values * values, -1, keepdims=True) + EPS)


def norm_back(values, scale, gain, grad):
    shaped = grad * gain
    inner = jnp.mean(shaped * values, -1, keepdims=True)
    return scale * shaped - values * (scale * scale * scale * inner)


def whole_call(kernel, scalars, inputs, out_shape, scratch, name, flops, moved, vmem_mib, left_out=()):
    def spec(index, array):
        if index in left_out:
            return pl.BlockSpec(memory_space=pl.ANY)
        return pl.BlockSpec(array.shape, lambda unused: (0,) * len(array.shape), pipeline_mode=pl.Buffered(1))

    return pl.pallas_call(
        kernel,
        grid=(1,),
        in_specs=[pl.BlockSpec(memory_space=pltpu.SMEM)] + [spec(i, array) for i, array in enumerate(inputs)],
        out_specs=[spec(None, array) for array in out_shape],
        out_shape=out_shape,
        scratch_shapes=scratch,
        compiler_params=pltpu.CompilerParams(vmem_limit_bytes=vmem_mib << 20),
        cost_estimate=pl.CostEstimate(flops=flops, bytes_accessed=moved, transcendentals=0),
        name=name,
    )(scalars, *inputs)


def project_kernel(x_ref, gain_ref, weight_ref, factor_ref, first_ref, out_ref, trade_ref):
    blocks = range(x_ref.shape[0])
    for g in blocks:
        x = x_ref[g].astype(F32)
        first_ref[g] = (x * norm_scale(x) * gain_ref[...]).astype(BF16)
    flat = [dot_nt(weight_ref[...], first_ref[g]) for g in blocks]
    for g in blocks:
        out_ref[g, :HD] = (flat[g][:HD] * factor_ref[...]).astype(BF16)
        low = flat[g][HD:].astype(BF16)
        out_ref[g, HD:] = low
        trade_ref[g] = low


def project_call(x, gain, weight, factor):
    step = 4
    whole = lambda *dims: pl.BlockSpec(dims, lambda g: (0,) * len(dims))
    block = lambda *dims: pl.BlockSpec((step,) + dims, lambda g: (g, 0, 0))
    return pl.pallas_call(
        project_kernel,
        grid=(16 // step,),
        in_specs=[block(256, D), whole(1, D), whole(3 * HD, D), whole(HD, 1)],
        out_specs=[block(256, D), block(3 * HD, 256), block(2 * HD, 256)],
        out_shape=[shape((16, 256, D), BF16), shape((16, 3 * HD, 256), BF16), shape((16, 2 * HD, 256), BF16)],
        compiler_params=pltpu.CompilerParams(vmem_limit_bytes=58 << 20),
        cost_estimate=pl.CostEstimate(flops=8 << 30, bytes_accessed=24 << 20, transcendentals=0),
        name="project",
    )(x, gain, weight, factor)


def rows_of(s):
    return pl.ds(pl.multiple_of(s * 128, 128), 128)


def wide_tile(ref, block, s, part=None):
    rows = slice(None) if part is None else slice(HD * part, HD * part + HD)
    return jnp.concatenate([ref[2 * block, rows, rows_of(s)], ref[2 * block + 1, rows, rows_of(s)]], 1)


def tall_tile(ref, which, block, s):
    return jnp.concatenate([ref[which, 2 * block, rows_of(s), :], ref[which, 2 * block + 1, rows_of(s), :]], 0)


def stand(out_ref, which, ref, part):
    row = lax.broadcasted_iota(jnp.int32, (128 - HD, 256), 0)
    ones = jnp.where(row < 3, 1.0, 0.0)

    def block(g, unused):
        wide = ref[g, HD * part : HD * part + HD].astype(F32)
        out_ref[which, g] = jnp.concatenate([wide, ones], 0).T.astype(BF16)
        return unused

    lax.fori_loop(0, 16, block, 0, unroll=4)


def put_wide(ref, block, s, value):
    ref[2 * block, :, rows_of(s)] = value[:, :128]
    ref[2 * block + 1, :, rows_of(s)] = value[:, 128:]


CHAINS = 4
GROUPS = 8 // CHAINS


def query_base():
    column = lax.broadcasted_iota(jnp.int32, (1, 256), 1)
    return column + jnp.where(column >= 128, 128, 0)


def fill_key_base(ref, core):
    row = lax.broadcasted_iota(jnp.int32, (512, 256), 0)
    inner = row % 256
    ref[...] = 128 * jnp.where(row < 256, core, 1 - core) + inner + jnp.where(inner >= 128, 128, 0)


def start_row(bounds, t, s):
    query_pos = 512 * t + 128 * bounds[32] + query_base()
    start = jnp.zeros_like(query_pos)
    for k in range(3):
        begin = bounds[33 + 3 * s + k]
        start = jnp.where(query_pos >= begin, begin, start)
    return start


def allowed(base_ref, bounds, starts, block, diagonal):
    keys = base_ref[...]
    mask = keys >= starts - 512 * block
    if diagonal:
        mask = mask & (keys <= query_base() + 128 * bounds[32])
    return mask


def group_loops(bounds, s, p, last, tile):
    first = CHAINS * p
    low, high = bounds[8 * s + first], bounds[16 + 8 * s + first + CHAINS - 1]
    pl.when(high <= first)(lambda: last(first, False))
    pl.when(high > first)(lambda: last(first, True))
    high = jnp.maximum(low, jnp.minimum(high, first))

    def loop(masked):
        def body(block, unused):
            tile(block, masked)
            return unused

        return body

    lax.fori_loop(high, first, loop(False), 0)
    lax.fori_loop(low, high, loop(True), 0)


LAST = [(j, c) for c in range(CHAINS) for j in range(c + 1)]


def forward_kernel(
    bounds, own_ref, far_ref, out_ref, low_ref, lse_ref, keys_ref, base_ref, best_ref, total_ref, accum_ref
):
    fill_key_base(base_ref, bounds[32])
    stand(keys_ref, 0, own_ref, 1)
    stand(keys_ref, 1, far_ref, 0)

    def group(index, unused):
        s, p = index // GROUPS, index % GROUPS
        queries = [wide_tile(own_ref, CHAINS * p + c, s, 0) for c in range(CHAINS)]
        starts = [start_row(bounds, CHAINS * p + c, s) for c in range(CHAINS)]
        keys_of = lambda block: jnp.concatenate([tall_tile(keys_ref, c, block, s) for c in range(2)], 0)[:, :HD]
        values_of = lambda block: jnp.concatenate([wide_tile(own_ref, block, s, 2), wide_tile(far_ref, block, s, 1)], 1)

        def last(first, masked):
            scores = {(j, c): dot(keys_of(first + j), queries[c]) for j, c in LAST}
            for j, c in LAST:
                if masked or j == c:
                    mask = allowed(base_ref, bounds, starts[c], first + j, j == c)
                    scores[j, c] = jnp.where(mask, scores[j, c], NEG)
            weights = []
            for c in range(CHAINS):
                best = jnp.max(scores[0, c], 0, keepdims=True)
                for j in range(1, c + 1):
                    best = jnp.maximum(best, jnp.max(scores[j, c], 0, keepdims=True))
                parts = [jnp.exp2(scores[j, c] - best) for j in range(c + 1)]
                best_ref[c] = best
                total_ref[c] = sum(jnp.sum(part, 0, keepdims=True) for part in parts)
                weights.append(jnp.concatenate([part.astype(BF16) for part in parts], 0))
            values = jnp.concatenate([values_of(first + j) for j in range(CHAINS)], 1)
            for c in range(CHAINS):
                accum_ref[c] = dot(values[:, : 512 * c + 512], weights[c])

        def tile(block, masked):
            keys, values = keys_of(block), values_of(block)
            scores = [dot(keys, queries[c]) for c in range(CHAINS)]
            weights, decay = [], []
            for c in range(CHAINS):
                if masked:
                    scores[c] = jnp.where(allowed(base_ref, bounds, starts[c], block, False), scores[c], NEG)
                best = best_ref[c]
                newest = jnp.maximum(best, jnp.max(scores[c], 0, keepdims=True))
                best_ref[c] = newest
                weights.append(jnp.exp2(scores[c] - newest))
                decay.append(jnp.exp2(best - newest))
                total_ref[c] = total_ref[c] * decay[c] + jnp.sum(weights[c], 0, keepdims=True)
            for c in range(CHAINS):
                accum_ref[c] = accum_ref[c] * decay[c] + dot(values, weights[c].astype(BF16))

        group_loops(bounds, s, p, last, tile)
        for c in range(CHAINS):
            t = CHAINS * p + c
            result = accum_ref[c] / total_ref[c]
            put_wide(out_ref, t, s, result)
            put_wide(low_ref, t, s, result.astype(BF16))
            put_wide(lse_ref, t, s, best_ref[c] + jnp.log2(total_ref[c]))
        return unused

    lax.fori_loop(0, 2 * GROUPS, group, 0)


def forward_call(bounds, *inputs):
    return whole_call(
        forward_kernel,
        bounds,
        inputs,
        [shape((16, HD, 256), F32), shape((16, HD, 256), BF16), shape((16, 1, 256), F32), shape((2, 16, 256, 128), BF16)],
        [
            pltpu.VMEM((512, 256), jnp.int32),
            pltpu.VMEM((CHAINS, 1, 256), F32),
            pltpu.VMEM((CHAINS, 1, 256), F32),
            pltpu.VMEM((CHAINS, HD, 256), F32),
        ],
        "attention",
        8 << 30,
        8 << 20,
        58,
    )


def tall(wide):
    return jnp.concatenate([wide, jnp.zeros((128 - HD, 256), F32)], 0).T.astype(BF16)


def with_row(wide, row):
    one = row.astype(BF16)
    rest = row - one.astype(F32)
    two = rest.astype(BF16)
    three = (rest - two.astype(F32)).astype(BF16)
    terms = jnp.concatenate([one.astype(F32), two.astype(F32), three.astype(F32), jnp.zeros((13, 256), F32)], 0)
    return jnp.concatenate([wide, terms.astype(BF16)], 0)


def backward_kernel(
    bounds, own_ref, far_ref, keys_ref, out_ref, lse_ref, grad_ref, factor_ref,
    dq_ref, scale_ref, dko_ref, dvo_ref, dkx_ref, dvx_ref,
    dko_acc, dvo_acc, dkx_acc, dvx_acc, base_ref, dq_acc, queries_ref, query_rows_ref, grads_ref, grad_rows_ref, values_ref,
):
    fill_key_base(base_ref, bounds[32])
    stand(values_ref, 0, own_ref, 2)
    stand(values_ref, 1, far_ref, 1)
    for ref in (dko_acc, dvo_acc, dkx_acc, dvx_acc):
        ref[...] = jnp.zeros_like(ref)
    scale_ref[...] = jnp.zeros_like(scale_ref)

    def group(index, unused):
        s, p = index // GROUPS, index % GROUPS
        starts = []
        for c in range(CHAINS):
            t = CHAINS * p + c
            starts.append(start_row(bounds, t, s))
            own = wide_tile(own_ref, t, s, 0)
            queries_ref[c] = with_row(own, -wide_tile(lse_ref, t, s))
            query_rows_ref[256 * c : 256 * c + 256] = tall(own.astype(F32))
            own = wide_tile(grad_ref, t, s)
            wide = own.astype(F32)
            grads_ref[c] = with_row(own, -jnp.sum(wide * wide_tile(out_ref, t, s), 0, keepdims=True))
            grad_rows_ref[256 * c : 256 * c + 256] = tall(wide)
        keys_of = lambda block: jnp.concatenate([tall_tile(keys_ref, c, block, s) for c in range(2)], 0)[:, :96]
        values_of = lambda block: jnp.concatenate([tall_tile(values_ref, c, block, s) for c in range(2)], 0)[:, :96]
        flat_of = lambda block: jnp.concatenate([wide_tile(own_ref, block, s, 1), wide_tile(far_ref, block, s, 0)], 1)

        def add(block, probs, dscores, least):
            dv = dot(jnp.concatenate(probs, 1), grad_rows_ref[256 * least :])
            dk = dot(jnp.concatenate(dscores, 1), query_rows_ref[256 * least :])
            for j in range(2):
                near, far = slice(128 * j, 128 * j + 128), slice(256 + 128 * j, 384 + 128 * j)
                dvo_acc[2 * block + j, rows_of(s), :] += dv[near]
                dko_acc[2 * block + j, rows_of(s), :] += dk[near]
                dvx_acc[2 * block + j, rows_of(s), :] += dv[far]
                dkx_acc[2 * block + j, rows_of(s), :] += dk[far]

        def weigh(scores, dprobs, mask):
            probs = jnp.exp2(scores)
            if mask is not None:
                probs = jnp.where(mask, probs, 0.0)
            return probs.astype(BF16), (probs * dprobs).astype(BF16)

        def last(first, masked):
            scores = {(j, c): dot(keys_of(first + j), queries_ref[c]) for j, c in LAST}
            dprobs = {(j, c): dot(values_of(first + j), grads_ref[c]) for j, c in LAST}
            pair = {}
            for j, c in LAST:
                mask = allowed(base_ref, bounds, starts[c], first + j, j == c) if masked or j == c else None
                pair[j, c] = weigh(scores[j, c], dprobs[j, c], mask)
            flat = jnp.concatenate([flat_of(first + j) for j in range(CHAINS)], 1)
            for c in range(CHAINS):
                dq_acc[c] = dot(flat[:, : 512 * c + 512], jnp.concatenate([pair[j, c][1] for j in range(c + 1)], 0))
            for j in range(CHAINS):
                probs, dscores = zip(*(pair[j, c] for c in range(j, CHAINS)))
                add(first + j, probs, dscores, j)

        def tile(block, masked):
            keys, values, flat = keys_of(block), values_of(block), flat_of(block)
            scores = [dot(keys, queries_ref[c]) for c in range(CHAINS)]
            dprobs = [dot(values, grads_ref[c]) for c in range(CHAINS)]
            masks = [allowed(base_ref, bounds, starts[c], block, False) if masked else None for c in range(CHAINS)]
            probs, dscores = zip(*(weigh(scores[c], dprobs[c], masks[c]) for c in range(CHAINS)))
            for c in range(CHAINS):
                dq_acc[c] += dot(flat, dscores[c])
            add(block, probs, dscores, 0)

        group_loops(bounds, s, p, last, tile)
        for c in range(CHAINS):
            t = CHAINS * p + c
            scale_ref[...] += dq_acc[c] * wide_tile(own_ref, t, s, 0).astype(F32)
            put_wide(dq_ref, t, s, (dq_acc[c] * factor_ref[...]).astype(BF16))
        return unused

    lax.fori_loop(0, 2 * GROUPS, group, 0)
    for ref, total in ((dkx_ref, dkx_acc), (dko_ref, dko_acc)):
        ref[...] = (total[...] * (1 / LOG2E)).astype(BF16)
    for ref, total in ((dvx_ref, dvx_acc), (dvo_ref, dvo_acc)):
        ref[...] = total[...].astype(BF16)


def backward_call(bounds, *inputs):
    rows = (16, 256, 128)
    return whole_call(
        backward_kernel,
        bounds,
        inputs,
        [shape((16, HD, 256), BF16), shape((HD, 256), F32)] + [shape(rows, BF16)] * 4,
        [
            *[pltpu.VMEM(rows, F32)] * 4,
            pltpu.VMEM((512, 256), jnp.int32),
            pltpu.VMEM((CHAINS, HD, 256), F32),
            pltpu.VMEM((CHAINS, 96, 256), BF16),
            pltpu.VMEM((CHAINS * 256, 128), BF16),
            pltpu.VMEM((CHAINS, 96, 256), BF16),
            pltpu.VMEM((CHAINS * 256, 128), BF16),
            pltpu.VMEM((2, 16, 256, 128), BF16),
        ],
        "attention_back",
        60 << 30,
        16 << 20,
        58,
    )


def weight_kernel(
    unused, dq_ref, dko_ref, dkr_ref, dvo_ref, dvr_ref, first_ref, send_ref, weight_ref, held, arrived
):
    copies = [pltpu.make_async_copy(first_ref.at[pl.ds(4 * i, 4)], held.at[pl.ds(4 * i, 4)], arrived.at[i]) for i in range(4)]
    for copy in copies:
        copy.start()

    def block(g, unused):
        send_ref[g, :HD] = dq_ref[g]
        for base, own_ref, far_ref in ((HD, dko_ref, dkr_ref), (2 * HD, dvo_ref, dvr_ref)):
            total = own_ref[g].astype(F32) + far_ref[g].astype(F32)
            send_ref[g, base : base + HD] = total.T[:HD].astype(BF16)
        return unused

    lax.fori_loop(0, 16, block, 0, unroll=2)
    total = 0.0
    for i in range(4):
        rows = jnp.concatenate([send_ref[g] for g in range(4 * i, 4 * i + 4)], 1)
        copies[i].wait()
        total = total + dot(rows, held[4 * i : 4 * i + 4].reshape(1024, D))
    weight_ref[...] = jnp.concatenate([total, jnp.zeros((16, D), F32)], 0).T


def weight_call(*inputs):
    return whole_call(
        weight_kernel,
        jnp.zeros((1,), jnp.int32),
        inputs,
        [shape((16, 3 * HD, 256), BF16), shape((D, 256), F32)],
        [pltpu.VMEM((16, 256, D), BF16), pltpu.SemaphoreType.DMA((4,))],
        "weight",
        12 << 30,
        24 << 20,
        58,
        (5,),
    )


def middle_kernel(
    place, att_ref, x_ref, dy_ref, gain_ref, weights_ref,
    grad_ref, branch_ref, pre_ref, second_ref, hidden_ref, output_ref, wide_ref, branch_half, pre_half, held, arrived,
):
    far = pl.ds(pl.multiple_of(640 * (1 - place[2]), 128), 640)
    gain = gain_ref[...]
    copies = [pltpu.make_async_copy(weights_ref.at[:, D * i : D * i + D], held.at[i], arrived.at[i]) for i in range(3)]
    for copy in copies:
        copy.start()
    out_ref, up_ref, down_ref = (held.at[i] for i in range(3))
    copies[0].wait()
    middle = x_ref[...].astype(F32) + dot_tn(att_ref[...], out_ref[...])
    scale = norm_scale(middle)
    second = (middle * scale * gain).astype(BF16)
    second_ref[...] = second
    upstream = dy_ref[...]
    copies[1].wait()
    hidden_pre = dot(second, up_ref[...])
    gate = jax.nn.sigmoid(hidden_pre)
    hidden_ref[...] = (hidden_pre * gate).astype(BF16)
    copies[2].wait()
    grad_hidden = dot_nt(upstream, down_ref[...])
    grad_pre = (grad_hidden * gate * (1.0 + hidden_pre * (1.0 - gate))).astype(BF16)
    pre_ref[...] = grad_pre
    grad_second = dot_nt(grad_pre, up_ref[...])
    grad_middle = upstream.astype(F32) + norm_back(middle, scale, gain, grad_second)
    wide_ref[...] = grad_middle
    branch = grad_middle.astype(BF16)
    branch_ref[...] = branch
    branch_half[...] = branch_ref[:, far]
    pre_half[...] = pre_ref[:, far]
    grad_ref[...] = dot_nt(out_ref[...], branch).astype(BF16)
    output_ref[...] = (middle + dot(hidden_ref[...], down_ref[...])).astype(BF16)


def middle_call(place, *inputs):
    rows = (256, D)
    return whole_call(
        middle_kernel,
        place,
        inputs,
        [shape((D, 256), BF16)] + [shape(rows, BF16)] * 5 + [shape(rows, F32)] + [shape((256, 640), BF16)] * 2,
        [pltpu.VMEM((3, D, D), BF16), pltpu.SemaphoreType.DMA((3,))],
        "middle",
        5 << 30,
        20 << 20,
        58,
        (4,),
    )


def square_kernel(place, *refs):
    inputs, (early_ref, late_ref, turned) = refs[:12], refs[12:]
    core = place[2]
    for m in range(3):
        left_ref, right_ref, left_far, right_far = inputs[m], inputs[3 + m], inputs[6 + m], inputs[9 + m]
        if m:
            turned[:, :256] = left_ref[...].T
            turned[:, 256:] = left_far[...].T
        else:
            turned[:, :256] = left_ref[...]
            turned[:, 256:] = left_far[...]
        near = right_ref[:, pl.ds(pl.multiple_of(640 * core, 128), 640)]
        right = jnp.concatenate([near, right_far[...]], 0)
        parts = [dot(turned[320 * i : 320 * i + 320], right).astype(BF16) for i in range(4)]
        for i in range(4):
            for k in range(5):
                block = parts[i][:, 128 * k : 128 * k + 128]
                index = 5 * m + k
                if index < 8:
                    early_ref[i, index] = block
                else:
                    late_ref[2 * index - 16, i] = block[:160]
                    late_ref[2 * index - 15, i] = block[160:]
    for index in (14, 15):
        late_ref[index] = jnp.zeros((4, 160, 128), BF16)


def square_call(place, *inputs):
    return whole_call(
        square_kernel,
        place,
        inputs,
        [shape((4, 8, 320, 128), BF16), shape((16, 4, 160, 128), BF16)],
        [pltpu.VMEM((D, 512), BF16)],
        "square",
        6 << 30,
        20 << 20,
        58,
    )


def row_totals(grad, weight):
    terms = grad * weight.astype(F32)
    terms = sum(terms[:, 128 * k : 128 * k + 128] for k in range(terms.shape[1] // 128))
    return jnp.sum(terms.T, 0, keepdims=True)


def assemble_kernel(which, part_ref, in_ref, up_ref, *refs):
    before, (in_grad_ref, out_grad_ref, up_grad_ref, down_grad_ref, one_ref, scale_ref, two_ref) = refs[:-7], refs[-7:]
    heads = [part_ref[h, :160].astype(F32) for h in range(HEADS)]
    for part in range(3):
        in_grad_ref[:, D * part : D * part + D] = jnp.concatenate([head[:, HD * part : HD * part + HD] for head in heads], 1)
    for k in range(15):
        ref = (out_grad_ref, up_grad_ref, down_grad_ref)[k // 5]
        for i in range(2):
            block = part_ref[2 * (k % 8) + i, 160:, 128 * (k // 8) : 128 * (k // 8) + 128]
            ref[160 * i : 160 * i + 160, 128 * (k % 5) : 128 * (k % 5) + 128] = block.astype(F32)
    one_ref[0] = row_totals(in_grad_ref[...], in_ref[...])
    scale = sum(head[:8] for head in heads)
    two = row_totals(up_grad_ref[...], up_ref[...])
    if before:
        scale, two = scale + before[-2][...], two + before[-1][...]
    scale_ref[...] = scale
    two_ref[...] = two


def assemble_call(which, part, attn_in, ffn_in, before=()):
    one = pl.Buffered(1)
    whole = lambda *dims: pl.BlockSpec(dims, lambda i, which: (0,) * len(dims), pipeline_mode=one)
    rows = pl.BlockSpec((160, 3 * D), lambda i, which: (which[0], 0), pipeline_mode=one)
    columns = pl.BlockSpec((320, 640), lambda i, which: (0, which[0]), pipeline_mode=one)
    row = pl.BlockSpec((1, 1, 160), lambda i, which: (which[0], 0, 0), pipeline_mode=one)
    kept = [pl.BlockSpec(memory_space=pl.ANY)] * 5 if before else []
    return pl.pallas_call(
        assemble_kernel,
        grid_spec=pltpu.PrefetchScalarGridSpec(
            num_scalar_prefetch=1,
            grid=(1,),
            in_specs=[pl.BlockSpec(memory_space=pltpu.VMEM), rows, columns] + kept + ([whole(8, 256), whole(1, 320)] if before else []),
            out_specs=[rows, columns, columns, columns, row, whole(8, 256), whole(1, 320)],
        ),
        out_shape=[shape((320, 3 * D), F32)] + [shape((320, D), F32)] * 3
        + [shape((2, 1, 160), F32), shape((8, 256), F32), shape((1, 320), F32)],
        input_output_aliases={4 + i: i for i in range(5)} if before else {},
        compiler_params=pltpu.CompilerParams(vmem_limit_bytes=32 << 20),
        cost_estimate=pl.CostEstimate(flops=1 << 20, bytes_accessed=10 << 20, transcendentals=0),
        name="assemble",
    )(which, part, attn_in, ffn_in, *before)


def shift(value, axis, step):
    return lax.ppermute(value, axis, [(i, (i + step) % 4) for i in range(4)])


def other_core(value):
    return lax.ppermute(value, "core", [(0, 1), (1, 0)])


def scatter_y(parts):
    y = lax.axis_index("y")
    piece = lambda step: lax.dynamic_index_in_dim(parts, (y + step) % 4, 0, keepdims=False)
    return [piece(0)] + [shift(piece(step).astype(BF16), "y", step) for step in (1, 3, 2)]


def total_of(parts):
    return sum(part.astype(F32) for part in parts)


def half_rows(value):
    rows = value.shape[0] // 2
    return lax.dynamic_slice_in_dim(value, lax.axis_index("core") * rows, rows, 0)


def gather_rows(half):
    return lax.all_gather(half, ("y", "core"), axis=0, tiled=True)


def swap(value):
    return lax.all_to_all(value, CHIPS, 0, 0, tiled=True)


def local(tokens, segment_ids, cotangent, attn_in, attn_out, ffn_in, ffn_out, gain_attn, gain_ffn, query_scale):
    core = lax.axis_index("core")
    place = jnp.stack([lax.axis_index("x"), lax.axis_index("z"), core]).astype(jnp.int32)
    head = place[0] * 4 + place[1]
    inputs_low = tokens.reshape(256, D)
    upstream = cotangent.reshape(256, D)

    gathered = lax.all_gather(inputs_low, CHIPS, axis=0, tiled=True).reshape(16, 256, D)

    small = jnp.stack([gain_attn, gain_ffn, jnp.pad(query_scale, (0, 300))], 1)
    mine = lax.dynamic_index_in_dim(attn_in.reshape(320, 3, HEADS, HD), head, 2, keepdims=False).reshape(320, 3 * HD)
    small = lax.all_gather(jnp.concatenate([mine, jnp.pad(small, ((0, 0), (0, 13)))], 1), "y", axis=0, tiled=True)
    head_weights = small[:, : 3 * HD].T
    gain_one = small[:, 240].reshape(1, D).astype(F32)
    gain_two = small[:, 241].reshape(1, D).astype(F32)
    scale_raw = small[:, 242].reshape(4, 320)[:, :20].reshape(HD).astype(F32)
    factor = (jax.nn.softplus(scale_raw) * (QCONST / math.sqrt(HD)))[:, None]

    segments = lax.all_gather(segment_ids, ("x", "z", "core"), axis=1, tiled=True)
    begins = jnp.stack([jnp.sum((segments < k).astype(jnp.int32), 1) for k in range(1, 4)], 1)
    first_row = 512 * jnp.arange(8, dtype=jnp.int32) + 128 * core.astype(jnp.int32)
    start_of = lambda pos: jnp.max(jnp.where(begins[:, None] <= pos[None, :, None], begins[:, None], 0), 2)
    low = start_of(first_row) // 512
    high = jnp.minimum((start_of(first_row + 383) + 511) // 512, jnp.arange(8, dtype=jnp.int32)[None])
    high = jnp.maximum(low, high)
    bounds = jnp.concatenate([low.reshape(16), high.reshape(16), core[None].astype(jnp.int32), begins.reshape(6)])

    square_weights = half_rows(jnp.concatenate([attn_out, ffn_in, ffn_out], 1))
    qkv_half, upstream_half = half_rows(attn_in), lax.dynamic_slice_in_dim(upstream, 640 * (1 - core), 640, 1)
    gathered, head_weights, bounds, gain_one, gain_two, factor, square_weights, qkv_half, upstream_half = lax.optimization_barrier(
        (gathered, head_weights, bounds, gain_one, gain_two, factor, square_weights, qkv_half, upstream_half)
    )
    weights = gather_rows(square_weights)
    first, own, trade = project_call(gathered, gain_one, head_weights, factor * LOG2E)
    far = other_core(trade)
    attended, attended_low, lse, keys = forward_call(bounds, own, far)
    attended_t = swap(attended_low).reshape(D, 256)
    grad_attended, branch, grad_pre, second, hidden, outputs, grad_middle, branch_half, pre_half = middle_call(
        place, attended_t, inputs_low, upstream, gain_two, weights
    )
    grad_attended = swap(grad_attended.reshape(16, HD, 256))

    lefts, rights = (attended_t, second, hidden), (branch, grad_pre, upstream)
    traded = [other_core(value) for value in lefts]
    traded += [other_core(value) for value in (branch_half, pre_half, upstream_half)]
    early, late = square_call(place, *lefts, *rights, *traded)

    grad_attended, early, late = lax.optimization_barrier((grad_attended, early, late))
    early = lax.psum_scatter(early, "y", scatter_dimension=0, tiled=True)[0]
    dq, scale_terms, dk_own, dv_own, dk_far, dv_far = backward_call(
        bounds, own, far, keys, attended, lse, grad_attended, factor
    )
    late, dq = lax.optimization_barrier((swap(late), dq))
    send, head_grad = weight_call(dq, dk_own, other_core(dk_far), dv_own, other_core(dv_far), first)
    early, send, head_grad = lax.optimization_barrier((swap(early.reshape(16, 160, 128)), send, head_grad))

    scale_part = jnp.sum(scale_terms, 1).reshape(4, 2, 10)
    head_parts = head_grad.reshape(4, 2, 160, 256)
    give = lax.dynamic_index_in_dim(head_parts, 1 - core, 1, keepdims=False).astype(BF16)
    head_sum = lax.dynamic_index_in_dim(head_parts, core, 1, keepdims=False) + other_core(give).astype(F32)
    head_sum = head_sum + jnp.pad(scale_part, ((0, 0), (0, 158), (240, 6)))
    late = jnp.sum(late.astype(F32), 0)
    late = jnp.concatenate([late[:, :80], late[:, 80:]], 2)
    total = total_of(scatter_y(jnp.concatenate([head_sum, late], 1)))
    grad_project, total = lax.optimization_barrier((swap(send), total))
    late = jnp.concatenate([total[160:, :128], total[160:, 128:]], 0)
    squares = jnp.concatenate([jnp.sum(early.astype(F32), 0), late], 1)
    payload = jnp.concatenate([total[:160], squares], 0).astype(BF16)
    w_qkv = gather_rows(qkv_half)
    columns = grad_project.reshape(HEADS, 3, HD, 256).transpose(1, 0, 2, 3).reshape(3 * D, 256)
    grad_first = lax.dot_general(columns, w_qkv, (((0,), (1,)), ((), ())), preferred_element_type=F32)
    inputs = inputs_low.astype(F32)
    input_grad = grad_middle + norm_back(inputs, norm_scale(inputs), gain_one, grad_first)
    payload = swap(jnp.broadcast_to(payload[None], (16, 320, 256)))
    payload, input_grad = lax.optimization_barrier((payload, input_grad))
    parts = assemble_call(place[2:], payload, attn_in, ffn_in)
    far_payload = other_core(payload)
    grad_in, grad_out, grad_up, grad_down, one, scale_sum, two = assemble_call(
        1 - place[2:], far_payload, attn_in, ffn_in, parts
    )
    own_scale = query_scale.astype(F32)
    slope = jax.nn.sigmoid(own_scale) / (jax.nn.softplus(own_scale) * LOG2E)
    return (
        outputs.reshape(2, 128, D),
        input_grad.reshape(2, 128, D),
        grad_in,
        grad_out,
        grad_up,
        grad_down,
        one.reshape(320) / gain_attn.astype(F32),
        two.reshape(320) / gain_ffn.astype(F32),
        scale_sum[:2, 240:250].reshape(20) * slope,
    )


def solution(mesh):
    split = Mesh(mesh.devices.reshape(4, 4, 2, 4), ("x", "z", "core", "y"))
    rows = P("y", ("x", "z", "core"), None)
    weight = P("y", None)
    vector = P("y")
    return jax.shard_map(
        local,
        mesh=split,
        in_specs=(rows, P("y", ("x", "z", "core")), rows) + (weight,) * 4 + (vector,) * 3,
        out_specs=(rows, rows) + (weight,) * 4 + (vector,) * 3,
        check_vma=False,
    )
```

```python
import math

import jax
import jax.numpy as jnp
from jax import lax
from jax.experimental import pallas as pl
from jax.experimental.pallas import tpu as pltpu
from jax.sharding import Mesh
from jax.sharding import PartitionSpec as P

D = 1280
HEADS = 16
HD = 80
EPS = 1e-06
QCONST = 1.442695041
NEG = -1e30
LOG2E = math.log2(math.e)
F32 = jnp.float32
BF16 = jnp.bfloat16
CHIPS = ("x", "z")
shape = jax.ShapeDtypeStruct


def dot(a, b):
    return jnp.dot(a, b, preferred_element_type=F32)


def dot_nt(a, b):
    return lax.dot_general(a, b, (((1,), (1,)), ((), ())), preferred_element_type=F32)


def dot_tn(a, b):
    return lax.dot_general(a, b, (((0,), (0,)), ((), ())), preferred_element_type=F32)


def norm_scale(values):
    return lax.rsqrt(jnp.mean(values * values, -1, keepdims=True) + EPS)


def norm_back(values, scale, gain, grad):
    shaped = grad * gain
    inner = jnp.mean(shaped * values, -1, keepdims=True)
    return scale * shaped - values * (scale * scale * scale * inner)


def whole_call(kernel, scalars, inputs, out_shape, scratch, name, flops, moved, vmem_mib, left_out=()):
    def spec(index, array):
        if index in left_out:
            return pl.BlockSpec(memory_space=pl.ANY)
        return pl.BlockSpec(array.shape, lambda unused: (0,) * len(array.shape), pipeline_mode=pl.Buffered(1))

    return pl.pallas_call(
        kernel,
        grid=(1,),
        in_specs=[pl.BlockSpec(memory_space=pltpu.SMEM)] + [spec(i, array) for i, array in enumerate(inputs)],
        out_specs=[spec(None, array) for array in out_shape],
        out_shape=out_shape,
        scratch_shapes=scratch,
        compiler_params=pltpu.CompilerParams(vmem_limit_bytes=vmem_mib << 20),
        cost_estimate=pl.CostEstimate(flops=flops, bytes_accessed=moved, transcendentals=0),
        name=name,
    )(scalars, *inputs)


def normed(x, gain):
    x = x.astype(F32)
    return (x * norm_scale(x) * gain).astype(BF16)


def project_kernel(x_ref, gain_ref, weight_ref, factor_ref, out_ref, trade_ref):
    blocks = range(x_ref.shape[0])
    first = [normed(x_ref[g], gain_ref[...]) for g in blocks]
    flat = [dot_nt(weight_ref[...], first[g]) for g in blocks]
    for g in blocks:
        out_ref[g, :HD] = (flat[g][:HD] * factor_ref[...]).astype(BF16)
        low = flat[g][HD:].astype(BF16)
        out_ref[g, HD:] = low
        trade_ref[g] = low


def project_call(x, gain, weight, factor):
    step = 4
    whole = lambda *dims: pl.BlockSpec(dims, lambda g: (0,) * len(dims))
    block = lambda *dims: pl.BlockSpec((step,) + dims, lambda g: (g, 0, 0))
    return pl.pallas_call(
        project_kernel,
        grid=(16 // step,),
        in_specs=[block(256, D), whole(1, D), whole(3 * HD, D), whole(HD, 1)],
        out_specs=[block(3 * HD, 256), block(2 * HD, 256)],
        out_shape=[shape((16, 3 * HD, 256), BF16), shape((16, 2 * HD, 256), BF16)],
        compiler_params=pltpu.CompilerParams(vmem_limit_bytes=58 << 20),
        cost_estimate=pl.CostEstimate(flops=8 << 30, bytes_accessed=24 << 20, transcendentals=0),
        name="project",
    )(x, gain, weight, factor)


def rows_of(s):
    return pl.ds(pl.multiple_of(s * 128, 128), 128)


def wide_tile(ref, block, s, part=None):
    rows = slice(None) if part is None else slice(HD * part, HD * part + HD)
    return jnp.concatenate([ref[2 * block, rows, rows_of(s)], ref[2 * block + 1, rows, rows_of(s)]], 1)


def tall_tile(ref, which, block, s):
    return jnp.concatenate([ref[which, 2 * block, rows_of(s), :], ref[which, 2 * block + 1, rows_of(s), :]], 0)


def stand(out_ref, which, ref, part):
    row = lax.broadcasted_iota(jnp.int32, (128 - HD, 256), 0)
    ones = jnp.where(row < 3, 1.0, 0.0)

    def block(g, unused):
        wide = ref[g, HD * part : HD * part + HD].astype(F32)
        out_ref[which, g] = jnp.concatenate([wide, ones], 0).T.astype(BF16)
        return unused

    lax.fori_loop(0, 16, block, 0, unroll=4)


def put_wide(ref, block, s, value):
    ref[2 * block, :, rows_of(s)] = value[:, :128]
    ref[2 * block + 1, :, rows_of(s)] = value[:, 128:]


CHAINS = 4
GROUPS = 8 // CHAINS


def query_base():
    column = lax.broadcasted_iota(jnp.int32, (1, 256), 1)
    return column + jnp.where(column >= 128, 128, 0)


def fill_key_base(ref, core):
    row = lax.broadcasted_iota(jnp.int32, (512, 256), 0)
    inner = row % 256
    ref[...] = 128 * jnp.where(row < 256, core, 1 - core) + inner + jnp.where(inner >= 128, 128, 0)


def start_row(bounds, t, s):
    query_pos = 512 * t + 128 * bounds[32] + query_base()
    start = jnp.zeros_like(query_pos)
    for k in range(3):
        begin = bounds[33 + 3 * s + k]
        start = jnp.where(query_pos >= begin, begin, start)
    return start


def allowed(base_ref, bounds, starts, block, diagonal):
    keys = base_ref[...]
    mask = keys >= starts - 512 * block
    if diagonal:
        mask = mask & (keys <= query_base() + 128 * bounds[32])
    return mask


def group_loops(bounds, s, p, last, tile):
    first = CHAINS * p
    low, high = bounds[8 * s + first], bounds[16 + 8 * s + first + CHAINS - 1]
    pl.when(high <= first)(lambda: last(first, False))
    pl.when(high > first)(lambda: last(first, True))
    high = jnp.maximum(low, jnp.minimum(high, first))

    def loop(masked):
        def body(block, unused):
            tile(block, masked)
            return unused

        return body

    lax.fori_loop(high, first, loop(False), 0)
    lax.fori_loop(low, high, loop(True), 0)


LAST = [(j, c) for c in range(CHAINS) for j in range(c + 1)]


def forward_kernel(
    bounds, own_ref, far_ref, out_ref, low_ref, lse_ref, keys_ref, base_ref, best_ref, total_ref, accum_ref
):
    fill_key_base(base_ref, bounds[32])
    stand(keys_ref, 0, own_ref, 1)
    stand(keys_ref, 1, far_ref, 0)

    def group(index, unused):
        s, p = index // GROUPS, index % GROUPS
        queries = [wide_tile(own_ref, CHAINS * p + c, s, 0) for c in range(CHAINS)]
        starts = [start_row(bounds, CHAINS * p + c, s) for c in range(CHAINS)]
        keys_of = lambda block: jnp.concatenate([tall_tile(keys_ref, c, block, s) for c in range(2)], 0)[:, :HD]
        values_of = lambda block: jnp.concatenate([wide_tile(own_ref, block, s, 2), wide_tile(far_ref, block, s, 1)], 1)

        def last(first, masked):
            scores = {(j, c): dot(keys_of(first + j), queries[c]) for j, c in LAST}
            for j, c in LAST:
                if masked or j == c:
                    mask = allowed(base_ref, bounds, starts[c], first + j, j == c)
                    scores[j, c] = jnp.where(mask, scores[j, c], NEG)
            weights = []
            for c in range(CHAINS):
                best = jnp.max(scores[0, c], 0, keepdims=True)
                for j in range(1, c + 1):
                    best = jnp.maximum(best, jnp.max(scores[j, c], 0, keepdims=True))
                parts = [jnp.exp2(scores[j, c] - best) for j in range(c + 1)]
                best_ref[c] = best
                total_ref[c] = sum(jnp.sum(part, 0, keepdims=True) for part in parts)
                weights.append(jnp.concatenate([part.astype(BF16) for part in parts], 0))
            values = jnp.concatenate([values_of(first + j) for j in range(CHAINS)], 1)
            for c in range(CHAINS):
                accum_ref[c] = dot(values[:, : 512 * c + 512], weights[c])

        def tile(block, masked):
            keys, values = keys_of(block), values_of(block)
            scores = [dot(keys, queries[c]) for c in range(CHAINS)]
            weights, decay = [], []
            for c in range(CHAINS):
                if masked:
                    scores[c] = jnp.where(allowed(base_ref, bounds, starts[c], block, False), scores[c], NEG)
                best = best_ref[c]
                newest = jnp.maximum(best, jnp.max(scores[c], 0, keepdims=True))
                best_ref[c] = newest
                weights.append(jnp.exp2(scores[c] - newest))
                decay.append(jnp.exp2(best - newest))
                total_ref[c] = total_ref[c] * decay[c] + jnp.sum(weights[c], 0, keepdims=True)
            for c in range(CHAINS):
                accum_ref[c] = accum_ref[c] * decay[c] + dot(values, weights[c].astype(BF16))

        group_loops(bounds, s, p, last, tile)
        for c in range(CHAINS):
            t = CHAINS * p + c
            result = accum_ref[c] / total_ref[c]
            put_wide(out_ref, t, s, result)
            put_wide(low_ref, t, s, result.astype(BF16))
            put_wide(lse_ref, t, s, best_ref[c] + jnp.log2(total_ref[c]))
        return unused

    lax.fori_loop(0, 2 * GROUPS, group, 0)


def forward_call(bounds, *inputs):
    return whole_call(
        forward_kernel,
        bounds,
        inputs,
        [shape((16, HD, 256), F32), shape((16, HD, 256), BF16), shape((16, 1, 256), F32), shape((2, 16, 256, 128), BF16)],
        [
            pltpu.VMEM((512, 256), jnp.int32),
            pltpu.VMEM((CHAINS, 1, 256), F32),
            pltpu.VMEM((CHAINS, 1, 256), F32),
            pltpu.VMEM((CHAINS, HD, 256), F32),
        ],
        "attention",
        8 << 30,
        8 << 20,
        58,
    )


def tall(wide):
    return jnp.concatenate([wide, jnp.zeros((128 - HD, 256), F32)], 0).T.astype(BF16)


def with_row(wide, row):
    one = row.astype(BF16)
    rest = row - one.astype(F32)
    two = rest.astype(BF16)
    three = (rest - two.astype(F32)).astype(BF16)
    terms = jnp.concatenate([one.astype(F32), two.astype(F32), three.astype(F32), jnp.zeros((13, 256), F32)], 0)
    return jnp.concatenate([wide, terms.astype(BF16)], 0)


def backward_kernel(
    bounds, own_ref, far_ref, keys_ref, out_ref, lse_ref, grad_ref, factor_ref,
    dq_ref, scale_ref, dko_ref, dvo_ref, dkx_ref, dvx_ref,
    dko_acc, dvo_acc, dkx_acc, dvx_acc, base_ref, dq_acc, queries_ref, query_rows_ref, grads_ref, grad_rows_ref, values_ref,
):
    fill_key_base(base_ref, bounds[32])
    stand(values_ref, 0, own_ref, 2)
    stand(values_ref, 1, far_ref, 1)
    for ref in (dko_acc, dvo_acc, dkx_acc, dvx_acc):
        ref[...] = jnp.zeros_like(ref)
    scale_ref[...] = jnp.zeros_like(scale_ref)

    def group(index, unused):
        s, p = index // GROUPS, index % GROUPS
        starts = []
        for c in range(CHAINS):
            t = CHAINS * p + c
            starts.append(start_row(bounds, t, s))
            own = wide_tile(own_ref, t, s, 0)
            queries_ref[c] = with_row(own, -wide_tile(lse_ref, t, s))
            query_rows_ref[256 * c : 256 * c + 256] = tall(own.astype(F32))
            own = wide_tile(grad_ref, t, s)
            wide = own.astype(F32)
            grads_ref[c] = with_row(own, -jnp.sum(wide * wide_tile(out_ref, t, s), 0, keepdims=True))
            grad_rows_ref[256 * c : 256 * c + 256] = tall(wide)
        keys_of = lambda block: jnp.concatenate([tall_tile(keys_ref, c, block, s) for c in range(2)], 0)[:, :96]
        values_of = lambda block: jnp.concatenate([tall_tile(values_ref, c, block, s) for c in range(2)], 0)[:, :96]
        flat_of = lambda block: jnp.concatenate([wide_tile(own_ref, block, s, 1), wide_tile(far_ref, block, s, 0)], 1)

        def add(block, probs, dscores, least):
            dv = dot(jnp.concatenate(probs, 1), grad_rows_ref[256 * least :])
            dk = dot(jnp.concatenate(dscores, 1), query_rows_ref[256 * least :])
            for j in range(2):
                near, far = slice(128 * j, 128 * j + 128), slice(256 + 128 * j, 384 + 128 * j)
                dvo_acc[2 * block + j, rows_of(s), :] += dv[near]
                dko_acc[2 * block + j, rows_of(s), :] += dk[near]
                dvx_acc[2 * block + j, rows_of(s), :] += dv[far]
                dkx_acc[2 * block + j, rows_of(s), :] += dk[far]

        def weigh(scores, dprobs, mask):
            probs = jnp.exp2(scores)
            if mask is not None:
                probs = jnp.where(mask, probs, 0.0)
            return probs.astype(BF16), (probs * dprobs).astype(BF16)

        def last(first, masked):
            scores = {(j, c): dot(keys_of(first + j), queries_ref[c]) for j, c in LAST}
            dprobs = {(j, c): dot(values_of(first + j), grads_ref[c]) for j, c in LAST}
            pair = {}
            for j, c in LAST:
                mask = allowed(base_ref, bounds, starts[c], first + j, j == c) if masked or j == c else None
                pair[j, c] = weigh(scores[j, c], dprobs[j, c], mask)
            flat = jnp.concatenate([flat_of(first + j) for j in range(CHAINS)], 1)
            for c in range(CHAINS):
                dq_acc[c] = dot(flat[:, : 512 * c + 512], jnp.concatenate([pair[j, c][1] for j in range(c + 1)], 0))
            for j in range(CHAINS):
                probs, dscores = zip(*(pair[j, c] for c in range(j, CHAINS)))
                add(first + j, probs, dscores, j)

        def tile(block, masked):
            keys, values, flat = keys_of(block), values_of(block), flat_of(block)
            scores = [dot(keys, queries_ref[c]) for c in range(CHAINS)]
            dprobs = [dot(values, grads_ref[c]) for c in range(CHAINS)]
            masks = [allowed(base_ref, bounds, starts[c], block, False) if masked else None for c in range(CHAINS)]
            probs, dscores = zip(*(weigh(scores[c], dprobs[c], masks[c]) for c in range(CHAINS)))
            for c in range(CHAINS):
                dq_acc[c] += dot(flat, dscores[c])
            add(block, probs, dscores, 0)

        group_loops(bounds, s, p, last, tile)
        for c in range(CHAINS):
            t = CHAINS * p + c
            scale_ref[...] += dq_acc[c] * wide_tile(own_ref, t, s, 0).astype(F32)
            put_wide(dq_ref, t, s, (dq_acc[c] * factor_ref[...]).astype(BF16))
        return unused

    lax.fori_loop(0, 2 * GROUPS, group, 0)
    for ref, total in ((dkx_ref, dkx_acc), (dko_ref, dko_acc)):
        ref[...] = (total[...] * (1 / LOG2E)).astype(BF16)
    for ref, total in ((dvx_ref, dvx_acc), (dvo_ref, dvo_acc)):
        ref[...] = total[...].astype(BF16)


def backward_call(bounds, *inputs):
    rows = (16, 256, 128)
    return whole_call(
        backward_kernel,
        bounds,
        inputs,
        [shape((16, HD, 256), BF16), shape((HD, 256), F32)] + [shape(rows, BF16)] * 4,
        [
            *[pltpu.VMEM(rows, F32)] * 4,
            pltpu.VMEM((512, 256), jnp.int32),
            pltpu.VMEM((CHAINS, HD, 256), F32),
            pltpu.VMEM((CHAINS, 96, 256), BF16),
            pltpu.VMEM((CHAINS * 256, 128), BF16),
            pltpu.VMEM((CHAINS, 96, 256), BF16),
            pltpu.VMEM((CHAINS * 256, 128), BF16),
            pltpu.VMEM((2, 16, 256, 128), BF16),
        ],
        "attention_back",
        60 << 30,
        16 << 20,
        58,
    )


def weight_kernel(
    unused, dq_ref, dko_ref, dkr_ref, dvo_ref, dvr_ref, gain_ref, tokens_ref, send_ref, weight_ref, held, arrived
):
    copies = [pltpu.make_async_copy(tokens_ref.at[pl.ds(4 * i, 4)], held.at[pl.ds(4 * i, 4)], arrived.at[i]) for i in range(4)]
    for copy in copies:
        copy.start()

    def block(g, unused):
        send_ref[g, :HD] = dq_ref[g]
        for base, own_ref, far_ref in ((HD, dko_ref, dkr_ref), (2 * HD, dvo_ref, dvr_ref)):
            total = own_ref[g].astype(F32) + far_ref[g].astype(F32)
            send_ref[g, base : base + HD] = total.T[:HD].astype(BF16)
        return unused

    lax.fori_loop(0, 16, block, 0, unroll=2)
    def first(i):
        copies[i].wait()
        return normed(held[4 * i : 4 * i + 4].reshape(1024, D), gain_ref[...])

    total, now = 0.0, first(0)
    for i in range(4):
        later = first(i + 1) if i < 3 else None
        total = total + dot(jnp.concatenate([send_ref[g] for g in range(4 * i, 4 * i + 4)], 1), now)
        now = later
    weight_ref[...] = jnp.concatenate([total, jnp.zeros((16, D), F32)], 0).T


def weight_call(*inputs):
    return whole_call(
        weight_kernel,
        jnp.zeros((1,), jnp.int32),
        inputs,
        [shape((16, 3 * HD, 256), BF16), shape((D, 256), F32)],
        [pltpu.VMEM((16, 256, D), BF16), pltpu.SemaphoreType.DMA((4,))],
        "weight",
        12 << 30,
        24 << 20,
        58,
        (6,),
    )


def middle_kernel(
    place, att_ref, x_ref, dy_ref, gain_ref, weights_ref, near_ref, far_ref,
    grad_ref, branch_ref, pre_ref, second_ref, hidden_ref, output_ref, wide_ref, branch_half, pre_half, held, arrived,
):
    far = pl.ds(pl.multiple_of(640 * (1 - place[2]), 128), 640)
    gain = gain_ref[...]
    copies = [pltpu.make_async_copy(weights_ref.at[:, D * i : D * i + D], held.at[i], arrived.at[i]) for i in range(2)]
    for k in range(4):
        row = 320 * ((place[3] + 4 - k) % 4)
        for j, (ref, c) in enumerate(((near_ref, place[2]), (far_ref, 1 - place[2]))):
            rows = held.at[2, pl.ds(pl.multiple_of(row + 160 * c, 32), 160)]
            copies.append(pltpu.make_async_copy(ref.at[k], rows, arrived.at[2 + 2 * k + j]))
    for copy in copies:
        copy.start()
    out_ref, up_ref, down_ref = (held.at[i] for i in range(3))
    copies[0].wait()
    middle = x_ref[...].astype(F32) + dot_tn(att_ref[...], out_ref[...])
    scale = norm_scale(middle)
    second = (middle * scale * gain).astype(BF16)
    second_ref[...] = second
    upstream = dy_ref[...]
    copies[1].wait()
    hidden_pre = dot(second, up_ref[...])
    gate = jax.nn.sigmoid(hidden_pre)
    hidden_ref[...] = (hidden_pre * gate).astype(BF16)
    for copy in copies[2:]:
        copy.wait()
    grad_hidden = dot_nt(upstream, down_ref[...])
    grad_pre = (grad_hidden * gate * (1.0 + hidden_pre * (1.0 - gate))).astype(BF16)
    pre_ref[...] = grad_pre
    grad_second = dot_nt(grad_pre, up_ref[...])
    grad_middle = upstream.astype(F32) + norm_back(middle, scale, gain, grad_second)
    wide_ref[...] = grad_middle
    branch = grad_middle.astype(BF16)
    branch_ref[...] = branch
    branch_half[...] = branch_ref[:, far]
    pre_half[...] = pre_ref[:, far]
    grad_ref[...] = dot_nt(out_ref[...], branch).astype(BF16)
    output_ref[...] = (middle + dot(hidden_ref[...], down_ref[...])).astype(BF16)


def middle_call(place, *inputs):
    rows = (256, D)
    return whole_call(
        middle_kernel,
        place,
        inputs,
        [shape((D, 256), BF16)] + [shape(rows, BF16)] * 5 + [shape(rows, F32)] + [shape((256, 640), BF16)] * 2,
        [pltpu.VMEM((3, D, D), BF16), pltpu.SemaphoreType.DMA((10,))],
        "middle",
        5 << 30,
        20 << 20,
        58,
        (4, 5, 6),
    )


def square_kernel(place, *refs):
    inputs, (early_ref, late_ref, turned) = refs[:12], refs[12:]
    core = place[2]
    for m in range(3):
        left_ref, right_ref, left_far, right_far = inputs[m], inputs[3 + m], inputs[6 + m], inputs[9 + m]
        if m:
            turned[:, :256] = left_ref[...].T
            turned[:, 256:] = left_far[...].T
        else:
            turned[:, :256] = left_ref[...]
            turned[:, 256:] = left_far[...]
        near = right_ref[:, pl.ds(pl.multiple_of(640 * core, 128), 640)]
        right = jnp.concatenate([near, right_far[...]], 0)
        parts = [dot(turned[320 * i : 320 * i + 320], right).astype(BF16) for i in range(4)]
        for i in range(4):
            for k in range(5):
                block = parts[i][:, 128 * k : 128 * k + 128]
                index = 5 * m + k
                if index < 8:
                    early_ref[i, index] = block
                else:
                    late_ref[2 * index - 16, i] = block[:160]
                    late_ref[2 * index - 15, i] = block[160:]
    for index in (14, 15):
        late_ref[index] = jnp.zeros((4, 160, 128), BF16)


def square_call(place, *inputs):
    return whole_call(
        square_kernel,
        place,
        inputs,
        [shape((4, 8, 320, 128), BF16), shape((16, 4, 160, 128), BF16)],
        [pltpu.VMEM((D, 512), BF16)],
        "square",
        6 << 30,
        20 << 20,
        58,
    )


def row_totals(grad, weight):
    terms = grad * weight.astype(F32)
    terms = sum(terms[:, 128 * k : 128 * k + 128] for k in range(terms.shape[1] // 128))
    return jnp.sum(terms.T, 0, keepdims=True)


def assemble_kernel(which, part_ref, in_ref, up_ref, *refs):
    before, (in_grad_ref, out_grad_ref, up_grad_ref, down_grad_ref, one_ref, scale_ref, two_ref) = refs[:-7], refs[-7:]
    heads = [part_ref[h, :160].astype(F32) for h in range(HEADS)]
    for part in range(3):
        in_grad_ref[:, D * part : D * part + D] = jnp.concatenate([head[:, HD * part : HD * part + HD] for head in heads], 1)
    for k in range(15):
        ref = (out_grad_ref, up_grad_ref, down_grad_ref)[k // 5]
        for i in range(2):
            block = part_ref[2 * (k % 8) + i, 160:, 128 * (k // 8) : 128 * (k // 8) + 128]
            ref[160 * i : 160 * i + 160, 128 * (k % 5) : 128 * (k % 5) + 128] = block.astype(F32)
    one_ref[0] = row_totals(in_grad_ref[...], in_ref[...])
    scale = sum(head[:8] for head in heads)
    two = row_totals(up_grad_ref[...], up_ref[...])
    if before:
        scale, two = scale + before[-2][...], two + before[-1][...]
    scale_ref[...] = scale
    two_ref[...] = two


def assemble_call(which, part, attn_in, ffn_in, before=()):
    one = pl.Buffered(1)
    whole = lambda *dims: pl.BlockSpec(dims, lambda i, which: (0,) * len(dims), pipeline_mode=one)
    rows = pl.BlockSpec((160, 3 * D), lambda i, which: (which[0], 0), pipeline_mode=one)
    columns = pl.BlockSpec((320, 640), lambda i, which: (0, which[0]), pipeline_mode=one)
    row = pl.BlockSpec((1, 1, 160), lambda i, which: (which[0], 0, 0), pipeline_mode=one)
    kept = [pl.BlockSpec(memory_space=pl.ANY)] * 5 if before else []
    return pl.pallas_call(
        assemble_kernel,
        grid_spec=pltpu.PrefetchScalarGridSpec(
            num_scalar_prefetch=1,
            grid=(1,),
            in_specs=[pl.BlockSpec(memory_space=pltpu.VMEM), rows, columns] + kept + ([whole(8, 256), whole(1, 320)] if before else []),
            out_specs=[rows, columns, columns, columns, row, whole(8, 256), whole(1, 320)],
        ),
        out_shape=[shape((320, 3 * D), F32)] + [shape((320, D), F32)] * 3
        + [shape((2, 1, 160), F32), shape((8, 256), F32), shape((1, 320), F32)],
        input_output_aliases={4 + i: i for i in range(5)} if before else {},
        compiler_params=pltpu.CompilerParams(vmem_limit_bytes=32 << 20),
        cost_estimate=pl.CostEstimate(flops=1 << 20, bytes_accessed=10 << 20, transcendentals=0),
        name="assemble",
    )(which, part, attn_in, ffn_in, *before)


def shift(value, axis, step):
    return lax.ppermute(value, axis, [(i, (i + step) % 4) for i in range(4)])


def other_core(value):
    return lax.ppermute(value, "core", [(0, 1), (1, 0)])


def scatter_y(parts):
    y = lax.axis_index("y")
    piece = lambda step: lax.dynamic_index_in_dim(parts, (y + step) % 4, 0, keepdims=False)
    return [piece(0)] + [shift(piece(step).astype(BF16), "y", step) for step in (1, 3, 2)]


def total_of(parts):
    return sum(part.astype(F32) for part in parts)


def half_rows(value):
    rows = value.shape[0] // 2
    return lax.dynamic_slice_in_dim(value, lax.axis_index("core") * rows, rows, 0)


def gather_rows(half):
    return lax.all_gather(half, ("y", "core"), axis=0, tiled=True)


def swap(value):
    return lax.all_to_all(value, CHIPS, 0, 0, tiled=True)


def local(tokens, segment_ids, cotangent, attn_in, attn_out, ffn_in, ffn_out, gain_attn, gain_ffn, query_scale):
    core = lax.axis_index("core")
    place = jnp.stack([lax.axis_index(axis) for axis in ("x", "z", "core", "y")]).astype(jnp.int32)
    head = place[0] * 4 + place[1]
    inputs_low = tokens.reshape(256, D)
    upstream = cotangent.reshape(256, D)

    gathered = lax.all_gather(inputs_low, CHIPS, axis=0, tiled=True).reshape(16, 256, D)

    small = jnp.stack([gain_attn, gain_ffn, jnp.pad(query_scale, (0, 300))], 1)
    mine = lax.dynamic_index_in_dim(attn_in.reshape(320, 3, HEADS, HD), head, 2, keepdims=False).reshape(320, 3 * HD)
    small = lax.all_gather(jnp.concatenate([mine, jnp.pad(small, ((0, 0), (0, 13)))], 1), "y", axis=0, tiled=True)
    head_weights = small[:, : 3 * HD].T
    gain_one = small[:, 240].reshape(1, D).astype(F32)
    gain_two = small[:, 241].reshape(1, D).astype(F32)
    scale_raw = small[:, 242].reshape(4, 320)[:, :20].reshape(HD).astype(F32)
    factor = (jax.nn.softplus(scale_raw) * (QCONST / math.sqrt(HD)))[:, None]

    segments = lax.all_gather(segment_ids, ("x", "z", "core"), axis=1, tiled=True)
    begins = jnp.stack([jnp.sum((segments < k).astype(jnp.int32), 1) for k in range(1, 4)], 1)
    first_row = 512 * jnp.arange(8, dtype=jnp.int32) + 128 * core.astype(jnp.int32)
    start_of = lambda pos: jnp.max(jnp.where(begins[:, None] <= pos[None, :, None], begins[:, None], 0), 2)
    low = start_of(first_row) // 512
    high = jnp.minimum((start_of(first_row + 383) + 511) // 512, jnp.arange(8, dtype=jnp.int32)[None])
    high = jnp.maximum(low, high)
    bounds = jnp.concatenate([low.reshape(16), high.reshape(16), core[None].astype(jnp.int32), begins.reshape(6)])

    square_weights = half_rows(jnp.concatenate([attn_out, ffn_in], 1))
    qkv_half, upstream_half = half_rows(attn_in), lax.dynamic_slice_in_dim(upstream, 640 * (1 - core), 640, 1)
    down = half_rows(ffn_out)
    down_near = jnp.stack([down, shift(down, "y", 1), shift(down, "y", 2), shift(down, "y", -1)])
    down_far = other_core(down_near)
    gathered, head_weights, bounds, gain_one, gain_two, factor, square_weights, qkv_half, upstream_half, down_near, down_far = (
        lax.optimization_barrier(
            (gathered, head_weights, bounds, gain_one, gain_two, factor, square_weights, qkv_half, upstream_half, down_near, down_far)
        )
    )
    weights = gather_rows(square_weights)
    own, trade = project_call(gathered, gain_one, head_weights, factor * LOG2E)
    far = other_core(trade)
    attended, attended_low, lse, keys = forward_call(bounds, own, far)
    attended_t = swap(attended_low).reshape(D, 256)
    grad_attended, branch, grad_pre, second, hidden, outputs, grad_middle, branch_half, pre_half = middle_call(
        place, attended_t, inputs_low, upstream, gain_two, weights, down_near, down_far
    )
    grad_attended = swap(grad_attended.reshape(16, HD, 256))

    lefts, rights = (attended_t, second, hidden), (branch, grad_pre, upstream)
    traded = [other_core(value) for value in lefts]
    traded += [other_core(value) for value in (branch_half, pre_half, upstream_half)]
    early, late = square_call(place, *lefts, *rights, *traded)

    grad_attended, early, late = lax.optimization_barrier((grad_attended, early, late))
    early = lax.psum_scatter(early, "y", scatter_dimension=0, tiled=True)[0]
    dq, scale_terms, dk_own, dv_own, dk_far, dv_far = backward_call(
        bounds, own, far, keys, attended, lse, grad_attended, factor
    )
    late, dq = lax.optimization_barrier((swap(late), dq))
    send, head_grad = weight_call(dq, dk_own, other_core(dk_far), dv_own, other_core(dv_far), gain_one, gathered)
    early, send, head_grad = lax.optimization_barrier((swap(early.reshape(16, 160, 128)), send, head_grad))

    scale_part = jnp.sum(scale_terms, 1).reshape(4, 2, 10)
    head_parts = head_grad.reshape(4, 2, 160, 256)
    give = lax.dynamic_index_in_dim(head_parts, 1 - core, 1, keepdims=False).astype(BF16)
    head_sum = lax.dynamic_index_in_dim(head_parts, core, 1, keepdims=False) + other_core(give).astype(F32)
    head_sum = head_sum + jnp.pad(scale_part, ((0, 0), (0, 158), (240, 6)))
    late = jnp.sum(late.astype(F32), 0)
    late = jnp.concatenate([late[:, :80], late[:, 80:]], 2)
    total = total_of(scatter_y(jnp.concatenate([head_sum, late], 1)))
    grad_project, total = lax.optimization_barrier((swap(send), total))
    late = jnp.concatenate([total[160:, :128], total[160:, 128:]], 0)
    squares = jnp.concatenate([jnp.sum(early.astype(F32), 0), late], 1)
    payload = jnp.concatenate([total[:160], squares], 0).astype(BF16)
    w_qkv = gather_rows(qkv_half)
    columns = grad_project.reshape(HEADS, 3, HD, 256).transpose(1, 0, 2, 3).reshape(3 * D, 256)
    grad_first = lax.dot_general(columns, w_qkv, (((0,), (1,)), ((), ())), preferred_element_type=F32)
    inputs = inputs_low.astype(F32)
    input_grad = grad_middle + norm_back(inputs, norm_scale(inputs), gain_one, grad_first)
    payload = swap(jnp.broadcast_to(payload[None], (16, 320, 256)))
    payload, input_grad = lax.optimization_barrier((payload, input_grad))
    parts = assemble_call(place[2:3], payload, attn_in, ffn_in)
    far_payload = other_core(payload)
    grad_in, grad_out, grad_up, grad_down, one, scale_sum, two = assemble_call(
        1 - place[2:3], far_payload, attn_in, ffn_in, parts
    )
    own_scale = query_scale.astype(F32)
    slope = jax.nn.sigmoid(own_scale) / (jax.nn.softplus(own_scale) * LOG2E)
    return (
        outputs.reshape(2, 128, D),
        input_grad.reshape(2, 128, D),
        grad_in,
        grad_out,
        grad_up,
        grad_down,
        one.reshape(320) / gain_attn.astype(F32),
        two.reshape(320) / gain_ffn.astype(F32),
        scale_sum[:2, 240:250].reshape(20) * slope,
    )


def solution(mesh):
    split = Mesh(mesh.devices.reshape(4, 4, 2, 4), ("x", "z", "core", "y"))
    rows = P("y", ("x", "z", "core"), None)
    weight = P("y", None)
    vector = P("y")
    return jax.shard_map(
        local,
        mesh=split,
        in_specs=(rows, P("y", ("x", "z", "core")), rows) + (weight,) * 4 + (vector,) * 3,
        out_specs=(rows, rows) + (weight,) * 4 + (vector,) * 3,
        check_vma=False,
    )
```

```python
import math

import jax
import jax.numpy as jnp
from jax import lax
from jax.experimental import pallas as pl
from jax.experimental.pallas import tpu as pltpu
from jax.sharding import Mesh
from jax.sharding import PartitionSpec as P

D = 1280
HEADS = 16
HD = 80
EPS = 1e-06
QCONST = 1.442695041
NEG = -1e30
LOG2E = math.log2(math.e)
F32 = jnp.float32
BF16 = jnp.bfloat16
CHIPS = ("x", "z")
shape = jax.ShapeDtypeStruct


def dot(a, b):
    return jnp.dot(a, b, preferred_element_type=F32)


def dot_nt(a, b):
    return lax.dot_general(a, b, (((1,), (1,)), ((), ())), preferred_element_type=F32)


def dot_tn(a, b):
    return lax.dot_general(a, b, (((0,), (0,)), ((), ())), preferred_element_type=F32)


def norm_scale(values):
    return lax.rsqrt(jnp.mean(values * values, -1, keepdims=True) + EPS)


def norm_back(values, scale, gain, grad):
    shaped = grad * gain
    inner = jnp.mean(shaped * values, -1, keepdims=True)
    return scale * shaped - values * (scale * scale * scale * inner)


def whole_call(kernel, scalars, inputs, out_shape, scratch, name, flops, moved, vmem_mib, left_out=()):
    def spec(index, array):
        if index in left_out:
            return pl.BlockSpec(memory_space=pl.ANY)
        return pl.BlockSpec(array.shape, lambda unused: (0,) * len(array.shape), pipeline_mode=pl.Buffered(1))

    return pl.pallas_call(
        kernel,
        grid=(1,),
        in_specs=[pl.BlockSpec(memory_space=pltpu.SMEM)] + [spec(i, array) for i, array in enumerate(inputs)],
        out_specs=[spec(None, array) for array in out_shape],
        out_shape=out_shape,
        scratch_shapes=scratch,
        compiler_params=pltpu.CompilerParams(vmem_limit_bytes=vmem_mib << 20),
        cost_estimate=pl.CostEstimate(flops=flops, bytes_accessed=moved, transcendentals=0),
        name=name,
    )(scalars, *inputs)


def normed(x, gain):
    x = x.astype(F32)
    return (x * norm_scale(x) * gain).astype(BF16)


def project_kernel(x_ref, gain_ref, weight_ref, factor_ref, out_ref, trade_ref):
    blocks = range(x_ref.shape[0])
    first = [normed(x_ref[g], gain_ref[...]) for g in blocks]
    flat = [dot_nt(weight_ref[...], first[g]) for g in blocks]
    for g in blocks:
        out_ref[g, :HD] = (flat[g][:HD] * factor_ref[...]).astype(BF16)
        low = flat[g][HD:].astype(BF16)
        out_ref[g, HD:] = low
        trade_ref[g] = low


def project_call(x, gain, weight, factor):
    step = 4
    whole = lambda *dims: pl.BlockSpec(dims, lambda g: (0,) * len(dims))
    block = lambda *dims: pl.BlockSpec((step,) + dims, lambda g: (g, 0, 0))
    return pl.pallas_call(
        project_kernel,
        grid=(16 // step,),
        in_specs=[block(256, D), whole(1, D), whole(3 * HD, D), whole(HD, 1)],
        out_specs=[block(3 * HD, 256), block(2 * HD, 256)],
        out_shape=[shape((16, 3 * HD, 256), BF16), shape((16, 2 * HD, 256), BF16)],
        compiler_params=pltpu.CompilerParams(vmem_limit_bytes=58 << 20),
        cost_estimate=pl.CostEstimate(flops=8 << 30, bytes_accessed=24 << 20, transcendentals=0),
        name="project",
    )(x, gain, weight, factor)


def rows_of(s):
    return pl.ds(pl.multiple_of(s * 128, 128), 128)


def wide_tile(ref, block, s, part=None):
    rows = slice(None) if part is None else slice(HD * part, HD * part + HD)
    return jnp.concatenate([ref[2 * block, rows, rows_of(s)], ref[2 * block + 1, rows, rows_of(s)]], 1)


def tall_tile(ref, which, block, s):
    return jnp.concatenate([ref[which, 2 * block, rows_of(s), :], ref[which, 2 * block + 1, rows_of(s), :]], 0)


def stand(out_ref, which, ref, part):
    row = lax.broadcasted_iota(jnp.int32, (128 - HD, 256), 0)
    ones = jnp.where(row < 3, 1.0, 0.0)

    def block(g, unused):
        wide = ref[g, HD * part : HD * part + HD].astype(F32)
        out_ref[which, g] = jnp.concatenate([wide, ones], 0).T.astype(BF16)
        return unused

    lax.fori_loop(0, 16, block, 0, unroll=4)


def put_wide(ref, block, s, value):
    ref[2 * block, :, rows_of(s)] = value[:, :128]
    ref[2 * block + 1, :, rows_of(s)] = value[:, 128:]


CHAINS = 4
GROUPS = 8 // CHAINS


def query_base():
    column = lax.broadcasted_iota(jnp.int32, (1, 256), 1)
    return column + jnp.where(column >= 128, 128, 0)


def fill_key_base(ref, core):
    row = lax.broadcasted_iota(jnp.int32, (512, 256), 0)
    inner = row % 256
    ref[...] = 128 * jnp.where(row < 256, core, 1 - core) + inner + jnp.where(inner >= 128, 128, 0)


def start_row(bounds, t, s):
    query_pos = 512 * t + 128 * bounds[32] + query_base()
    start = jnp.zeros_like(query_pos)
    for k in range(3):
        begin = bounds[33 + 3 * s + k]
        start = jnp.where(query_pos >= begin, begin, start)
    return start


def allowed(base_ref, bounds, starts, block, diagonal):
    keys = base_ref[...]
    mask = keys >= starts - 512 * block
    if diagonal:
        mask = mask & (keys <= query_base() + 128 * bounds[32])
    return mask


def group_loops(bounds, s, p, last, tile):
    first = CHAINS * p
    low, high = bounds[8 * s + first], bounds[16 + 8 * s + first + CHAINS - 1]
    pl.when(high <= first)(lambda: last(first, False))
    pl.when(high > first)(lambda: last(first, True))
    high = jnp.maximum(low, jnp.minimum(high, first))

    def loop(masked):
        def body(block, unused):
            tile(block, masked)
            return unused

        return body

    lax.fori_loop(high, first, loop(False), 0)
    lax.fori_loop(low, high, loop(True), 0)


LAST = [(j, c) for c in range(CHAINS) for j in range(c + 1)]


def forward_kernel(
    bounds, own_ref, far_ref, out_ref, low_ref, lse_ref, keys_ref, base_ref, best_ref, total_ref, accum_ref
):
    fill_key_base(base_ref, bounds[32])
    stand(keys_ref, 0, own_ref, 1)
    stand(keys_ref, 1, far_ref, 0)

    def group(index, unused):
        s, p = index // GROUPS, index % GROUPS
        queries = [wide_tile(own_ref, CHAINS * p + c, s, 0) for c in range(CHAINS)]
        starts = [start_row(bounds, CHAINS * p + c, s) for c in range(CHAINS)]
        keys_of = lambda block: jnp.concatenate([tall_tile(keys_ref, c, block, s) for c in range(2)], 0)[:, :HD]
        values_of = lambda block: jnp.concatenate([wide_tile(own_ref, block, s, 2), wide_tile(far_ref, block, s, 1)], 1)

        def last(first, masked):
            scores = {(j, c): dot(keys_of(first + j), queries[c]) for j, c in LAST}
            for j, c in LAST:
                if masked or j == c:
                    mask = allowed(base_ref, bounds, starts[c], first + j, j == c)
                    scores[j, c] = jnp.where(mask, scores[j, c], NEG)
            weights = []
            for c in range(CHAINS):
                best = jnp.max(scores[0, c], 0, keepdims=True)
                for j in range(1, c + 1):
                    best = jnp.maximum(best, jnp.max(scores[j, c], 0, keepdims=True))
                parts = [jnp.exp2(scores[j, c] - best) for j in range(c + 1)]
                best_ref[c] = best
                total_ref[c] = sum(jnp.sum(part, 0, keepdims=True) for part in parts)
                weights.append(jnp.concatenate([part.astype(BF16) for part in parts], 0))
            values = jnp.concatenate([values_of(first + j) for j in range(CHAINS)], 1)
            for c in range(CHAINS):
                accum_ref[c] = dot(values[:, : 512 * c + 512], weights[c])

        def tile(block, masked):
            keys, values = keys_of(block), values_of(block)
            scores = [dot(keys, queries[c]) for c in range(CHAINS)]
            weights, decay = [], []
            for c in range(CHAINS):
                if masked:
                    scores[c] = jnp.where(allowed(base_ref, bounds, starts[c], block, False), scores[c], NEG)
                best = best_ref[c]
                newest = jnp.maximum(best, jnp.max(scores[c], 0, keepdims=True))
                best_ref[c] = newest
                weights.append(jnp.exp2(scores[c] - newest))
                decay.append(jnp.exp2(best - newest))
                total_ref[c] = total_ref[c] * decay[c] + jnp.sum(weights[c], 0, keepdims=True)
            for c in range(CHAINS):
                accum_ref[c] = accum_ref[c] * decay[c] + dot(values, weights[c].astype(BF16))

        group_loops(bounds, s, p, last, tile)
        for c in range(CHAINS):
            t = CHAINS * p + c
            result = accum_ref[c] / total_ref[c]
            put_wide(out_ref, t, s, result)
            put_wide(low_ref, t, s, result.astype(BF16))
            put_wide(lse_ref, t, s, best_ref[c] + jnp.log2(total_ref[c]))
        return unused

    lax.fori_loop(0, 2 * GROUPS, group, 0)


def forward_call(bounds, *inputs):
    return whole_call(
        forward_kernel,
        bounds,
        inputs,
        [shape((16, HD, 256), F32), shape((16, HD, 256), BF16), shape((16, 1, 256), F32)],
        [
            pltpu.VMEM((2, 16, 256, 128), BF16),
            pltpu.VMEM((512, 256), jnp.int32),
            pltpu.VMEM((CHAINS, 1, 256), F32),
            pltpu.VMEM((CHAINS, 1, 256), F32),
            pltpu.VMEM((CHAINS, HD, 256), F32),
        ],
        "attention",
        8 << 30,
        8 << 20,
        58,
    )


def tall(wide):
    return jnp.concatenate([wide, jnp.zeros((128 - HD, 256), F32)], 0).T.astype(BF16)


def with_row(wide, row):
    one = row.astype(BF16)
    rest = row - one.astype(F32)
    two = rest.astype(BF16)
    three = (rest - two.astype(F32)).astype(BF16)
    terms = jnp.concatenate([one.astype(F32), two.astype(F32), three.astype(F32), jnp.zeros((13, 256), F32)], 0)
    return jnp.concatenate([wide, terms.astype(BF16)], 0)


def backward_kernel(
    bounds, own_ref, far_ref, out_ref, lse_ref, grad_ref, factor_ref,
    dq_ref, scale_ref, dko_ref, dvo_ref, dkx_ref, dvx_ref,
    dko_acc, dvo_acc, dkx_acc, dvx_acc, base_ref, dq_acc, queries_ref, query_rows_ref, grads_ref, grad_rows_ref, keys_ref, values_ref,
):
    fill_key_base(base_ref, bounds[32])
    stand(keys_ref, 0, own_ref, 1)
    stand(keys_ref, 1, far_ref, 0)
    stand(values_ref, 0, own_ref, 2)
    stand(values_ref, 1, far_ref, 1)
    for ref in (dko_acc, dvo_acc, dkx_acc, dvx_acc):
        ref[...] = jnp.zeros_like(ref)
    scale_ref[...] = jnp.zeros_like(scale_ref)

    def group(index, unused):
        s, p = index // GROUPS, index % GROUPS
        starts = []
        for c in range(CHAINS):
            t = CHAINS * p + c
            starts.append(start_row(bounds, t, s))
            own = wide_tile(own_ref, t, s, 0)
            queries_ref[c] = with_row(own, -wide_tile(lse_ref, t, s))
            query_rows_ref[256 * c : 256 * c + 256] = tall(own.astype(F32))
            own = wide_tile(grad_ref, t, s)
            wide = own.astype(F32)
            grads_ref[c] = with_row(own, -jnp.sum(wide * wide_tile(out_ref, t, s), 0, keepdims=True))
            grad_rows_ref[256 * c : 256 * c + 256] = tall(wide)
        keys_of = lambda block: jnp.concatenate([tall_tile(keys_ref, c, block, s) for c in range(2)], 0)[:, :96]
        values_of = lambda block: jnp.concatenate([tall_tile(values_ref, c, block, s) for c in range(2)], 0)[:, :96]
        flat_of = lambda block: jnp.concatenate([wide_tile(own_ref, block, s, 1), wide_tile(far_ref, block, s, 0)], 1)

        def add(block, probs, dscores, least):
            dv = dot(jnp.concatenate(probs, 1), grad_rows_ref[256 * least :])
            dk = dot(jnp.concatenate(dscores, 1), query_rows_ref[256 * least :])
            for j in range(2):
                near, far = slice(128 * j, 128 * j + 128), slice(256 + 128 * j, 384 + 128 * j)
                dvo_acc[2 * block + j, rows_of(s), :] += dv[near]
                dko_acc[2 * block + j, rows_of(s), :] += dk[near]
                dvx_acc[2 * block + j, rows_of(s), :] += dv[far]
                dkx_acc[2 * block + j, rows_of(s), :] += dk[far]

        def weigh(scores, dprobs, mask):
            probs = jnp.exp2(scores)
            if mask is not None:
                probs = jnp.where(mask, probs, 0.0)
            return probs.astype(BF16), (probs * dprobs).astype(BF16)

        def last(first, masked):
            scores = {(j, c): dot(keys_of(first + j), queries_ref[c]) for j, c in LAST}
            dprobs = {(j, c): dot(values_of(first + j), grads_ref[c]) for j, c in LAST}
            pair = {}
            for j, c in LAST:
                mask = allowed(base_ref, bounds, starts[c], first + j, j == c) if masked or j == c else None
                pair[j, c] = weigh(scores[j, c], dprobs[j, c], mask)
            flat = jnp.concatenate([flat_of(first + j) for j in range(CHAINS)], 1)
            for c in range(CHAINS):
                dq_acc[c] = dot(flat[:, : 512 * c + 512], jnp.concatenate([pair[j, c][1] for j in range(c + 1)], 0))
            for j in range(CHAINS):
                probs, dscores = zip(*(pair[j, c] for c in range(j, CHAINS)))
                add(first + j, probs, dscores, j)

        def tile(block, masked):
            keys, values, flat = keys_of(block), values_of(block), flat_of(block)
            scores = [dot(keys, queries_ref[c]) for c in range(CHAINS)]
            dprobs = [dot(values, grads_ref[c]) for c in range(CHAINS)]
            masks = [allowed(base_ref, bounds, starts[c], block, False) if masked else None for c in range(CHAINS)]
            probs, dscores = zip(*(weigh(scores[c], dprobs[c], masks[c]) for c in range(CHAINS)))
            for c in range(CHAINS):
                dq_acc[c] += dot(flat, dscores[c])
            add(block, probs, dscores, 0)

        group_loops(bounds, s, p, last, tile)
        for c in range(CHAINS):
            t = CHAINS * p + c
            scale_ref[...] += dq_acc[c] * wide_tile(own_ref, t, s, 0).astype(F32)
            put_wide(dq_ref, t, s, (dq_acc[c] * factor_ref[...]).astype(BF16))
        return unused

    lax.fori_loop(0, 2 * GROUPS, group, 0)
    for ref, total in ((dkx_ref, dkx_acc), (dko_ref, dko_acc)):
        ref[...] = (total[...] * (1 / LOG2E)).astype(BF16)
    for ref, total in ((dvx_ref, dvx_acc), (dvo_ref, dvo_acc)):
        ref[...] = total[...].astype(BF16)


def backward_call(bounds, *inputs):
    rows = (16, 256, 128)
    return whole_call(
        backward_kernel,
        bounds,
        inputs,
        [shape((16, HD, 256), BF16), shape((HD, 256), F32)] + [shape(rows, BF16)] * 4,
        [
            *[pltpu.VMEM(rows, F32)] * 4,
            pltpu.VMEM((512, 256), jnp.int32),
            pltpu.VMEM((CHAINS, HD, 256), F32),
            pltpu.VMEM((CHAINS, 96, 256), BF16),
            pltpu.VMEM((CHAINS * 256, 128), BF16),
            pltpu.VMEM((CHAINS, 96, 256), BF16),
            pltpu.VMEM((CHAINS * 256, 128), BF16),
            pltpu.VMEM((2, 16, 256, 128), BF16),
            pltpu.VMEM((2, 16, 256, 128), BF16),
        ],
        "attention_back",
        60 << 30,
        16 << 20,
        58,
    )


def weight_kernel(
    unused, dq_ref, dko_ref, dkr_ref, dvo_ref, dvr_ref, gain_ref, tokens_ref, send_ref, weight_ref, held, arrived
):
    copies = [pltpu.make_async_copy(tokens_ref.at[pl.ds(4 * i, 4)], held.at[pl.ds(4 * i, 4)], arrived.at[i]) for i in range(4)]
    for copy in copies:
        copy.start()

    def block(g, unused):
        send_ref[g, :HD] = dq_ref[g]
        for base, own_ref, far_ref in ((HD, dko_ref, dkr_ref), (2 * HD, dvo_ref, dvr_ref)):
            total = own_ref[g].astype(F32) + far_ref[g].astype(F32)
            send_ref[g, base : base + HD] = total.T[:HD].astype(BF16)
        return unused

    lax.fori_loop(0, 16, block, 0, unroll=2)
    def first(i):
        copies[i].wait()
        return normed(held[4 * i : 4 * i + 4].reshape(1024, D), gain_ref[...])

    total, now = 0.0, first(0)
    for i in range(4):
        later = first(i + 1) if i < 3 else None
        total = total + dot(jnp.concatenate([send_ref[g] for g in range(4 * i, 4 * i + 4)], 1), now)
        now = later
    weight_ref[...] = jnp.concatenate([total, jnp.zeros((16, D), F32)], 0).T


def weight_call(*inputs):
    return whole_call(
        weight_kernel,
        jnp.zeros((1,), jnp.int32),
        inputs,
        [shape((16, 3 * HD, 256), BF16), shape((D, 256), F32)],
        [pltpu.VMEM((16, 256, D), BF16), pltpu.SemaphoreType.DMA((4,))],
        "weight",
        12 << 30,
        24 << 20,
        58,
        (6,),
    )


def middle_kernel(
    place, att_ref, x_ref, dy_ref, gain_ref, weights_ref, near_ref, far_ref,
    grad_ref, branch_ref, pre_ref, second_ref, hidden_ref, output_ref, wide_ref, branch_half, pre_half, held, arrived,
):
    far = pl.ds(pl.multiple_of(640 * (1 - place[2]), 128), 640)
    gain = gain_ref[...]
    copies = [pltpu.make_async_copy(weights_ref.at[:, D * i : D * i + D], held.at[i], arrived.at[i]) for i in range(2)]
    for k in range(4):
        row = 320 * ((place[3] + 4 - k) % 4)
        for j, (ref, c) in enumerate(((near_ref, place[2]), (far_ref, 1 - place[2]))):
            rows = held.at[2, pl.ds(pl.multiple_of(row + 160 * c, 32), 160)]
            copies.append(pltpu.make_async_copy(ref.at[k], rows, arrived.at[2 + 2 * k + j]))
    for copy in copies:
        copy.start()
    out_ref, up_ref, down_ref = (held.at[i] for i in range(3))
    copies[0].wait()
    middle = x_ref[...].astype(F32) + dot_tn(att_ref[...], out_ref[...])
    scale = norm_scale(middle)
    second = (middle * scale * gain).astype(BF16)
    second_ref[...] = second
    upstream = dy_ref[...]
    copies[1].wait()
    hidden_pre = dot(second, up_ref[...])
    gate = jax.nn.sigmoid(hidden_pre)
    hidden_ref[...] = (hidden_pre * gate).astype(BF16)
    for copy in copies[2:]:
        copy.wait()
    grad_hidden = dot_nt(upstream, down_ref[...])
    grad_pre = (grad_hidden * gate * (1.0 + hidden_pre * (1.0 - gate))).astype(BF16)
    pre_ref[...] = grad_pre
    grad_second = dot_nt(grad_pre, up_ref[...])
    grad_middle = upstream.astype(F32) + norm_back(middle, scale, gain, grad_second)
    wide_ref[...] = grad_middle
    branch = grad_middle.astype(BF16)
    branch_ref[...] = branch
    branch_half[...] = branch_ref[:, far]
    pre_half[...] = pre_ref[:, far]
    grad_ref[...] = dot_nt(out_ref[...], branch).astype(BF16)
    output_ref[...] = (middle + dot(hidden_ref[...], down_ref[...])).astype(BF16)


def middle_call(place, *inputs):
    rows = (256, D)
    return whole_call(
        middle_kernel,
        place,
        inputs,
        [shape((D, 256), BF16)] + [shape(rows, BF16)] * 5 + [shape(rows, F32)] + [shape((256, 640), BF16)] * 2,
        [pltpu.VMEM((3, D, D), BF16), pltpu.SemaphoreType.DMA((10,))],
        "middle",
        5 << 30,
        20 << 20,
        58,
        (4, 5, 6),
    )


def square_kernel(place, *refs):
    inputs, (early_ref, late_ref, turned) = refs[:12], refs[12:]
    core = place[2]
    for m in range(3):
        left_ref, right_ref, left_far, right_far = inputs[m], inputs[3 + m], inputs[6 + m], inputs[9 + m]
        if m:
            turned[:, :256] = left_ref[...].T
            turned[:, 256:] = left_far[...].T
        else:
            turned[:, :256] = left_ref[...]
            turned[:, 256:] = left_far[...]
        near = right_ref[:, pl.ds(pl.multiple_of(640 * core, 128), 640)]
        right = jnp.concatenate([near, right_far[...]], 0)
        parts = [dot(turned[320 * i : 320 * i + 320], right).astype(BF16) for i in range(4)]
        for i in range(4):
            for k in range(5):
                block = parts[i][:, 128 * k : 128 * k + 128]
                index = 5 * m + k
                if index < 8:
                    early_ref[i, index] = block
                else:
                    late_ref[2 * index - 16, i] = block[:160]
                    late_ref[2 * index - 15, i] = block[160:]
    for index in (14, 15):
        late_ref[index] = jnp.zeros((4, 160, 128), BF16)


def square_call(place, *inputs):
    return whole_call(
        square_kernel,
        place,
        inputs,
        [shape((4, 8, 320, 128), BF16), shape((16, 4, 160, 128), BF16)],
        [pltpu.VMEM((D, 512), BF16)],
        "square",
        6 << 30,
        20 << 20,
        58,
    )


def row_totals(grad, weight):
    terms = grad * weight.astype(F32)
    terms = sum(terms[:, 128 * k : 128 * k + 128] for k in range(terms.shape[1] // 128))
    return jnp.sum(terms.T, 0, keepdims=True)


def assemble_kernel(which, part_ref, in_ref, up_ref, *refs):
    before, (in_grad_ref, out_grad_ref, up_grad_ref, down_grad_ref, one_ref, scale_ref, two_ref) = refs[:-7], refs[-7:]
    heads = [part_ref[h, :160].astype(F32) for h in range(HEADS)]
    for part in range(3):
        in_grad_ref[:, D * part : D * part + D] = jnp.concatenate([head[:, HD * part : HD * part + HD] for head in heads], 1)
    for k in range(15):
        ref = (out_grad_ref, up_grad_ref, down_grad_ref)[k // 5]
        for i in range(2):
            block = part_ref[2 * (k % 8) + i, 160:, 128 * (k // 8) : 128 * (k // 8) + 128]
            ref[160 * i : 160 * i + 160, 128 * (k % 5) : 128 * (k % 5) + 128] = block.astype(F32)
    one_ref[0] = row_totals(in_grad_ref[...], in_ref[...])
    scale = sum(head[:8] for head in heads)
    two = row_totals(up_grad_ref[...], up_ref[...])
    if before:
        scale, two = scale + before[-2][...], two + before[-1][...]
    scale_ref[...] = scale
    two_ref[...] = two


def assemble_call(which, part, attn_in, ffn_in, before=()):
    one = pl.Buffered(1)
    whole = lambda *dims: pl.BlockSpec(dims, lambda i, which: (0,) * len(dims), pipeline_mode=one)
    rows = pl.BlockSpec((160, 3 * D), lambda i, which: (which[0], 0), pipeline_mode=one)
    columns = pl.BlockSpec((320, 640), lambda i, which: (0, which[0]), pipeline_mode=one)
    row = pl.BlockSpec((1, 1, 160), lambda i, which: (which[0], 0, 0), pipeline_mode=one)
    kept = [pl.BlockSpec(memory_space=pl.ANY)] * 5 if before else []
    return pl.pallas_call(
        assemble_kernel,
        grid_spec=pltpu.PrefetchScalarGridSpec(
            num_scalar_prefetch=1,
            grid=(1,),
            in_specs=[pl.BlockSpec(memory_space=pltpu.VMEM), rows, columns] + kept + ([whole(8, 256), whole(1, 320)] if before else []),
            out_specs=[rows, columns, columns, columns, row, whole(8, 256), whole(1, 320)],
        ),
        out_shape=[shape((320, 3 * D), F32)] + [shape((320, D), F32)] * 3
        + [shape((2, 1, 160), F32), shape((8, 256), F32), shape((1, 320), F32)],
        input_output_aliases={4 + i: i for i in range(5)} if before else {},
        compiler_params=pltpu.CompilerParams(vmem_limit_bytes=32 << 20),
        cost_estimate=pl.CostEstimate(flops=1 << 20, bytes_accessed=10 << 20, transcendentals=0),
        name="assemble",
    )(which, part, attn_in, ffn_in, *before)


def shift(value, axis, step):
    return lax.ppermute(value, axis, [(i, (i + step) % 4) for i in range(4)])


def other_core(value):
    return lax.ppermute(value, "core", [(0, 1), (1, 0)])


def scatter_y(parts):
    y = lax.axis_index("y")
    piece = lambda step: lax.dynamic_index_in_dim(parts, (y + step) % 4, 0, keepdims=False)
    return [piece(0)] + [shift(piece(step).astype(BF16), "y", step) for step in (1, 3, 2)]


def total_of(parts):
    return sum(part.astype(F32) for part in parts)


def half_rows(value):
    rows = value.shape[0] // 2
    return lax.dynamic_slice_in_dim(value, lax.axis_index("core") * rows, rows, 0)


def gather_rows(half):
    return lax.all_gather(half, ("y", "core"), axis=0, tiled=True)


def swap(value):
    return lax.all_to_all(value, CHIPS, 0, 0, tiled=True)


def local(tokens, segment_ids, cotangent, attn_in, attn_out, ffn_in, ffn_out, gain_attn, gain_ffn, query_scale):
    core = lax.axis_index("core")
    place = jnp.stack([lax.axis_index(axis) for axis in ("x", "z", "core", "y")]).astype(jnp.int32)
    head = place[0] * 4 + place[1]
    inputs_low = tokens.reshape(256, D)
    upstream = cotangent.reshape(256, D)

    gathered = lax.all_gather(inputs_low, CHIPS, axis=0, tiled=True).reshape(16, 256, D)

    small = jnp.stack([gain_attn, gain_ffn, jnp.pad(query_scale, (0, 300))], 1)
    mine = lax.dynamic_index_in_dim(attn_in.reshape(320, 3, HEADS, HD), head, 2, keepdims=False).reshape(320, 3 * HD)
    small = lax.all_gather(jnp.concatenate([mine, jnp.pad(small, ((0, 0), (0, 13)))], 1), "y", axis=0, tiled=True)
    head_weights = small[:, : 3 * HD].T
    gain_one = small[:, 240].reshape(1, D).astype(F32)
    gain_two = small[:, 241].reshape(1, D).astype(F32)
    scale_raw = small[:, 242].reshape(4, 320)[:, :20].reshape(HD).astype(F32)
    factor = (jax.nn.softplus(scale_raw) * (QCONST / math.sqrt(HD)))[:, None]

    segments = lax.all_gather(segment_ids, ("x", "z", "core"), axis=1, tiled=True)
    begins = jnp.stack([jnp.sum((segments < k).astype(jnp.int32), 1) for k in range(1, 4)], 1)
    first_row = 512 * jnp.arange(8, dtype=jnp.int32) + 128 * core.astype(jnp.int32)
    start_of = lambda pos: jnp.max(jnp.where(begins[:, None] <= pos[None, :, None], begins[:, None], 0), 2)
    low = start_of(first_row) // 512
    high = jnp.minimum((start_of(first_row + 383) + 511) // 512, jnp.arange(8, dtype=jnp.int32)[None])
    high = jnp.maximum(low, high)
    bounds = jnp.concatenate([low.reshape(16), high.reshape(16), core[None].astype(jnp.int32), begins.reshape(6)])

    square_weights = half_rows(jnp.concatenate([attn_out, ffn_in], 1))
    qkv_half, upstream_half = half_rows(attn_in), lax.dynamic_slice_in_dim(upstream, 640 * (1 - core), 640, 1)
    down = half_rows(ffn_out)
    down_near = jnp.stack([down, shift(down, "y", 1), shift(down, "y", 2), shift(down, "y", -1)])
    down_far = other_core(down_near)
    gathered, head_weights, bounds, gain_one, gain_two, factor, square_weights, qkv_half, upstream_half, down_near, down_far = (
        lax.optimization_barrier(
            (gathered, head_weights, bounds, gain_one, gain_two, factor, square_weights, qkv_half, upstream_half, down_near, down_far)
        )
    )
    weights = gather_rows(square_weights)
    own, trade = project_call(gathered, gain_one, head_weights, factor * LOG2E)
    far = other_core(trade)
    attended, attended_low, lse = forward_call(bounds, own, far)
    attended_t = swap(attended_low).reshape(D, 256)
    grad_attended, branch, grad_pre, second, hidden, outputs, grad_middle, branch_half, pre_half = middle_call(
        place, attended_t, inputs_low, upstream, gain_two, weights, down_near, down_far
    )
    grad_attended = swap(grad_attended.reshape(16, HD, 256))

    lefts, rights = (attended_t, second, hidden), (branch, grad_pre, upstream)
    traded = [other_core(value) for value in lefts]
    traded += [other_core(value) for value in (branch_half, pre_half, upstream_half)]
    early, late = square_call(place, *lefts, *rights, *traded)

    grad_attended, early, late = lax.optimization_barrier((grad_attended, early, late))
    early = lax.psum_scatter(early, "y", scatter_dimension=0, tiled=True)[0]
    dq, scale_terms, dk_own, dv_own, dk_far, dv_far = backward_call(
        bounds, own, far, attended, lse, grad_attended, factor
    )
    late, dq = lax.optimization_barrier((swap(late), dq))
    send, head_grad = weight_call(dq, dk_own, other_core(dk_far), dv_own, other_core(dv_far), gain_one, gathered)
    early, send, head_grad = lax.optimization_barrier((swap(early.reshape(16, 160, 128)), send, head_grad))

    scale_part = jnp.sum(scale_terms, 1).reshape(4, 2, 10)
    head_parts = head_grad.reshape(4, 2, 160, 256)
    give = lax.dynamic_index_in_dim(head_parts, 1 - core, 1, keepdims=False).astype(BF16)
    head_sum = lax.dynamic_index_in_dim(head_parts, core, 1, keepdims=False) + other_core(give).astype(F32)
    head_sum = head_sum + jnp.pad(scale_part, ((0, 0), (0, 158), (240, 6)))
    late = jnp.sum(late.astype(F32), 0)
    late = jnp.concatenate([late[:, :80], late[:, 80:]], 2)
    total = total_of(scatter_y(jnp.concatenate([head_sum, late], 1)))
    grad_project, total = lax.optimization_barrier((swap(send), total))
    late = jnp.concatenate([total[160:, :128], total[160:, 128:]], 0)
    squares = jnp.concatenate([jnp.sum(early.astype(F32), 0), late], 1)
    payload = jnp.concatenate([total[:160], squares], 0).astype(BF16)
    w_qkv = gather_rows(qkv_half)
    columns = grad_project.reshape(HEADS, 3, HD, 256).transpose(1, 0, 2, 3).reshape(3 * D, 256)
    grad_first = lax.dot_general(columns, w_qkv, (((0,), (1,)), ((), ())), preferred_element_type=F32)
    inputs = inputs_low.astype(F32)
    input_grad = grad_middle + norm_back(inputs, norm_scale(inputs), gain_one, grad_first)
    payload = swap(jnp.broadcast_to(payload[None], (16, 320, 256)))
    payload, input_grad = lax.optimization_barrier((payload, input_grad))
    parts = assemble_call(place[2:3], payload, attn_in, ffn_in)
    far_payload = other_core(payload)
    grad_in, grad_out, grad_up, grad_down, one, scale_sum, two = assemble_call(
        1 - place[2:3], far_payload, attn_in, ffn_in, parts
    )
    own_scale = query_scale.astype(F32)
    slope = jax.nn.sigmoid(own_scale) / (jax.nn.softplus(own_scale) * LOG2E)
    return (
        outputs.reshape(2, 128, D),
        input_grad.reshape(2, 128, D),
        grad_in,
        grad_out,
        grad_up,
        grad_down,
        one.reshape(320) / gain_attn.astype(F32),
        two.reshape(320) / gain_ffn.astype(F32),
        scale_sum[:2, 240:250].reshape(20) * slope,
    )


def solution(mesh):
    split = Mesh(mesh.devices.reshape(4, 4, 2, 4), ("x", "z", "core", "y"))
    rows = P("y", ("x", "z", "core"), None)
    weight = P("y", None)
    vector = P("y")
    return jax.shard_map(
        local,
        mesh=split,
        in_specs=(rows, P("y", ("x", "z", "core")), rows) + (weight,) * 4 + (vector,) * 3,
        out_specs=(rows, rows) + (weight,) * 4 + (vector,) * 3,
        check_vma=False,
    )
```
